128 devices in a mesh: gx: 16 (over x, z_lo, core), gy: 8 (over y, z_hi).
Axes of the slice: x: 4, y: 4, z: 4 (z_hi: 2, z_lo: 2; z = z_hi * 2 + z_lo), core: 2. Of those that a mesh axis runs over, the one named last changes fastest.
Arguments:
- coarse: bfloat16 [128, 64, 32, 64], P(None, 'gx', 'gy'), may hold values from -6 to 6
- skip: bfloat16 [64, 128, 64, 128], P(None, 'gx', 'gy'), may hold values from -6 to 6
- occupancy: int32 [16, 8, 16], P('gx', 'gy'), may hold values 0 or 1
- cotangent: bfloat16 [64, 128, 64, 128], P(None, 'gx', 'gy'), may hold values from -6 to 6
- up_weight: bfloat16 [4, 4, 4, 128, 64], replicated, may hold values from -0.1875 to 0.1875
- conv_weight: bfloat16 [3, 3, 3, 64, 64], replicated, may hold values from -0.15625 to 0.15625
- conv_bias: float32 [64], replicated, may hold values from -3 to 3
Outputs:
- features: bfloat16 [64, 128, 64, 128], P(None, 'gx', 'gy')
- grad_skip: bfloat16 [64, 128, 64, 128], P(None, 'gx', 'gy')
- grad_coarse: bfloat16 [128, 64, 32, 64], P(None, 'gx', 'gy')
- grad_up: float32 [4, 4, 4, 128, 64], replicated
- grad_conv: float32 [3, 3, 3, 64, 64], replicated
- grad_bias: float32 [64], replicated
The draws below stay inside these ranges and needn't reach their ends.
All inputs are finite; a program needn't handle non-finite values. No bound on the sum of `occupancy` on one device may be relied on, other than what follows from the above.
Results may differ from the reference program's by a relative error of at most 0.0075.
Values may be sent and summed in bfloat16 or wider, within the bound.
A program may use at most 128 MiB of HBM per device.

```python
import jax
import jax.numpy as jnp
from jax import lax

C = 64
CIN = 128
EDGE = 8
NBZ = 16
NX = 128
NY = 64
NZ = 128
N_GX = 16
N_GY = 8


def plant(drawn, key, low, high):
    dims = drawn.shape
    place = [jax.random.randint(jax.random.fold_in(key, axis), (), 0, dims[axis]) for axis in range(len(dims))]
    drawn = drawn.at[tuple(place)].set(low)
    longest = dims.index(max(dims))
    place[longest] = (place[longest] + 1) % dims[longest]
    return drawn.at[tuple(place)].set(high)


def levels(rng, dims, split, low, top_value):
    def one(position, shards_of):
        steps = jax.random.uniform(jax.random.fold_in(jax.random.fold_in(rng, 6), position), (shards_of,), jnp.float32, low / len(split), top_value / len(split))
        return jnp.repeat(jnp.exp(steps), dims[position] // shards_of).reshape((-1,) + (1,) * (len(dims) - position - 1))

    factor_of = one(*split[0])
    for cut in split[1:]:
        factor_of = factor_of * one(*cut)
    return factor_of


def scatter_about(own_key, dims, scale, reach, split=(), kind=jnp.bfloat16):
    values = jax.random.normal(own_key, dims, jnp.float32) * scale
    if len(split) > 0:
        values = levels(own_key, dims, split, -0.22, 0.18) * values
    return jnp.clip(values, min=-reach, max=reach).astype(kind)


def setup_inputs(seed: int = 0) -> dict:
    streams_of = jax.random.split(jax.random.key(seed), 8)
    coarse = scatter_about(streams_of[0], (CIN, NX // 2, NY // 2, NZ // 2), 1.0, 6.0, ((1, 16), (2, 8)))
    skip = scatter_about(streams_of[1], (C, NX, NY, NZ), 1.0, 6.0, ((1, 16), (2, 8)))
    occupancy = plant((jax.random.randint(streams_of[2], (N_GX, N_GY, NBZ), 0, 3) < 2).astype(jnp.int32), jax.random.fold_in(streams_of[2], 1), 0, 1)
    cotangent = scatter_about(streams_of[3], (C, NX, NY, NZ), 1.0, 6.0, ((1, 16), (2, 8)))
    up_weight = scatter_about(streams_of[4], (4, 4, 4, CIN, C), (8 * CIN) ** -0.5, 0.1875)
    conv_weight = scatter_about(streams_of[5], (3, 3, 3, C, C), (27 * C) ** -0.5, 0.15625)
    conv_bias = scatter_about(streams_of[6], (C,), 0.5, 3.0, (), jnp.float32)
    return {"coarse": coarse, "skip": skip, "occupancy": occupancy, "cotangent": cotangent, "up_weight": up_weight, "conv_weight": conv_weight, "conv_bias": conv_bias}


NUMBERS = ("NCDHW", "DHWIO", "NCDHW")


def spread(occupancy, factor):
    grown = jnp.repeat(occupancy, factor, axis=0)
    grown = jnp.repeat(grown, factor, axis=1)
    return jnp.repeat(grown, factor, axis=2) > 0


def convolve(field, kernel, strides, padding, dilation):
    return lax.conv_general_dilated(field.astype(jnp.float32)[None], kernel.astype(jnp.float32), strides, padding, lhs_dilation=dilation, dimension_numbers=NUMBERS, precision=lax.Precision.HIGHEST)[0]


def reference(coarse, skip, occupancy, cotangent, up_weight, conv_weight, conv_bias):
    fine_mask = spread(occupancy, EDGE)
    coarse_mask = spread(occupancy, EDGE // 2)
    active = jnp.where(coarse_mask, coarse, jnp.zeros_like(coarse))
    upsampled = convolve(active, jnp.flip(up_weight, (0, 1, 2)), (1, 1, 1), [(2, 2)] * 3, (2, 2, 2))
    mixed = jnp.where(fine_mask, upsampled + skip.astype(jnp.float32), jnp.float32(0.0)).astype(jnp.bfloat16)
    pre = convolve(mixed, conv_weight, (1, 1, 1), [(1, 1)] * 3, (1, 1, 1)) + conv_bias[:, None, None, None]
    sig = jax.nn.sigmoid(pre)
    features = jnp.where(fine_mask, pre * sig, jnp.float32(0.0)).astype(jnp.bfloat16)
    slope = sig * (1.0 + pre * (1.0 - sig))
    grad_pre = jnp.where(fine_mask, cotangent.astype(jnp.float32) * slope, jnp.float32(0.0)).astype(jnp.bfloat16)
    back = convolve(grad_pre, jnp.swapaxes(jnp.flip(conv_weight, (0, 1, 2)), 3, 4), (1, 1, 1), [(1, 1)] * 3, (1, 1, 1))
    grad_skip = jnp.where(fine_mask, back, jnp.float32(0.0)).astype(jnp.bfloat16)
    delta_pad = jnp.pad(grad_skip.astype(jnp.float32), ((0, 0), (1, 1), (1, 1), (1, 1)))
    lowered = convolve(delta_pad, jnp.swapaxes(up_weight, 3, 4), (2, 2, 2), [(0, 0)] * 3, (1, 1, 1))
    grad_coarse = jnp.where(coarse_mask, lowered, jnp.float32(0.0)).astype(jnp.bfloat16)
    scale = float(NX * NY * NZ) ** -0.5
    mixed_pad = jnp.pad(mixed.astype(jnp.float32), ((0, 0), (1, 1), (1, 1), (1, 1)))
    grad_float = grad_pre.astype(jnp.float32)
    across = grad_float.shape[1]
    along_y = grad_float.shape[2]
    along_z = grad_float.shape[3]
    conv_terms = []
    for shift_x in range(3):
        for shift_y in range(3):
            for shift_z in range(3):
                window = mixed_pad[:, shift_x:shift_x + across, shift_y:shift_y + along_y, shift_z:shift_z + along_z]
                conv_terms.append(jnp.einsum("cxyz,oxyz->co", window, grad_float, precision=lax.Precision.HIGHEST))
    grad_conv = jnp.stack(conv_terms).reshape(3, 3, 3, conv_weight.shape[3], conv_weight.shape[4]) * scale
    grad_bias = jnp.sum(grad_float, axis=(1, 2, 3)) * scale
    active_float = active.astype(jnp.float32)
    inner_x = active.shape[1]
    inner_y = active.shape[2]
    inner_z = active.shape[3]
    up_terms = []
    for shift_x in range(4):
        for shift_y in range(4):
            for shift_z in range(4):
                window = delta_pad[:, shift_x:shift_x + 2 * inner_x:2, shift_y:shift_y + 2 * inner_y:2, shift_z:shift_z + 2 * inner_z:2]
                up_terms.append(jnp.einsum("cxyz,oxyz->co", active_float, window, precision=lax.Precision.HIGHEST))
    grad_up = jnp.stack(up_terms).reshape(4, 4, 4, up_weight.shape[3], up_weight.shape[4]) * scale
    return features, grad_skip, grad_coarse, grad_up, grad_conv, grad_bias
```

```python
import jax
import jax.numpy as jnp
from jax import lax
from jax.experimental import pallas as pl
from jax.experimental.pallas import tpu as pltpu
from jax.sharding import PartitionSpec as P

BF = jnp.bfloat16
F32 = jnp.float32
EDGE = 8
MESH = pl.DeviceIdType.MESH
VMEM = pl.BlockSpec(memory_space=pltpu.VMEM)
LIMIT = 56 * 2**20

U_ROWS = 4096
C_ROWS = 592
ROWS = 6144


def mm(a, b):
    return lax.dot_general(a, b, (((1,), (0,)), ((), ())), preferred_element_type=F32)


def mm_t(a, b):
    return lax.dot_general(a, b, (((1,), (1,)), ((), ())), preferred_element_type=F32)


def lanes(parts):
    return jnp.concatenate(parts, axis=1)


def call(body, out, scratch=(), collective=None):
    extra = {} if collective is None else {"collective_id": collective, "has_side_effects": True}
    return pl.pallas_call(
        body,
        out_shape=out,
        scratch_shapes=list(scratch),
        compiler_params=pltpu.CompilerParams(vmem_limit_bytes=LIMIT, **extra),
    )


def shape(dims, kind=BF):
    return jax.ShapeDtypeStruct(dims, kind)


AROUND = [(1, 0), (-1, 0), (0, 1), (0, -1), (1, 1), (1, -1), (-1, 1), (-1, -1)]


def neighbour(dx, dy):
    nx, ny = lax.axis_size("gx"), lax.axis_size("gy")
    gx, gy = lax.axis_index("gx"), lax.axis_index("gy")
    return lax.rem(gx + (dx + nx), nx), lax.rem(gy + (dy + ny), ny)


def greet_around():
    barrier = pltpu.get_barrier_semaphore()
    for dx, dy in AROUND:
        pl.semaphore_signal(barrier, inc=1, device_id=neighbour(dx, dy), device_id_type=MESH)
    pl.semaphore_wait(barrier, len(AROUND))


def edge(step, count):
    if step == 0:
        return pl.ds(0, count), pl.ds(1, count)
    if step > 0:
        return pl.ds(count - 1, 1), pl.ds(0, 1)
    return pl.ds(0, 1), pl.ds(count + 1, 1)


def halo_copies(block, field, send, recv, first):
    copies = []
    for at, (dx, dy) in enumerate(AROUND):
        sx, tx = edge(dx, block.shape[0])
        sy, ty = edge(dy, block.shape[1])
        copies.append(
            pltpu.make_async_remote_copy(
                src_ref=block.at[sx, sy],
                dst_ref=field.at[tx, ty],
                send_sem=send.at[first + at],
                recv_sem=recv.at[first + at],
                device_id=neighbour(dx, dy),
                device_id_type=MESH,
            )
        )
    return copies


def fill_middle(block, field):
    across, along = block.shape[0], block.shape[1]

    def row(x, carry):
        field[x + 1, pl.ds(1, along)] = block[x]
        return carry

    lax.fori_loop(0, across, row, 0)


def clear_outside(field):
    across, along = field.shape[0], field.shape[1]
    nx, ny = lax.axis_size("gx"), lax.axis_size("gy")
    gx, gy = lax.axis_index("gx"), lax.axis_index("gy")
    row = jnp.zeros((1,) + field.shape[1:], field.dtype)
    column = jnp.zeros((across, 1) + field.shape[2:], field.dtype)

    @pl.when(gx == 0)
    def _():
        field[0:1] = row

    @pl.when(gx == nx - 1)
    def _():
        field[across - 1 : across] = row

    @pl.when(gy == 0)
    def _():
        field[:, 0:1] = column

    @pl.when(gy == ny - 1)
    def _():
        field[:, along - 1 : along] = column


def exchange_body(*refs):
    count = (len(refs) - 2) // 2
    blocks, fields = refs[:count], refs[count : 2 * count]
    send, recv = refs[2 * count :]
    greet_around()
    copies = []
    for at in range(count):
        copies += halo_copies(blocks[at], fields[at], send, recv, at * len(AROUND))
    for copy in copies:
        copy.start()
    for at in range(count):
        fill_middle(blocks[at], fields[at])
    for copy in copies:
        copy.wait()
    for at in range(count):
        clear_outside(fields[at])


def exchange(blocks, collective):
    outs = [shape((b.shape[0] + 2, b.shape[1] + 2) + b.shape[2:], b.dtype) for b in blocks]
    sems = [pltpu.SemaphoreType.DMA((len(AROUND) * len(blocks),))] * 2
    return call(exchange_body, outs, sems, collective)(*blocks)


def lane_of(dims):
    return lax.broadcasted_iota(jnp.int32, dims, len(dims) - 1)


def conv_window(field, i, y):
    return jnp.concatenate(
        [
            lanes(
                [
                    field[i + 4 * h + k, pl.ds(y + e, 3)].reshape(192, 128)
                    for e in range(2)
                    for h in range(2)
                ]
            )
            for k in range(3)
        ],
        axis=0,
    )


def join_taps(taps, lane):
    back = jnp.where(lane == 0, 0.0, pltpu.roll(taps[0:64], 1, 1))
    ahead = jnp.where(lane == 127, 0.0, pltpu.roll(taps[128:192], 127, 1))
    return taps[64:128] + back + ahead


def front_body(
    sf, cf, cot, wu, wc, bias, spread_up, widen, feat, gp, ac, gconv, mx, g3, masks, gacc
):
    lane = lane_of((64, 128))
    for dx in range(3):
        for dy in range(3):
            row = cf[(0, 1, 5)[dx], (0, 1, 5)[dy], 0:16]
            masks[dx, dy] = mm(row, widen[...])

    def pair_coarse(t, carry):
        i, y = t // 6, t % 6
        left = cf[i, y].astype(F32)
        right = pltpu.roll(cf[i + 2, y].astype(F32), 64, 1)
        ac[i, y] = jnp.where(lane_of((128, 128)) < 64, left, right).astype(BF)
        return carry

    lax.fori_loop(0, 24, pair_coarse, 0)

    def mask_of(x, y):
        bx = jnp.where(x == 0, 0, jnp.where(x == 9, 2, 1))
        by = jnp.where(y == 0, 0, jnp.where(y == 9, 2, 1))
        return masks[bx, by, 0:1, :] > 0.5

    def mix(p, q, taps):
        wide = jnp.concatenate(
            [
                lanes([taps[(s * 4 + kz) * 64 : (s * 4 + kz + 1) * 64] for kz in range(4)])
                for s in range(4)
            ],
            axis=0,
        )
        up = mm(wide, spread_up[...])
        for s in range(4):
            for h in range(2):
                x = 2 * p + s // 2 + 4 * h
                y = 2 * q + s % 2
                value = up[s * 64 : s * 64 + 64, h * 128 : h * 128 + 128] + sf[x, y].astype(F32)
                mx[x, y] = jnp.where(mask_of(x, y), value, 0.0).astype(BF)

    def up_pair(t, carry):
        p, q = t // 2, (t % 2) * 2
        window = lanes([ac[pl.ds(p, 2), pl.ds(q + e, 2)].reshape(512, 128) for e in range(2)])
        taps = mm(wu[...], window).astype(BF)
        for e in range(2):
            mix(p, q + e, taps[:, e * 128 : e * 128 + 128])
        return carry

    lax.fori_loop(0, 6, up_pair, 0)

    def up_last(p, carry):
        taps = mm(wu[...], ac[pl.ds(p, 2), pl.ds(4, 2)].reshape(512, 128)).astype(BF)
        mix(p, 4, taps)
        return carry

    lax.fori_loop(0, 3, up_last, 0)

    inside = masks[1, 1, 0:1, :] > 0.5

    def conv(t, carry):
        i, y = t // 4, (t % 4) * 2
        taps = mm(wc[...], conv_window(mx, i, y))
        for e in range(2):
            for h in range(2):
                at = (e * 2 + h) * 128
                pre = join_taps(taps[:, at : at + 128], lane) + bias[...]
                sig = 1.0 / (1.0 + jnp.exp(-pre))
                feat[i + 4 * h, y + e] = jnp.where(inside, pre * sig, 0.0).astype(BF)
                slope = sig * (1.0 + pre * (1.0 - sig))
                grad = cot[i + 4 * h, y + e].astype(F32) * slope
                grad = jnp.where(inside, grad, 0.0).astype(BF)
                gp[i + 4 * h, y + e] = grad
                wide = grad.astype(F32)
                before = jnp.where(lane == 127, 0.0, pltpu.roll(wide, 127, 1)).astype(BF)
                after = jnp.where(lane == 0, 0.0, pltpu.roll(wide, 1, 1)).astype(BF)
                g3[i, y + e, :, h * 128 : h * 128 + 128] = jnp.concatenate(
                    [before, grad, after], axis=0
                )
        return carry

    lax.fori_loop(0, 16, conv, 0)

    gacc[...] = jnp.zeros_like(gacc)

    def kernel_grad(t, carry):
        i, y = t // 2, (t % 2) * 4
        grads = lanes([g3[i, y + j] for j in range(4)])
        for k in range(3):
            cells = lanes(
                [
                    mx[i + 4 * h + k, pl.ds(y + j, 3)].reshape(192, 128)
                    for j in range(4)
                    for h in range(2)
                ]
            )
            gacc[k * 192 : k * 192 + 192, :] += mm_t(cells, grads)
        gacc[576:592, :] += mm_t(jnp.ones((16, 1024), BF), grads)
        return carry

    lax.fori_loop(0, 8, kernel_grad, 0)
    gconv[0:592, :] = gacc[:, 0:128].astype(BF)
    gconv[592:1184, 0:64] = gacc[:, 128:192].astype(BF)
    gconv[592:1184, 64:128] = jnp.zeros((592, 64), BF)


def back_body(gpf, ac, wb, gather_z, mask, gs, gup, d4):
    lane = lane_of((64, 128))
    inside = mask[0:1, :] > 0.5

    def conv(t, carry):
        i, y = t // 4, (t % 4) * 2
        taps = mm(wb[...], conv_window(gpf, i, y))
        for e in range(2):
            both = []
            for h in range(2):
                at = (e * 2 + h) * 128
                grad = join_taps(taps[:, at : at + 128], lane)
                grad = jnp.where(inside, grad, 0.0).astype(BF)
                gs[i + 4 * h, y + e] = grad
                both.append(grad)
            apart = mm(lanes(both), gather_z[...]).astype(BF)
            for kz in range(4):
                d4[i, y + e, kz * 64 : kz * 64 + 64, :] = apart[:, kz * 128 : kz * 128 + 128]
        return carry

    lax.fori_loop(0, 16, conv, 0)

    for sx in range(2):
        for sy in range(2):
            spots = [
                (pi, qi)
                for pi in range(1 - sx, 3 - sx)
                for qi in range(1 - sy, 5 - sy)
            ]
            grads = lanes([d4[2 * pi - 1 + sx, 2 * qi - 1 + sy] for pi, qi in spots])
            cells = jnp.concatenate(
                [
                    lanes([ac[pi + tx, qi + ty] for pi, qi in spots])
                    for tx in range(2)
                    for ty in range(2)
                ],
                axis=0,
            )
            total = mm_t(cells, grads).astype(BF)
            for tx in range(2):
                for ty in range(2):
                    tap = (2 + sx - 2 * tx) * 4 + 2 + sy - 2 * ty
                    rows = (tx * 2 + ty) * 128
                    for half in range(2):
                        at = (tap * 2 + half) * 128
                        gup[at : at + 128, :] = total[
                            rows : rows + 128, half * 128 : half * 128 + 128
                        ]


def lower_body(gsf, wl, gather_z, mask, low, d4):
    def apart(t, carry):
        i, y = t // 10, t % 10
        pieces = mm(lanes([gsf[i, y], gsf[i + 4, y]]), gather_z[...]).astype(BF)
        for kz in range(4):
            d4[i, y, kz * 64 : kz * 64 + 64, :] = pieces[:, kz * 128 : kz * 128 + 128]
        return carry

    lax.fori_loop(0, 60, apart, 0)
    inside = lanes([mask[0:1, :]] * 2) > 0.5

    def lower(t, carry):
        ix, iy = t // 2, (t % 2) * 2
        window = lanes(
            [
                d4[pl.ds(2 * ix, 4), pl.ds(2 * (iy + e), 4)].reshape(4096, 128)
                for e in range(2)
            ]
        )
        grad = jnp.where(inside, mm(wl[...], window), 0.0).astype(BF)
        for e in range(2):
            low[ix, iy + e] = grad[:, e * 128 : e * 128 + 128]
        return carry

    lax.fori_loop(0, 4, lower, 0)


def sum_body(gup, gconv, out, mine, got0, got1, got2, acc1, acc2, send, recv):
    gx, gy = lax.axis_index("gx"), lax.axis_index("gy")
    core, zlo, x = lax.rem(gx, 2), lax.rem(gx // 2, 2), gx // 4
    zhi, y = lax.rem(gy, 2), gy // 2
    z = zhi * 2 + zlo

    def device(px, py, pz, pc):
        return px * 4 + lax.rem(pz, 2) * 2 + pc, py * 2 + pz // 2

    first = jnp.where(core == 0, x, y)
    second = jnp.where(core == 0, y, x)

    def along_first(step):
        other = lax.rem(first + step, 4)
        return other, device(
            jnp.where(core == 0, other, x), jnp.where(core == 0, y, other), z, core
        )

    def in_plane(step):
        a, b = lax.rem(second + step // 4, 4), lax.rem(z + step % 4, 4)
        return a * 4 + b, device(
            jnp.where(core == 0, x, a), jnp.where(core == 0, a, y), b, core
        )

    twin = device(x, y, z, 1 - core)
    place = second * 4 + z
    barrier = pltpu.get_barrier_semaphore()
    pl.semaphore_signal(barrier, inc=1, device_id=twin, device_id_type=MESH)
    for step in range(1, 4):
        pl.semaphore_signal(barrier, inc=1, device_id=along_first(step)[1], device_id_type=MESH)
    for step in range(1, 16):
        pl.semaphore_signal(barrier, inc=1, device_id=in_plane(step)[1], device_id_type=MESH)

    mine[0:U_ROWS] = gup[...]
    mine[U_ROWS : U_ROWS + 2 * C_ROWS] = gconv[...]
    mine[U_ROWS + 2 * C_ROWS : ROWS] = jnp.zeros((ROWS - U_ROWS - 2 * C_ROWS, 128), BF)
    pl.semaphore_wait(barrier, 19)

    half, quarter, chunk = ROWS // 2, ROWS // 8, ROWS // 128

    def remote(src, dst, at, to):
        return pltpu.make_async_remote_copy(
            src_ref=src,
            dst_ref=dst,
            send_sem=send.at[at],
            recv_sem=recv.at[at],
            device_id=to,
            device_id_type=MESH,
        )

    def rows(start, count):
        return pl.ds(pl.multiple_of(start, 16), count)

    copy = remote(mine.at[rows((1 - core) * half, half)], got0, 0, twin)
    copy.start()
    copy.wait()

    def add0(t, carry):
        at = rows(t * 256, 256)
        own = mine[rows(core * half + t * 256, 256)].astype(F32)
        got0[at] = (own + got0[at].astype(F32)).astype(BF)
        return carry

    lax.fori_loop(0, half // 256, add0, 0)

    copies = []
    for step in range(1, 4):
        other, to = along_first(step)
        copies.append(remote(got0.at[rows(other * quarter, quarter)], got1.at[step - 1], step, to))
    for copy in copies:
        copy.start()
    for copy in copies:
        copy.wait()

    def add1(t, carry):
        at = rows(t * 128, 128)
        total = got0[rows(first * quarter + t * 128, 128)].astype(F32)
        for step in range(3):
            total += got1[step, at].astype(F32)
        acc1[at] = total.astype(BF)
        return carry

    lax.fori_loop(0, quarter // 128, add1, 0)

    copies = []
    for step in range(1, 16):
        other, to = in_plane(step)
        copies.append(
            remote(acc1.at[rows(other * chunk, chunk)], got2.at[step - 1], 3 + step, to)
        )
    for copy in copies:
        copy.start()
    for copy in copies:
        copy.wait()
    total = acc1[rows(place * chunk, chunk)].astype(F32)
    for step in range(15):
        total += got2[step].astype(F32)
    acc2[rows(place * chunk, chunk)] = total.astype(BF)

    copies = []
    for step in range(1, 16):
        other, to = in_plane(step)
        own = acc2.at[rows(place * chunk, chunk)]
        copies.append(remote(own, own, 18 + step, to))
    for copy in copies:
        copy.start()
    for copy in copies:
        copy.wait()
    base = core * half + first * quarter
    copies = []
    for step in range(1, 4):
        other, to = along_first(step)
        copies.append(remote(acc2, out.at[rows(base, quarter)], 33 + step, to))
    for copy in copies:
        copy.start()
    out[rows(base, quarter)] = acc2[...]
    for copy in copies:
        copy.wait()
    own = out.at[rows(core * half, half)]
    copy = remote(own, own, 37, twin)
    copy.start()
    copy.wait()


def sum_over_devices(gup, gconv):
    return call(
        sum_body,
        shape((ROWS, 128)),
        [
            pltpu.VMEM((ROWS, 128), BF),
            pltpu.VMEM((ROWS // 2, 128), BF),
            pltpu.VMEM((3, ROWS // 8, 128), BF),
            pltpu.VMEM((15, ROWS // 128, 128), BF),
            pltpu.VMEM((ROWS // 8, 128), BF),
            pltpu.VMEM((ROWS // 8, 128), BF),
            pltpu.SemaphoreType.DMA((38,)),
            pltpu.SemaphoreType.DMA((38,)),
        ],
        5,
    )(gup, gconv)


def spread_matrix():
    row = lax.broadcasted_iota(jnp.int32, (512, 256), 0)
    column = lax.broadcasted_iota(jnp.int32, (512, 256), 1)
    kz, h, j = row // 128, (row // 64) % 2, row % 64
    hit = (h == column // 128) & (column % 128 == 2 * j - 1 + kz)
    return hit.astype(BF)


def widen_matrix():
    row = lax.broadcasted_iota(jnp.int32, (128, 128), 0)
    column = lax.broadcasted_iota(jnp.int32, (128, 128), 1)
    return (row == 64 + column // 2).astype(BF)


def body(coarse, skip, occupancy, cotangent, up_weight, conv_weight, conv_bias):
    active_z = occupancy[0, 0] > 0
    coarse_mask = jnp.repeat(active_z, EDGE // 2)
    fine_mask = jnp.repeat(active_z, EDGE).astype(F32)
    coarse_t = jnp.transpose(coarse, (1, 2, 0, 3))
    coarse_t = jnp.concatenate(
        [
            jnp.where(coarse_mask, coarse_t, jnp.zeros_like(coarse_t)),
            jnp.broadcast_to(coarse_mask.astype(BF), coarse_t.shape),
        ],
        axis=3,
    )
    skip_t = jnp.transpose(skip, (1, 2, 0, 3))
    cot_t = jnp.transpose(cotangent, (1, 2, 0, 3))
    split = jnp.flip(up_weight.reshape(2, 2, 2, 2, 4, 128, 64), (0, 2))
    wu = jnp.transpose(split, (1, 3, 4, 6, 0, 2, 5)).reshape(1024, 512)
    wl = jnp.transpose(up_weight, (3, 0, 1, 2, 4)).reshape(128, 4096)
    wc = jnp.transpose(conv_weight, (2, 4, 0, 1, 3)).reshape(192, 576)
    flipped = jnp.flip(conv_weight, (0, 1, 2))
    wb = jnp.transpose(flipped, (2, 3, 0, 1, 4)).reshape(192, 576)
    bias = jnp.broadcast_to(conv_bias[:, None], (64, 128))
    spread_up = spread_matrix()
    gather_z = spread_up.T
    mask8 = jnp.broadcast_to(fine_mask, (8, 128))
    cmask = coarse_mask.astype(F32)
    cmask8 = jnp.broadcast_to(jnp.concatenate([cmask, cmask]), (8, 128))

    sf, cf = exchange([skip_t, coarse_t], 1)
    feat, gp, ac, gconv = call(
        front_body,
        [
            shape((8, 8, 64, 128)),
            shape((8, 8, 64, 128)),
            shape((4, 6, 128, 128)),
            shape((2 * C_ROWS, 128)),
        ],
        [
            pltpu.VMEM((10, 10, 64, 128), BF),
            pltpu.VMEM((4, 8, 192, 256), BF),
            pltpu.VMEM((3, 3, 16, 128), F32),
            pltpu.VMEM((C_ROWS, 192), F32),
        ],
    )(sf, cf, cot_t, wu, wc, bias, spread_up, widen_matrix())
    (gpf,) = exchange([gp], 2)
    gs, gup = call(
        back_body,
        [shape((8, 8, 64, 128)), shape((U_ROWS, 128))],
        [pltpu.VMEM((4, 8, 256, 128), BF)],
    )(gpf, ac, wb, gather_z, mask8)
    (gsf,) = exchange([gs], 3)
    total = sum_over_devices(gup, gconv)
    low = call(
        lower_body,
        shape((2, 4, 128, 128)),
        [pltpu.VMEM((6, 10, 256, 128), BF)],
    )(gsf, wl, gather_z, cmask8)

    features = jnp.transpose(feat, (2, 0, 1, 3))
    grad_skip = jnp.transpose(gs, (2, 0, 1, 3))
    low = low.reshape(2, 4, 128, 2, 64)
    grad_coarse = jnp.transpose(low, (2, 3, 0, 1, 4)).reshape(128, 4, 4, 64)
    cells = 8192 * lax.axis_size("gx") * lax.axis_size("gy")
    scale = float(cells) ** -0.5
    up = total[:U_ROWS].astype(F32).reshape(4, 4, 2, 128, 2, 64)
    grad_up = jnp.transpose(up, (0, 1, 2, 4, 3, 5)).reshape(4, 4, 4, 128, 64) * scale
    left = total[U_ROWS : U_ROWS + C_ROWS].astype(F32)
    right = total[U_ROWS + C_ROWS : U_ROWS + 2 * C_ROWS].astype(F32)
    left, right = left * scale, right * scale
    taps = jnp.stack([left[:576, 0:64], left[:576, 64:128], right[:576, 0:64]])
    grad_conv = jnp.transpose(taps.reshape(3, 3, 3, 64, 64), (1, 2, 0, 3, 4))
    grad_bias = left[576, 64:128]
    return features, grad_skip, grad_coarse, grad_up, grad_conv, grad_bias


def solution(mesh):
    field = P(None, "gx", "gy", None)
    return jax.shard_map(
        body,
        mesh=mesh,
        in_specs=(field, field, P("gx", "gy", None), field, P(), P(), P()),
        out_specs=(field, field, field, P(), P(), P()),
        check_vma=False,
    )
```

```python
import jax
import jax.numpy as jnp
import ml_dtypes
import numpy as np
from jax import lax
from jax.experimental import pallas as pl
from jax.experimental.pallas import tpu as pltpu
from jax.sharding import PartitionSpec as P

BF = jnp.bfloat16
F32 = jnp.float32
EDGE = 8
MESH = pl.DeviceIdType.MESH
LIMIT = 56 * 2**20

C_ROWS = 592
PIECE = 2048
HALF, QUARTER, CHUNK = PIECE // 2, PIECE // 8, PIECE // 128


def mm(a, b):
    return lax.dot_general(a, b, (((1,), (0,)), ((), ())), preferred_element_type=F32)


def mm_t(a, b):
    return lax.dot_general(a, b, (((1,), (1,)), ((), ())), preferred_element_type=F32)


def lanes(parts):
    return jnp.concatenate(parts, axis=1)


def rows(parts):
    return jnp.concatenate(parts, axis=0)


def shape(dims, kind=BF):
    return jax.ShapeDtypeStruct(dims, kind)


AROUND = [(0, 1), (0, -1), (1, 0), (-1, 0), (1, 1), (1, -1), (-1, 1), (-1, -1)]


def neighbour(dx, dy):
    nx, ny = lax.axis_size("gx"), lax.axis_size("gy")
    gx, gy = lax.axis_index("gx"), lax.axis_index("gy")
    return lax.rem(gx + (dx + nx), nx), lax.rem(gy + (dy + ny), ny)


def outer(step, count):
    if step == 0:
        return pl.ds(1, count), pl.ds(1, count)
    if step > 0:
        return pl.ds(count, 1), pl.ds(0, 1)
    return pl.ds(1, 1), pl.ds(count + 1, 1)


def padding(step, count):
    if step == 0:
        return pl.ds(1, count), pl.ds(1, count)
    if step > 0:
        return pl.ds(count + 1, 1), pl.ds(0, 1)
    return pl.ds(0, 1), pl.ds(count + 1, 1)


def halo_copies(source, target, send, recv, first, place=outer):
    across, along = source.shape[0] - 2, source.shape[1] - 2
    copies = []
    for at, (dx, dy) in enumerate(AROUND):
        sx, tx = place(dx, across)
        sy, ty = place(dy, along)
        copies.append(
            pltpu.make_async_remote_copy(
                src_ref=source.at[sx, sy],
                dst_ref=target.at[tx, ty],
                send_sem=send.at[first + at],
                recv_sem=recv.at[first + at],
                device_id=neighbour(dx, dy),
                device_id_type=MESH,
            )
        )
    return copies


def start(copies):
    for copy in copies:
        copy.start()


def finish(copies):
    for copy in copies:
        copy.wait()


def clear_outside(field):
    across, along = field.shape[0], field.shape[1]
    nx, ny = lax.axis_size("gx"), lax.axis_size("gy")
    gx, gy = lax.axis_index("gx"), lax.axis_index("gy")
    row = jnp.zeros((1,) + field.shape[1:], field.dtype)
    column = jnp.zeros((across, 1) + field.shape[2:], field.dtype)

    @pl.when(gx == 0)
    def _():
        field[0:1] = row

    @pl.when(gx == nx - 1)
    def _():
        field[across - 1 : across] = row

    @pl.when(gy == 0)
    def _():
        field[:, 0:1] = column

    @pl.when(gy == ny - 1)
    def _():
        field[:, along - 1 : along] = column


class Ring:
    def __init__(self):
        gx, gy = lax.axis_index("gx"), lax.axis_index("gy")
        self.core = lax.rem(gx, 2)
        self.x, self.y = gx // 4, gy // 2
        self.z = lax.rem(gy, 2) * 2 + lax.rem(gx // 2, 2)
        self.first = jnp.where(self.core == 0, self.x, self.y)
        self.second = jnp.where(self.core == 0, self.y, self.x)
        self.place = self.second * 4 + self.z
        self.twin = self.device(self.x, self.y, self.z, 1 - self.core)

    def device(self, x, y, z, core):
        return x * 4 + lax.rem(z, 2) * 2 + core, y * 2 + z // 2

    def along_first(self, step):
        other = lax.rem(self.first + step, 4)
        x = jnp.where(self.core == 0, other, self.x)
        y = jnp.where(self.core == 0, self.y, other)
        return other, self.device(x, y, self.z, self.core)

    def in_plane(self, step):
        a, b = lax.rem(self.second + step // 4, 4), lax.rem(self.z + step % 4, 4)
        x = jnp.where(self.core == 0, self.x, a)
        y = jnp.where(self.core == 0, a, self.y)
        return a * 4 + b, self.device(x, y, b, self.core)

    def greet(self, barrier):
        partners = [self.twin]
        partners += [self.along_first(step)[1] for step in range(1, 4)]
        partners += [self.in_plane(step)[1] for step in range(1, 16)]
        for partner in partners:
            pl.semaphore_signal(barrier, inc=1, device_id=partner, device_id_type=MESH)
        return len(partners)


def span(begin, count):
    return pl.ds(pl.multiple_of(begin, 16), count)


class Piece:
    def __init__(self, ring, index, mine, got0, got1, got2, acc1, acc2, out, send, recv):
        self.ring, self.base = ring, index * 38
        self.mine, self.got0, self.got1 = mine.at[index], got0.at[index], got1.at[index]
        self.got2, self.acc1, self.acc2 = got2.at[index], acc1.at[index], acc2.at[index]
        self.out, self.send, self.recv = out.at[index], send, recv
        self.flying = []

    def remote(self, src, dst, at, to):
        return pltpu.make_async_remote_copy(
            src_ref=src,
            dst_ref=dst,
            send_sem=self.send.at[self.base + at],
            recv_sem=self.recv.at[self.base + at],
            device_id=to,
            device_id_type=MESH,
        )

    def launch(self, copies):
        start(copies)
        self.flying = copies

    def step0(self):
        ring = self.ring
        theirs = self.mine.at[span((1 - ring.core) * HALF, HALF)]
        self.launch([self.remote(theirs, self.got0, 0, ring.twin)])

    def step1(self):
        ring = self.ring
        finish(self.flying)

        def add(t, carry):
            own = self.mine[span(ring.core * HALF + t * 256, 256)].astype(F32)
            at = span(t * 256, 256)
            self.got0[at] = (own + self.got0[at].astype(F32)).astype(BF)
            return carry

        lax.fori_loop(0, HALF // 256, add, 0)
        copies = []
        for step in range(1, 4):
            other, to = ring.along_first(step)
            theirs = self.got0.at[span(other * QUARTER, QUARTER)]
            copies.append(self.remote(theirs, self.got1.at[step - 1], step, to))
        self.launch(copies)

    def step2(self):
        ring = self.ring
        finish(self.flying)
        total = self.got0[span(ring.first * QUARTER, QUARTER)].astype(F32)
        for step in range(3):
            total += self.got1[step].astype(F32)
        self.acc1[...] = total.astype(BF)
        copies = []
        for step in range(1, 16):
            other, to = ring.in_plane(step)
            theirs = self.acc1.at[span(other * CHUNK, CHUNK)]
            copies.append(self.remote(theirs, self.got2.at[step - 1], 3 + step, to))
        self.launch(copies)

    def step3(self):
        ring = self.ring
        finish(self.flying)
        total = self.acc1[span(ring.place * CHUNK, CHUNK)].astype(F32)
        for step in range(15):
            total += self.got2[step].astype(F32)
        own = span(ring.place * CHUNK, CHUNK)
        self.acc2[own] = total.astype(BF)
        copies = []
        for step in range(1, 16):
            other, to = ring.in_plane(step)
            copies.append(self.remote(self.acc2.at[own], self.acc2.at[own], 18 + step, to))
        self.launch(copies)

    def step4(self):
        ring = self.ring
        finish(self.flying)
        own = span(ring.core * HALF + ring.first * QUARTER, QUARTER)
        copies = []
        for step in range(1, 4):
            other, to = ring.along_first(step)
            copies.append(self.remote(self.acc2, self.out.at[own], 33 + step, to))
        self.launch(copies)
        self.out[own] = self.acc2[...]

    def step5(self):
        ring = self.ring
        finish(self.flying)
        own = self.out.at[span(ring.core * HALF, HALF)]
        self.launch([self.remote(own, own, 37, ring.twin)])

    def step6(self):
        finish(self.flying)


def lane_of(dims):
    return lax.broadcasted_iota(jnp.int32, dims, len(dims) - 1)


def conv_window(field, i, y):
    return rows(
        [
            lanes(
                [
                    field[i + 4 * h + k, pl.ds(y + e, 3)].reshape(192, 128)
                    for e in range(2)
                    for h in range(2)
                ]
            )
            for k in range(3)
        ]
    )


def join_taps(taps, lane):
    back = jnp.where(lane == 0, 0.0, pltpu.roll(taps[0:64], 1, 1))
    ahead = jnp.where(lane == 127, 0.0, pltpu.roll(taps[128:192], 127, 1))
    return taps[64:128] + back + ahead


def main_body(
    skip,
    cot,
    coarse,
    upw,
    wc,
    wb,
    bias,
    mask_row,
    coarse_mask,
    spread_up,
    gather_z,
    feat,
    gs,
    low,
    total,
    sf,
    cf,
    mf,
    masks,
    cot_t,
    wu,
    wt,
    ac,
    ups,
    mx,
    gpf,
    g3,
    gacc,
    d4,
    acc,
    part,
    part_in,
    mine,
    got0,
    got1,
    got2,
    acc1,
    acc2,
    halo_send,
    halo_recv,
    sum_send,
    sum_recv,
):
    ring = Ring()
    barrier = pltpu.get_barrier_semaphore()
    for dx, dy in AROUND:
        pl.semaphore_signal(barrier, inc=1, device_id=neighbour(dx, dy), device_id_type=MESH)
    greeted = ring.greet(barrier) + len(AROUND)
    lane = lane_of((64, 128))

    keep = coarse_mask[...] > 0.5

    def fill_coarse(t, carry):
        x, y = t // 4, t % 4
        cf[x + 1, y + 1] = jnp.where(keep, coarse[x, y].astype(F32), 0.0).astype(BF)
        return carry

    lax.fori_loop(0, 16, fill_coarse, 0)
    mf[1, 1] = mask_row[...]
    pl.semaphore_wait(barrier, greeted)
    coarse_copies = halo_copies(cf, cf, halo_send, halo_recv, 0)
    mask_copies = halo_copies(mf, mf, halo_send, halo_recv, 8)
    start(coarse_copies)
    start(mask_copies)

    def fill_skip(x, carry):
        sf[x + 1, pl.ds(1, 8)] = jnp.swapaxes(skip[:, x], 0, 1)
        return carry

    lax.fori_loop(0, 8, fill_skip, 0)
    skip_copies = halo_copies(sf, sf, halo_send, halo_recv, 16)
    start(skip_copies)

    def fill_cot(x, carry):
        cot_t[x] = jnp.swapaxes(cot[:, x], 0, 1)
        return carry

    lax.fori_loop(0, 8, fill_cot, 0)
    for sx in range(2):
        for sy in range(2):
            for tx in range(2):
                for ty in range(2):
                    block = upw[2 + sx - 2 * tx, 2 + sy - 2 * ty].reshape(256, 128)
                    at, col = (sx * 2 + sy) * 256, (tx * 2 + ty) * 128
                    wu[at : at + 256, col : col + 128] = block
                    wt[sy, col : col + 128, sx * 256 : sx * 256 + 256] = block.T
    finish(coarse_copies)
    clear_outside(cf)

    def pair_coarse(t, carry):
        i, y = t // 6, t % 6
        ac[i, y] = rows([cf[i, y], cf[i + 2, y]]).T
        return carry

    lax.fori_loop(0, 24, pair_coarse, 0)

    def join(p, q, taps):
        wide = rows(
            [
                lanes([taps[(s * 4 + kz) * 64 : (s * 4 + kz + 1) * 64] for kz in range(4)])
                for s in range(4)
            ]
        )
        up = mm(wide, spread_up[...])
        for s in range(4):
            for h in range(2):
                ups[2 * p + s // 2 + 4 * h, 2 * q + s % 2] = up[
                    s * 64 : s * 64 + 64, h * 128 : h * 128 + 128
                ]

    def up_pair(t, carry):
        p, q = t // 2, (t % 2) * 2
        window = lanes([ac[pl.ds(p, 2), pl.ds(q + e, 2)].reshape(512, 128) for e in range(2)])
        taps = mm(wu[...], window).astype(BF)
        for e in range(2):
            join(p, q + e, taps[:, e * 128 : e * 128 + 128])
        return carry

    lax.fori_loop(0, 6, up_pair, 0)

    def up_last(p, carry):
        join(p, 4, mm(wu[...], ac[pl.ds(p, 2), pl.ds(4, 2)].reshape(512, 128)).astype(BF))
        return carry

    lax.fori_loop(0, 3, up_last, 0)

    finish(mask_copies)
    clear_outside(mf)
    for bx in range(3):
        for by in range(3):
            masks[bx, by] = mf[bx, by].astype(F32)
    finish(skip_copies)

    def mix(t, carry):
        x, y = t // 10, t % 10
        bx = jnp.where(x == 0, 0, jnp.where(x == 9, 2, 1))
        by = jnp.where(y == 0, 0, jnp.where(y == 9, 2, 1))
        value = ups[x, y] + sf[x, y].astype(F32)
        mx[x, y] = jnp.where(masks[bx, by, 0:1, :] > 0.5, value, 0.0).astype(BF)
        return carry

    lax.fori_loop(0, 100, mix, 0, unroll=2)

    inside = masks[1, 1, 0:1, :] > 0.5

    def conv(i, y):
        taps = mm(wc[...], conv_window(mx, i, y))
        for e in range(2):
            for h in range(2):
                at = (e * 2 + h) * 128
                pre = join_taps(taps[:, at : at + 128], lane) + bias[...]
                sig = 1.0 / (1.0 + jnp.exp(-pre))
                feat[i + 4 * h, y + e] = jnp.where(inside, pre * sig, 0.0).astype(BF)
                slope = sig * (1.0 + pre * (1.0 - sig))
                grad = cot_t[i + 4 * h, y + e].astype(F32) * slope
                grad = jnp.where(inside, grad, 0.0).astype(BF)
                gpf[i + 4 * h + 1, y + e + 1] = grad
                wide = grad.astype(F32)
                before = jnp.where(lane == 127, 0.0, pltpu.roll(wide, 127, 1)).astype(BF)
                after = jnp.where(lane == 0, 0.0, pltpu.roll(wide, 1, 1)).astype(BF)
                g3[i, y + e, :, h * 128 : h * 128 + 128] = rows([before, grad, after])

    def conv_outer(t, carry):
        conv(t // 2, (t % 2) * 6)
        return carry

    def conv_inner(t, carry):
        conv(t // 2, 2 + (t % 2) * 2)
        return carry

    gp_copies = halo_copies(gpf, gpf, halo_send, halo_recv, 24)
    lax.fori_loop(0, 8, conv_outer, 0)
    start(gp_copies[0:2])
    start(gp_copies[4:8])
    lax.fori_loop(0, 8, conv_inner, 0)
    start(gp_copies[2:4])

    gacc[...] = jnp.zeros_like(gacc)

    def kernel_grad(t, carry):
        i, y = t // 2, (t % 2) * 4
        grads = lanes([g3[i, y + j] for j in range(4)])
        for k in range(3):
            cells = lanes(
                [
                    mx[i + 4 * h + k, pl.ds(y + j, 3)].reshape(192, 128)
                    for j in range(4)
                    for h in range(2)
                ]
            )
            gacc[k * 192 : k * 192 + 192, :] += mm_t(cells, grads)
        gacc[576:592, :] += mm_t(jnp.ones((16, 1024), BF), grads)
        return carry

    lax.fori_loop(0, 8, kernel_grad, 0)
    mine[2, 0:592] = gacc[:, 0:128].astype(BF)
    mine[2, 592:1184, 0:64] = gacc[:, 128:192].astype(BF)
    mine[2, 592:1184, 64:128] = jnp.zeros((592, 64), BF)
    mine[2, 1184:PIECE] = jnp.zeros((PIECE - 1184, 128), BF)
    sums = [
        Piece(ring, at, mine, got0, got1, got2, acc1, acc2, total, sum_send, sum_recv)
        for at in range(3)
    ]
    sums[2].step0()

    finish(gp_copies)
    clear_outside(gpf)

    def back(t, carry):
        i, y = t // 4, (t % 4) * 2
        taps = mm(wb[...], conv_window(gpf, i, y))
        for e in range(2):
            both = []
            for h in range(2):
                at = (e * 2 + h) * 128
                grad = join_taps(taps[:, at : at + 128], lane)
                grad = jnp.where(inside, grad, 0.0).astype(BF)
                gs[i + 4 * h, y + e] = grad
                both.append(grad)
            apart = mm(lanes(both), gather_z[...]).astype(BF)
            for kz in range(4):
                d4[i, y + e, kz * 64 : kz * 64 + 64, :] = apart[:, kz * 128 : kz * 128 + 128]
        return carry

    lax.fori_loop(0, 8, back, 0)
    sums[2].step1()
    lax.fori_loop(8, 16, back, 0)
    sums[2].step2()

    def up_grad(sx, sy):
        spots = [(pi, qi) for pi in range(1 - sx, 3 - sx) for qi in range(1 - sy, 5 - sy)]
        grads = lanes([d4[2 * pi - 1 + sx, 2 * qi - 1 + sy] for pi, qi in spots])
        cells = rows(
            [
                lanes([ac[pi + tx, qi + ty] for pi, qi in spots])
                for tx in range(2)
                for ty in range(2)
            ]
        )
        result = mm_t(grads, cells).astype(BF)
        for tx in range(2):
            for ty in range(2):
                at, col = (tx * 4 + 2 + sy - 2 * ty) * 256, (tx * 2 + ty) * 128
                mine[sx, at : at + 256, :] = result[:, col : col + 128]

    up_grad(0, 0)
    up_grad(0, 1)
    sums[0].step0()
    sums[2].step3()
    up_grad(1, 0)
    up_grad(1, 1)
    sums[1].step0()
    sums[0].step1()
    sums[2].step4()

    acc[...] = jnp.zeros_like(acc)

    def lower(sy, across):
        if across == 1:
            weight = wt[sy]
            cells = rows([lanes([d4[1 + sx, 2 * q + 1 - sy] for q in range(4)]) for sx in range(2)])
        else:
            sx, i = (1, 0) if across == 0 else (0, 3)
            weight = wt[sy, :, sx * 256 : sx * 256 + 256]
            cells = lanes([d4[i, 2 * q + 1 - sy] for q in range(4)])
        result = mm(weight, cells)
        for tx in range(2):
            for ty in range(2):
                at = (tx * 2 + ty) * 128
                for q in range(4):
                    acc[across + tx, q + ty + 1 - sy] += result[
                        at : at + 128, q * 128 : q * 128 + 128
                    ]

    lower(0, 0)
    lower(1, 0)
    sums[1].step1()
    sums[0].step2()
    sums[2].step5()
    lower(0, 1)
    sums[1].step2()
    sums[0].step3()
    lower(1, 1)
    sums[1].step3()
    sums[0].step4()
    lower(0, 2)
    lower(1, 2)

    def turned(i, y):
        return acc[i, y].T

    def fold(y, carry):
        cells = [turned(i, y) for i in range(4)]
        left, right = [c[0:64] for c in cells], [c[64:128] for c in cells]
        folded = [
            left[0],
            left[1],
            left[2] + right[0],
            left[3] + right[1],
            right[2],
            right[3],
        ]
        for x in range(6):
            part[x, y] = folded[x].astype(BF)
        return carry

    lax.fori_loop(0, 6, fold, 0)
    part_copies = halo_copies(part, part_in, halo_send, halo_recv, 32, padding)
    start(part_copies)
    sums[1].step4()
    sums[0].step5()
    finish(part_copies)
    clear_outside(part_in)
    for x in range(4):
        for y in range(4):
            across = [x + 1] + [0] * (x == 0) + [5] * (x == 3)
            along = [y + 1] + [0] * (y == 0) + [5] * (y == 3)
            value = part[x + 1, y + 1].astype(F32)
            for px in across:
                for py in along:
                    if (px, py) != (x + 1, y + 1):
                        value += part_in[px, py].astype(F32)
            low[x, y] = jnp.where(keep, value, 0.0).astype(BF)
    sums[1].step5()
    sums[2].step6()
    sums[0].step6()
    sums[1].step6()


def spread_matrix():
    row, column = np.arange(512)[:, None], np.arange(256)[None, :]
    kz, h, j = row // 128, (row // 64) % 2, row % 64
    hit = (h == column // 128) & (column % 128 == 2 * j - 1 + kz)
    return hit.astype(ml_dtypes.bfloat16)


def body(coarse, skip, occupancy, cotangent, up_weight, conv_weight, conv_bias):
    active_z = occupancy[0, 0] > 0
    mask_row = jnp.broadcast_to(jnp.repeat(active_z, EDGE).astype(BF), (16, 128))
    coarse_mask = jnp.repeat(active_z, EDGE // 2).astype(F32)
    coarse_mask = jnp.broadcast_to(coarse_mask[:, None], (64, 128))
    coarse_n = jnp.transpose(coarse, (1, 2, 3, 0))
    upw = jnp.transpose(up_weight, (0, 1, 2, 4, 3))
    wc = jnp.transpose(conv_weight, (2, 4, 0, 1, 3)).reshape(192, 576)
    flipped = jnp.flip(conv_weight, (0, 1, 2))
    wb = jnp.transpose(flipped, (2, 3, 0, 1, 4)).reshape(192, 576)
    bias = jnp.broadcast_to(conv_bias[:, None], (64, 128))
    spread_up = spread_matrix()

    feat, gs, low, total = pl.pallas_call(
        main_body,
        out_shape=[
            shape((8, 8, 64, 128)),
            shape((8, 8, 64, 128)),
            shape((4, 4, 64, 128)),
            shape((3, PIECE, 128)),
        ],
        scratch_shapes=[
            pltpu.VMEM((10, 10, 64, 128), BF),
            pltpu.VMEM((6, 6, 64, 128), BF),
            pltpu.VMEM((3, 3, 16, 128), BF),
            pltpu.VMEM((3, 3, 16, 128), F32),
            pltpu.VMEM((8, 8, 64, 128), BF),
            pltpu.VMEM((1024, 512), BF),
            pltpu.VMEM((2, 512, 512), BF),
            pltpu.VMEM((4, 6, 128, 128), BF),
            pltpu.VMEM((10, 10, 64, 128), F32),
            pltpu.VMEM((10, 10, 64, 128), BF),
            pltpu.VMEM((10, 10, 64, 128), BF),
            pltpu.VMEM((4, 8, 192, 256), BF),
            pltpu.VMEM((C_ROWS, 192), F32),
            pltpu.VMEM((4, 8, 256, 128), BF),
            pltpu.VMEM((4, 6, 128, 128), F32),
            pltpu.VMEM((6, 6, 64, 128), BF),
            pltpu.VMEM((6, 6, 64, 128), BF),
            pltpu.VMEM((3, PIECE, 128), BF),
            pltpu.VMEM((3, HALF, 128), BF),
            pltpu.VMEM((3, 3, QUARTER, 128), BF),
            pltpu.VMEM((3, 15, CHUNK, 128), BF),
            pltpu.VMEM((3, QUARTER, 128), BF),
            pltpu.VMEM((3, QUARTER, 128), BF),
            pltpu.SemaphoreType.DMA((40,)),
            pltpu.SemaphoreType.DMA((40,)),
            pltpu.SemaphoreType.DMA((3 * 38,)),
            pltpu.SemaphoreType.DMA((3 * 38,)),
        ],
        compiler_params=pltpu.CompilerParams(
            vmem_limit_bytes=LIMIT, collective_id=1, has_side_effects=True
        ),
    )(
        skip,
        cotangent,
        coarse_n,
        upw,
        wc,
        wb,
        bias,
        mask_row,
        coarse_mask,
        spread_up,
        np.ascontiguousarray(spread_up.T),
    )

    features = jnp.transpose(feat, (2, 0, 1, 3))
    grad_skip = jnp.transpose(gs, (2, 0, 1, 3))
    grad_coarse = jnp.transpose(low, (3, 0, 1, 2))
    cells = 8192 * lax.axis_size("gx") * lax.axis_size("gy")
    scale = float(cells) ** -0.5
    up = total[0:2].reshape(2, 2, 4, 4, 64, 128)
    up = jnp.stack([up[0, 1], up[1, 1], up[0, 0], up[1, 0]]).astype(F32) * scale
    grad_up = jnp.transpose(up, (0, 1, 2, 4, 3))
    left = total[2, 0:C_ROWS].astype(F32) * scale
    right = total[2, C_ROWS : 2 * C_ROWS].astype(F32) * scale
    taps = jnp.stack([left[:576, 0:64], left[:576, 64:128], right[:576, 0:64]])
    grad_conv = jnp.transpose(taps.reshape(3, 3, 3, 64, 64), (1, 2, 0, 3, 4))
    grad_bias = left[576, 64:128]
    return features, grad_skip, grad_coarse, grad_up, grad_conv, grad_bias


def solution(mesh):
    field = P(None, "gx", "gy", None)
    return jax.shard_map(
        body,
        mesh=mesh,
        in_specs=(field, field, P("gx", "gy", None), field, P(), P(), P()),
        out_specs=(field, field, field, P(), P(), P()),
        check_vma=False,
    )
```

```python
import functools

import jax
import jax.numpy as jnp
import ml_dtypes
import numpy as np
from jax import lax
from jax.experimental import pallas as pl
from jax.experimental.pallas import tpu as pltpu
from jax.sharding import PartitionSpec as P

BF = jnp.bfloat16
F32 = jnp.float32
EDGE = 8
MESH = pl.DeviceIdType.MESH
LIMIT = 56 * 2**20

C_ROWS = 592
PIECE = 2048
HALF, QUARTER, CHUNK = PIECE // 2, PIECE // 8, PIECE // 128


def mm(a, b):
    return lax.dot_general(a, b, (((1,), (0,)), ((), ())), preferred_element_type=F32)


def mm_t(a, b):
    return lax.dot_general(a, b, (((1,), (1,)), ((), ())), preferred_element_type=F32)


def lanes(parts):
    return jnp.concatenate(parts, axis=1)


def rows(parts):
    return jnp.concatenate(parts, axis=0)


def shape(dims, kind=BF):
    return jax.ShapeDtypeStruct(dims, kind)


AROUND = [(0, 1), (0, -1), (1, 0), (-1, 0), (1, 1), (1, -1), (-1, 1), (-1, -1)]


def neighbour(dx, dy):
    nx, ny = lax.axis_size("gx"), lax.axis_size("gy")
    gx, gy = lax.axis_index("gx"), lax.axis_index("gy")
    return lax.rem(gx + (dx + nx), nx), lax.rem(gy + (dy + ny), ny)


def outer(step, count):
    if step == 0:
        return pl.ds(1, count), pl.ds(1, count)
    if step > 0:
        return pl.ds(count, 1), pl.ds(0, 1)
    return pl.ds(1, 1), pl.ds(count + 1, 1)


def padding(step, count):
    if step == 0:
        return pl.ds(1, count), pl.ds(1, count)
    if step > 0:
        return pl.ds(count + 1, 1), pl.ds(0, 1)
    return pl.ds(0, 1), pl.ds(count + 1, 1)


def halo_copies(source, target, send, recv, first, place=outer):
    across, along = source.shape[0] - 2, source.shape[1] - 2
    copies = []
    for at, (dx, dy) in enumerate(AROUND):
        sx, tx = place(dx, across)
        sy, ty = place(dy, along)
        copies.append(
            pltpu.make_async_remote_copy(
                src_ref=source.at[sx, sy],
                dst_ref=target.at[tx, ty],
                send_sem=send.at[first + at],
                recv_sem=recv.at[first + at],
                device_id=neighbour(dx, dy),
                device_id_type=MESH,
            )
        )
    return copies


def start(copies):
    for copy in copies:
        copy.start()


def finish(copies):
    for copy in copies:
        copy.wait()


def clear_outside(field):
    across, along = field.shape[0], field.shape[1]
    nx, ny = lax.axis_size("gx"), lax.axis_size("gy")
    gx, gy = lax.axis_index("gx"), lax.axis_index("gy")
    row = jnp.zeros((1,) + field.shape[1:], field.dtype)
    column = jnp.zeros((across, 1) + field.shape[2:], field.dtype)

    @pl.when(gx == 0)
    def _():
        field[0:1] = row

    @pl.when(gx == nx - 1)
    def _():
        field[across - 1 : across] = row

    @pl.when(gy == 0)
    def _():
        field[:, 0:1] = column

    @pl.when(gy == ny - 1)
    def _():
        field[:, along - 1 : along] = column


class Ring:
    def __init__(self):
        gx, gy = lax.axis_index("gx"), lax.axis_index("gy")
        self.core = lax.rem(gx, 2)
        self.x, self.y = gx // 4, gy // 2
        self.z = lax.rem(gy, 2) * 2 + lax.rem(gx // 2, 2)
        self.first = jnp.where(self.core == 0, self.x, self.y)
        self.second = jnp.where(self.core == 0, self.y, self.x)
        self.place = self.second * 4 + self.z
        self.twin = self.device(self.x, self.y, self.z, 1 - self.core)

    def device(self, x, y, z, core):
        return x * 4 + lax.rem(z, 2) * 2 + core, y * 2 + z // 2

    def along_first(self, step):
        other = lax.rem(self.first + step, 4)
        x = jnp.where(self.core == 0, other, self.x)
        y = jnp.where(self.core == 0, self.y, other)
        return other, self.device(x, y, self.z, self.core)

    def in_plane(self, step):
        a, b = lax.rem(self.second + step // 4, 4), lax.rem(self.z + step % 4, 4)
        x = jnp.where(self.core == 0, self.x, a)
        y = jnp.where(self.core == 0, a, self.y)
        return a * 4 + b, self.device(x, y, b, self.core)

    def greet(self, barrier):
        partners = [self.twin]
        partners += [self.along_first(step)[1] for step in range(1, 4)]
        partners += [self.in_plane(step)[1] for step in range(1, 16)]
        for partner in partners:
            pl.semaphore_signal(barrier, inc=1, device_id=partner, device_id_type=MESH)
        return len(partners)


def span(begin, count):
    return pl.ds(pl.multiple_of(begin, 16), count)


class Piece:
    def __init__(self, ring, index, mine, got0, got1, got2, acc1, acc2, out, send, recv):
        self.ring, self.base = ring, index * 38
        self.mine, self.got0, self.got1 = mine.at[index], got0.at[index], got1.at[index]
        self.got2, self.acc1, self.acc2 = got2.at[index], acc1.at[index], acc2.at[index]
        self.out, self.send, self.recv = out.at[index], send, recv
        self.flying = []

    def remote(self, src, dst, at, to):
        return pltpu.make_async_remote_copy(
            src_ref=src,
            dst_ref=dst,
            send_sem=self.send.at[self.base + at],
            recv_sem=self.recv.at[self.base + at],
            device_id=to,
            device_id_type=MESH,
        )

    def launch(self, copies):
        start(copies)
        self.flying = copies

    def step0(self):
        ring = self.ring
        theirs = self.mine.at[span((1 - ring.core) * HALF, HALF)]
        self.launch([self.remote(theirs, self.got0, 0, ring.twin)])

    def step1(self):
        ring = self.ring
        finish(self.flying)

        def add(t, carry):
            own = self.mine[span(ring.core * HALF + t * 256, 256)].astype(F32)
            at = span(t * 256, 256)
            self.got0[at] = (own + self.got0[at].astype(F32)).astype(BF)
            return carry

        lax.fori_loop(0, HALF // 256, add, 0)
        copies = []
        for step in range(1, 4):
            other, to = ring.along_first(step)
            theirs = self.got0.at[span(other * QUARTER, QUARTER)]
            copies.append(self.remote(theirs, self.got1.at[step - 1], step, to))
        self.launch(copies)

    def step2(self):
        ring = self.ring
        finish(self.flying)
        total = self.got0[span(ring.first * QUARTER, QUARTER)].astype(F32)
        for step in range(3):
            total += self.got1[step].astype(F32)
        self.acc1[...] = total.astype(BF)
        copies = []
        for step in range(1, 16):
            other, to = ring.in_plane(step)
            theirs = self.acc1.at[span(other * CHUNK, CHUNK)]
            copies.append(self.remote(theirs, self.got2.at[step - 1], 3 + step, to))
        self.launch(copies)

    def step3(self):
        ring = self.ring
        finish(self.flying)
        total = self.acc1[span(ring.place * CHUNK, CHUNK)].astype(F32)
        for step in range(15):
            total += self.got2[step].astype(F32)
        own = span(ring.place * CHUNK, CHUNK)
        self.acc2[own] = total.astype(BF)
        copies = []
        for step in range(1, 16):
            other, to = ring.in_plane(step)
            copies.append(self.remote(self.acc2.at[own], self.acc2.at[own], 18 + step, to))
        self.launch(copies)

    def step4(self):
        ring = self.ring
        finish(self.flying)
        own = span(ring.core * HALF + ring.first * QUARTER, QUARTER)
        copies = []
        for step in range(1, 4):
            other, to = ring.along_first(step)
            copies.append(self.remote(self.acc2, self.out.at[own], 33 + step, to))
        self.launch(copies)
        self.out[own] = self.acc2[...]

    def step5(self):
        ring = self.ring
        finish(self.flying)
        own = self.out.at[span(ring.core * HALF, HALF)]
        self.launch([self.remote(own, own, 37, ring.twin)])

    def step6(self):
        finish(self.flying)


def lane_of(dims):
    return lax.broadcasted_iota(jnp.int32, dims, len(dims) - 1)


def conv_window(field, i, y):
    return rows(
        [
            lanes(
                [
                    field[i + 4 * h + k, pl.ds(y + e, 3)].reshape(192, 128)
                    for e in range(2)
                    for h in range(2)
                ]
            )
            for k in range(3)
        ]
    )


def join_taps(taps, lane):
    back = jnp.where(lane == 0, 0.0, pltpu.roll(taps[0:64], 1, 1))
    ahead = jnp.where(lane == 127, 0.0, pltpu.roll(taps[128:192], 127, 1))
    return taps[64:128] + back + ahead


def main_body(
    skip_any,
    cot_any,
    upw_any,
    coarse,
    convw,
    conv_bias,
    occupancy,
    spread_up,
    gather_z,
    wide_rows,
    wide_columns,
    feat_any,
    gs_any,
    low,
    total,
    skip,
    cot,
    upw,
    feat,
    gs,
    feat_t,
    gs_t,
    local_sem,
    sf,
    cf,
    mf,
    masks,
    keep_ref,
    bias,
    cot_t,
    wc,
    wb,
    wu,
    wt,
    ac,
    ups,
    mx,
    gpf,
    g3,
    gacc,
    d4,
    acc,
    part,
    part_in,
    mine,
    got0,
    got1,
    got2,
    acc1,
    acc2,
    halo_send,
    halo_recv,
    sum_send,
    sum_recv,
):
    ring = Ring()
    barrier = pltpu.get_barrier_semaphore()
    for dx, dy in AROUND:
        pl.semaphore_signal(barrier, inc=1, device_id=neighbour(dx, dy), device_id_type=MESH)
    greeted = ring.greet(barrier) + len(AROUND)
    loads = [
        pltpu.make_async_copy(skip_any, skip, local_sem.at[0]),
        pltpu.make_async_copy(cot_any, cot, local_sem.at[1]),
        pltpu.make_async_copy(upw_any, upw, local_sem.at[2]),
    ]
    start(loads)
    lane = lane_of((64, 128))

    there = jnp.where(occupancy[0] > 0, 1.0, 0.0)
    mf[1, 1] = mm(jnp.broadcast_to(there, (16, 16)).astype(BF), wide_rows[...]).astype(BF)
    keep_ref[...] = mm_t(wide_columns[...], jnp.broadcast_to(there, (128, 16)).astype(BF))

    def fill_coarse(t, carry):
        x, y = t // 4, t % 4
        own = jnp.where(keep_ref[...] > 0.5, coarse[x, y].astype(F32), 0.0)
        cf[x + 1, y + 1] = own.astype(BF)
        return carry

    lax.fori_loop(0, 16, fill_coarse, 0, unroll=4)
    pl.semaphore_wait(barrier, greeted)
    coarse_copies = halo_copies(cf, cf, halo_send, halo_recv, 0)
    mask_copies = halo_copies(mf, mf, halo_send, halo_recv, 8)
    start(coarse_copies)
    start(mask_copies)

    loads[0].wait()

    def fill_skip(x, carry):
        sf[x + 1, pl.ds(1, 8)] = jnp.swapaxes(skip[:, x], 0, 1)
        return carry

    lax.fori_loop(0, 8, fill_skip, 0, unroll=2)
    skip_copies = halo_copies(sf, sf, halo_send, halo_recv, 16)
    start(skip_copies)

    loads[1].wait()

    def fill_cot(x, carry):
        cot_t[x] = jnp.swapaxes(cot[:, x], 0, 1)
        return carry

    lax.fori_loop(0, 8, fill_cot, 0, unroll=2)
    bias[...] = jnp.broadcast_to(conv_bias[...], (128, 64)).T
    for kz in range(3):
        for pair in range(5):
            taps = [(k // 3, k % 3) for k in (2 * pair, 2 * pair + 1) if k < 9]
            fore = [convw[kx, ky, kz] for kx, ky in taps]
            aft = [convw[2 - kx, 2 - ky, 2 - kz] for kx, ky in taps]
            at, col = kz * 64, pair * 128
            wide = 64 * len(taps)
            wc[at : at + 64, col : col + wide] = rows(fore).T
            wb[at : at + 64, col : col + wide] = lanes(aft)
    loads[2].wait()
    for sx in range(2):
        for sy in range(2):
            for tx in range(2):
                for ty in range(2):
                    block = upw[2 + sx - 2 * tx, 2 + sy - 2 * ty].reshape(256, 128)
                    at, col = (sx * 2 + sy) * 256, (tx * 2 + ty) * 128
                    wu[at : at + 256, col : col + 128] = block
                    wt[sy, col : col + 128, sx * 256 : sx * 256 + 256] = block.T
    finish(coarse_copies)
    clear_outside(cf)

    def pair_coarse(t, carry):
        i, y = t // 6, t % 6
        ac[i, y] = rows([cf[i, y], cf[i + 2, y]]).T
        return carry

    lax.fori_loop(0, 24, pair_coarse, 0, unroll=4)

    def join(p, q, taps):
        wide = rows(
            [
                lanes([taps[(s * 4 + kz) * 64 : (s * 4 + kz + 1) * 64] for kz in range(4)])
                for s in range(4)
            ]
        )
        up = mm(wide, spread_up[...])
        for s in range(4):
            for h in range(2):
                ups[2 * p + s // 2 + 4 * h, 2 * q + s % 2] = up[
                    s * 64 : s * 64 + 64, h * 128 : h * 128 + 128
                ]

    def up_pair(t, carry):
        p, q = t // 2, (t % 2) * 2
        window = lanes([ac[pl.ds(p, 2), pl.ds(q + e, 2)].reshape(512, 128) for e in range(2)])
        taps = mm(wu[...], window).astype(BF)
        for e in range(2):
            join(p, q + e, taps[:, e * 128 : e * 128 + 128])
        return carry

    lax.fori_loop(0, 6, up_pair, 0, unroll=2)

    def up_last(p, carry):
        join(p, 4, mm(wu[...], ac[pl.ds(p, 2), pl.ds(4, 2)].reshape(512, 128)).astype(BF))
        return carry

    lax.fori_loop(0, 3, up_last, 0, unroll=3)

    finish(mask_copies)
    clear_outside(mf)
    for bx in range(3):
        for by in range(3):
            masks[bx, by] = mf[bx, by].astype(F32)
    finish(skip_copies)

    def mix(t, carry):
        x, y = t // 10, t % 10
        bx = jnp.where(x == 0, 0, jnp.where(x == 9, 2, 1))
        by = jnp.where(y == 0, 0, jnp.where(y == 9, 2, 1))
        value = ups[x, y] + sf[x, y].astype(F32)
        mx[x, y] = jnp.where(masks[bx, by, 0:1, :] > 0.5, value, 0.0).astype(BF)
        return carry

    lax.fori_loop(0, 100, mix, 0, unroll=4)

    inside = masks[1, 1, 0:1, :] > 0.5

    def conv(i, y):
        taps = mm(wc[...], conv_window(mx, i, y))
        for e in range(2):
            for h in range(2):
                at = (e * 2 + h) * 128
                pre = join_taps(taps[:, at : at + 128], lane) + bias[...]
                sig = 1.0 / (1.0 + jnp.exp(-pre))
                feat[i + 4 * h, y + e] = jnp.where(inside, pre * sig, 0.0).astype(BF)
                slope = sig * (1.0 + pre * (1.0 - sig))
                grad = cot_t[i + 4 * h, y + e].astype(F32) * slope
                grad = jnp.where(inside, grad, 0.0).astype(BF)
                gpf[i + 4 * h + 1, y + e + 1] = grad
                wide = grad.astype(F32)
                before = jnp.where(lane == 127, 0.0, pltpu.roll(wide, 127, 1)).astype(BF)
                after = jnp.where(lane == 0, 0.0, pltpu.roll(wide, 1, 1)).astype(BF)
                g3[i, y + e, :, h * 128 : h * 128 + 128] = rows([before, grad, after])

    def conv_outer(t, carry):
        conv(t // 2, (t % 2) * 6)
        return carry

    def conv_inner(t, carry):
        conv(t // 2, 2 + (t % 2) * 2)
        return carry

    gp_copies = halo_copies(gpf, gpf, halo_send, halo_recv, 24)
    lax.fori_loop(0, 8, conv_outer, 0, unroll=4)
    start(gp_copies[0:2])
    start(gp_copies[4:8])
    lax.fori_loop(0, 8, conv_inner, 0, unroll=4)
    start(gp_copies[2:4])

    gacc[...] = jnp.zeros_like(gacc)

    def kernel_grad(t, carry):
        i, y = t // 2, (t % 2) * 4
        grads = lanes([g3[i, y + j] for j in range(4)])
        for k in range(3):
            cells = lanes(
                [
                    mx[i + 4 * h + k, pl.ds(y + j, 3)].reshape(192, 128)
                    for j in range(4)
                    for h in range(2)
                ]
            )
            gacc[k * 192 : k * 192 + 192, :] += mm_t(cells, grads)
        gacc[576:592, :] += mm_t(jnp.ones((16, 1024), BF), grads)
        return carry

    lax.fori_loop(0, 8, kernel_grad, 0, unroll=4)
    mine[2, 0:592] = gacc[:, 0:128].astype(BF)
    mine[2, 592:1184, 0:64] = gacc[:, 128:192].astype(BF)
    mine[2, 592:1184, 64:128] = jnp.zeros((592, 64), BF)
    mine[2, 1184:PIECE] = jnp.zeros((PIECE - 1184, 128), BF)
    sums = [
        Piece(ring, at, mine, got0, got1, got2, acc1, acc2, total, sum_send, sum_recv)
        for at in range(3)
    ]
    sums[2].step0()

    finish(gp_copies)
    clear_outside(gpf)

    def back(t, carry):
        i, y = t // 4, (t % 4) * 2
        taps = mm(wb[...], conv_window(gpf, i, y))
        for e in range(2):
            both = []
            for h in range(2):
                at = (e * 2 + h) * 128
                grad = join_taps(taps[:, at : at + 128], lane)
                grad = jnp.where(inside, grad, 0.0).astype(BF)
                gs[i + 4 * h, y + e] = grad
                both.append(grad)
            apart = mm(lanes(both), gather_z[...]).astype(BF)
            for kz in range(4):
                d4[i, y + e, kz * 64 : kz * 64 + 64, :] = apart[:, kz * 128 : kz * 128 + 128]
        return carry

    lax.fori_loop(0, 4, back, 0, unroll=4)
    sums[2].step1()
    lax.fori_loop(4, 8, back, 0, unroll=4)
    sums[2].step2()
    lax.fori_loop(8, 12, back, 0, unroll=4)
    sums[2].step3()
    lax.fori_loop(12, 16, back, 0, unroll=4)
    sums[2].step4()

    def up_grad(sx, sy):
        spots = [(pi, qi) for pi in range(1 - sx, 3 - sx) for qi in range(1 - sy, 5 - sy)]
        grads = lanes([d4[2 * pi - 1 + sx, 2 * qi - 1 + sy] for pi, qi in spots])
        cells = rows(
            [
                lanes([ac[pi + tx, qi + ty] for pi, qi in spots])
                for tx in range(2)
                for ty in range(2)
            ]
        )
        result = mm_t(grads, cells).astype(BF)
        for tx in range(2):
            for ty in range(2):
                at, col = (tx * 4 + 2 + sy - 2 * ty) * 256, (tx * 2 + ty) * 128
                mine[sx, at : at + 256, :] = result[:, col : col + 128]

    up_grad(0, 0)
    up_grad(0, 1)
    sums[0].step0()
    up_grad(1, 0)
    up_grad(1, 1)
    sums[1].step0()

    acc[...] = jnp.zeros_like(acc)

    def lower(sy, across):
        if across == 1:
            weight = wt[sy]
            cells = rows([lanes([d4[1 + sx, 2 * q + 1 - sy] for q in range(4)]) for sx in range(2)])
        else:
            sx, i = (1, 0) if across == 0 else (0, 3)
            weight = wt[sy, :, sx * 256 : sx * 256 + 256]
            cells = lanes([d4[i, 2 * q + 1 - sy] for q in range(4)])
        result = mm(weight, cells)
        for tx in range(2):
            for ty in range(2):
                at = (tx * 2 + ty) * 128
                for q in range(4):
                    acc[across + tx, q + ty + 1 - sy] += result[
                        at : at + 128, q * 128 : q * 128 + 128
                    ]

    lower(0, 0)
    lower(1, 0)
    lower(0, 1)
    sums[0].step1()
    lower(1, 1)
    lower(0, 2)
    lower(1, 2)
    sums[1].step1()
    sums[2].step5()

    def turned(i, y):
        return acc[i, y].T

    def fold(y, carry):
        cells = [turned(i, y) for i in range(4)]
        left, right = [c[0:64] for c in cells], [c[64:128] for c in cells]
        folded = [
            left[0],
            left[1],
            left[2] + right[0],
            left[3] + right[1],
            right[2],
            right[3],
        ]
        for x in range(6):
            part[x, y] = folded[x].astype(BF)
        return carry

    lax.fori_loop(0, 6, fold, 0)
    part_copies = halo_copies(part, part_in, halo_send, halo_recv, 32, padding)
    start(part_copies)
    sums[0].step2()
    sums[1].step2()

    def turn_feat(x, carry):
        feat_t[:, x] = jnp.swapaxes(feat[x], 0, 1)
        return carry

    lax.fori_loop(0, 8, turn_feat, 0, unroll=2)
    stores = [
        pltpu.make_async_copy(feat_t, feat_any, local_sem.at[3]),
        pltpu.make_async_copy(gs_t, gs_any, local_sem.at[4]),
    ]
    start(stores[0:1])
    sums[0].step3()
    sums[1].step3()

    def turn_gs(x, carry):
        gs_t[:, x] = jnp.swapaxes(gs[x], 0, 1)
        return carry

    lax.fori_loop(0, 8, turn_gs, 0, unroll=2)
    start(stores[1:2])
    sums[0].step4()
    sums[1].step4()
    finish(part_copies)
    clear_outside(part_in)
    for x in range(4):
        for y in range(4):
            across = [x + 1] + [0] * (x == 0) + [5] * (x == 3)
            along = [y + 1] + [0] * (y == 0) + [5] * (y == 3)
            value = part[x + 1, y + 1].astype(F32)
            for px in across:
                for py in along:
                    if (px, py) != (x + 1, y + 1):
                        value += part_in[px, py].astype(F32)
            low[x, y] = jnp.where(keep_ref[...] > 0.5, value, 0.0).astype(BF)
    sums[0].step5()
    sums[1].step5()
    sums[2].step6()
    finish(stores)
    sums[0].step6()
    sums[1].step6()


def final_body(
    scale, feat, gs, low, total, features, grad_skip, grad_coarse, up, conv, bias, v0, v1, v2, sem
):
    arrive = [
        pltpu.make_async_copy(feat, v0, sem.at[0]),
        pltpu.make_async_copy(gs, v1, sem.at[1]),
        pltpu.make_async_copy(low, v2, sem.at[2]),
    ]
    leave = [
        pltpu.make_async_copy(v0, features, sem.at[3]),
        pltpu.make_async_copy(v1, grad_skip, sem.at[4]),
        pltpu.make_async_copy(v2, grad_coarse, sem.at[5]),
    ]
    start(arrive)
    for come, go in zip(arrive, leave):
        come.wait()
        go.start()
    for kx in range(4):
        sx, tx = kx % 2, 1 - kx // 2

        def column(t, carry):
            block = total[sx, pl.ds(pl.multiple_of(tx * 1024 + t * 256, 256), 256)]
            up[kx, t] = (block.astype(F32) * scale).reshape(4, 64, 128)
            return carry

        lax.fori_loop(0, 4, column, 0)
    for tap in range(9):
        left = total[2, tap * 64 : tap * 64 + 64].astype(F32) * scale
        right = total[2, C_ROWS + tap * 64 : C_ROWS + tap * 64 + 64].astype(F32) * scale
        conv[tap // 3, tap % 3, 0] = left[:, 0:64]
        conv[tap // 3, tap % 3, 1] = left[:, 64:128]
        conv[tap // 3, tap % 3, 2] = right[:, 0:64]
    bias[...] = (total[2, 576:592].astype(F32) * scale)[0:1, 64:128]
    finish(leave)


def spread_matrix():
    row, column = np.arange(512)[:, None], np.arange(256)[None, :]
    kz, h, j = row // 128, (row // 64) % 2, row % 64
    hit = (h == column // 128) & (column % 128 == 2 * j - 1 + kz)
    return hit.astype(ml_dtypes.bfloat16)


def body(coarse, skip, occupancy, cotangent, up_weight, conv_weight, conv_bias):
    spread_up = spread_matrix()
    wide_rows = np.repeat(np.eye(16), EDGE, axis=1).astype(ml_dtypes.bfloat16)
    wide_columns = np.repeat(np.eye(16), EDGE // 2, axis=0).astype(ml_dtypes.bfloat16)
    vmem, anywhere = pl.BlockSpec(memory_space=pltpu.VMEM), pl.BlockSpec(memory_space=pl.ANY)
    plane = (64, 8, 8, 128)
    feat, gs, low, total = pl.pallas_call(
        main_body,
        out_shape=[shape(plane), shape(plane), shape((4, 4, 64, 128)), shape((3, PIECE, 128))],
        in_specs=[anywhere] * 3 + [vmem] * 8,
        out_specs=[anywhere] * 2 + [vmem] * 2,
        scratch_shapes=[
            pltpu.VMEM(plane, BF),
            pltpu.VMEM(plane, BF),
            pltpu.VMEM((4, 4, 4, 64, 128), BF),
            pltpu.VMEM((8, 8, 64, 128), BF),
            pltpu.VMEM((8, 8, 64, 128), BF),
            pltpu.VMEM(plane, BF),
            pltpu.VMEM(plane, BF),
            pltpu.SemaphoreType.DMA((5,)),
            pltpu.VMEM((10, 10, 64, 128), BF),
            pltpu.VMEM((6, 6, 64, 128), BF),
            pltpu.VMEM((3, 3, 16, 128), BF),
            pltpu.VMEM((3, 3, 16, 128), F32),
            pltpu.VMEM((64, 128), F32),
            pltpu.VMEM((64, 128), F32),
            pltpu.VMEM((8, 8, 64, 128), BF),
            pltpu.VMEM((192, 576), BF),
            pltpu.VMEM((192, 576), BF),
            pltpu.VMEM((1024, 512), BF),
            pltpu.VMEM((2, 512, 512), BF),
            pltpu.VMEM((4, 6, 128, 128), BF),
            pltpu.VMEM((10, 10, 64, 128), F32),
            pltpu.VMEM((10, 10, 64, 128), BF),
            pltpu.VMEM((10, 10, 64, 128), BF),
            pltpu.VMEM((4, 8, 192, 256), BF),
            pltpu.VMEM((C_ROWS, 192), F32),
            pltpu.VMEM((4, 8, 256, 128), BF),
            pltpu.VMEM((4, 6, 128, 128), F32),
            pltpu.VMEM((6, 6, 64, 128), BF),
            pltpu.VMEM((6, 6, 64, 128), BF),
            pltpu.VMEM((3, PIECE, 128), BF),
            pltpu.VMEM((3, HALF, 128), BF),
            pltpu.VMEM((3, 3, QUARTER, 128), BF),
            pltpu.VMEM((3, 15, CHUNK, 128), BF),
            pltpu.VMEM((3, QUARTER, 128), BF),
            pltpu.VMEM((3, QUARTER, 128), BF),
            pltpu.SemaphoreType.DMA((40,)),
            pltpu.SemaphoreType.DMA((40,)),
            pltpu.SemaphoreType.DMA((3 * 38,)),
            pltpu.SemaphoreType.DMA((3 * 38,)),
        ],
        compiler_params=pltpu.CompilerParams(
            vmem_limit_bytes=LIMIT, collective_id=1, has_side_effects=True
        ),
    )(
        skip,
        cotangent,
        jnp.transpose(up_weight, (0, 1, 2, 4, 3)),
        jnp.transpose(coarse, (1, 2, 3, 0)),
        conv_weight,
        conv_bias[None],
        occupancy[0],
        spread_up,
        np.ascontiguousarray(spread_up.T),
        wide_rows,
        wide_columns,
    )
    cells = 8192 * lax.axis_size("gx") * lax.axis_size("gy")
    features, grad_skip, low, up, grad_conv, bias = pl.pallas_call(
        functools.partial(final_body, float(cells) ** -0.5),
        out_shape=[
            shape(plane),
            shape(plane),
            shape((4, 4, 64, 128)),
            shape((4, 4, 4, 64, 128), F32),
            shape((3, 3, 3, 64, 64), F32),
            shape((1, 64), F32),
        ],
        in_specs=[anywhere] * 3 + [vmem],
        out_specs=[anywhere] * 3 + [vmem] * 3,
        scratch_shapes=[
            pltpu.VMEM(plane, BF),
            pltpu.VMEM(plane, BF),
            pltpu.VMEM((4, 4, 64, 128), BF),
            pltpu.SemaphoreType.DMA((6,)),
        ],
        compiler_params=pltpu.CompilerParams(vmem_limit_bytes=LIMIT),
    )(feat, gs, low, total)
    grad_coarse = jnp.transpose(low, (3, 0, 1, 2))
    grad_up = jnp.transpose(up, (0, 1, 2, 4, 3))
    return features, grad_skip, grad_coarse, grad_up, grad_conv, bias[0]


def solution(mesh):
    field = P(None, "gx", "gy", None)
    return jax.shard_map(
        body,
        mesh=mesh,
        in_specs=(field, field, P("gx", "gy", None), field, P(), P(), P()),
        out_specs=(field, field, field, P(), P(), P()),
        check_vma=False,
    )
```

```python
import functools

import jax
import jax.numpy as jnp
import ml_dtypes
import numpy as np
from jax import lax
from jax.experimental import pallas as pl
from jax.experimental.pallas import tpu as pltpu
from jax.sharding import PartitionSpec as P

BF = jnp.bfloat16
F32 = jnp.float32
EDGE = 8
MESH = pl.DeviceIdType.MESH
LIMIT = 56 * 2**20

C_ROWS = 592
SUB = 1024
HALF, QUARTER, CHUNK = 3 * SUB, 3 * SUB // 4, 3 * SUB // 64


def mm(a, b):
    return lax.dot_general(a, b, (((1,), (0,)), ((), ())), preferred_element_type=F32)


def mm_t(a, b):
    return lax.dot_general(a, b, (((1,), (1,)), ((), ())), preferred_element_type=F32)


def lanes(parts):
    return jnp.concatenate(parts, axis=1)


def rows(parts):
    return jnp.concatenate(parts, axis=0)


def shape(dims, kind=BF):
    return jax.ShapeDtypeStruct(dims, kind)


AROUND = [(0, 1), (0, -1), (1, 0), (-1, 0), (1, 1), (1, -1), (-1, 1), (-1, -1)]


def neighbour(dx, dy):
    nx, ny = lax.axis_size("gx"), lax.axis_size("gy")
    gx, gy = lax.axis_index("gx"), lax.axis_index("gy")
    return lax.rem(gx + (dx + nx), nx), lax.rem(gy + (dy + ny), ny)


def outer(step, count):
    if step == 0:
        return pl.ds(1, count), pl.ds(1, count)
    if step > 0:
        return pl.ds(count, 1), pl.ds(0, 1)
    return pl.ds(1, 1), pl.ds(count + 1, 1)


def padding(step, count):
    if step == 0:
        return pl.ds(1, count), pl.ds(1, count)
    if step > 0:
        return pl.ds(count + 1, 1), pl.ds(0, 1)
    return pl.ds(0, 1), pl.ds(count + 1, 1)


def halo_copies(source, target, send, recv, first, place=outer):
    across, along = source.shape[0] - 2, source.shape[1] - 2
    copies = []
    for at, (dx, dy) in enumerate(AROUND):
        sx, tx = place(dx, across)
        sy, ty = place(dy, along)
        copies.append(
            pltpu.make_async_remote_copy(
                src_ref=source.at[sx, sy],
                dst_ref=target.at[tx, ty],
                send_sem=send.at[first + at],
                recv_sem=recv.at[first + at],
                device_id=neighbour(dx, dy),
                device_id_type=MESH,
            )
        )
    return copies


def start(copies):
    for copy in copies:
        copy.start()


def finish(copies):
    for copy in copies:
        copy.wait()


def clear_outside(field):
    across, along = field.shape[0], field.shape[1]
    nx, ny = lax.axis_size("gx"), lax.axis_size("gy")
    gx, gy = lax.axis_index("gx"), lax.axis_index("gy")
    row = jnp.zeros((1,) + field.shape[1:], field.dtype)
    column = jnp.zeros((across, 1) + field.shape[2:], field.dtype)

    @pl.when(gx == 0)
    def _():
        field[0:1] = row

    @pl.when(gx == nx - 1)
    def _():
        field[across - 1 : across] = row

    @pl.when(gy == 0)
    def _():
        field[:, 0:1] = column

    @pl.when(gy == ny - 1)
    def _():
        field[:, along - 1 : along] = column


class Ring:
    def __init__(self):
        gx, gy = lax.axis_index("gx"), lax.axis_index("gy")
        self.core = lax.rem(gx, 2)
        self.x, self.y = gx // 4, gy // 2
        self.z = lax.rem(gy, 2) * 2 + lax.rem(gx // 2, 2)
        self.first = jnp.where(self.core == 0, self.x, self.y)
        self.second = jnp.where(self.core == 0, self.y, self.x)
        self.place = self.second * 4 + self.z
        self.twin = self.device(self.x, self.y, self.z, 1 - self.core)

    def device(self, x, y, z, core):
        return x * 4 + lax.rem(z, 2) * 2 + core, y * 2 + z // 2

    def along_first(self, step):
        other = lax.rem(self.first + step, 4)
        x = jnp.where(self.core == 0, other, self.x)
        y = jnp.where(self.core == 0, self.y, other)
        return other, self.device(x, y, self.z, self.core)

    def in_plane(self, step):
        a, b = lax.rem(self.second + step // 4, 4), lax.rem(self.z + step % 4, 4)
        x = jnp.where(self.core == 0, self.x, a)
        y = jnp.where(self.core == 0, a, self.y)
        return a * 4 + b, self.device(x, y, b, self.core)

    def across_first(self, step):
        x = jnp.where(self.core == 0, self.x, lax.rem(self.x + step, 4))
        y = jnp.where(self.core == 0, lax.rem(self.y + step, 4), self.y)
        return self.device(x, y, self.z, 1 - self.core)

    def both_cores(self, step):
        other = lax.rem(self.first + step, 4)
        x = jnp.where(self.core == 0, other, self.x)
        y = jnp.where(self.core == 0, self.y, other)
        return [self.device(x, y, self.z, self.core), self.device(x, y, self.z, 1 - self.core)]

    def greet(self, barrier):
        partners = [self.twin]
        partners += [self.along_first(step)[1] for step in range(1, 4)]
        partners += [self.across_first(step) for step in range(1, 4)]
        partners += [self.in_plane(step)[1] for step in range(1, 16)]
        for partner in partners:
            pl.semaphore_signal(barrier, inc=1, device_id=partner, device_id_type=MESH)
        return len(partners)


def span(begin, count):
    return pl.ds(pl.multiple_of(begin, 16), count)


class Sums:
    def __init__(self, ring, mine, got0, got1, got2, acc1, acc2, out, send, recv):
        self.ring, self.mine, self.out = ring, mine, out
        self.got0, self.got1, self.got2, self.acc1, self.acc2 = got0, got1, got2, acc1, acc2
        self.send, self.recv = send, recv
        self.flying = []

    def remote(self, src, dst, at, to):
        return pltpu.make_async_remote_copy(
            src_ref=src,
            dst_ref=dst,
            send_sem=self.send.at[at],
            recv_sem=self.recv.at[at],
            device_id=to,
            device_id_type=MESH,
        )

    def launch(self, copies):
        start(copies)
        self.flying = copies

    def step0(self, sub):
        ring = self.ring
        theirs = self.mine.at[1 - ring.core, sub]
        copy = self.remote(theirs, self.got0.at[pl.ds(sub * SUB, SUB)], sub, ring.twin)
        copy.start()
        self.flying = self.flying + [copy]

    def step1(self):
        ring = self.ring
        finish(self.flying)
        for sub in range(3):

            def add(t, carry):
                own = self.mine[ring.core, sub, span(t * 256, 256)].astype(F32)
                at = span(sub * SUB + t * 256, 256)
                self.got0[at] = (own + self.got0[at].astype(F32)).astype(BF)
                return carry

            lax.fori_loop(0, SUB // 256, add, 0)
        copies = []
        for step in range(1, 4):
            other, to = ring.along_first(step)
            theirs = self.got0.at[span(other * QUARTER, QUARTER)]
            copies.append(self.remote(theirs, self.got1.at[step - 1], 2 + step, to))
        self.launch(copies)

    def step2(self):
        ring = self.ring
        finish(self.flying)

        def add(t, carry):
            at = span(t * 256, 256)
            total = self.got0[span(ring.first * QUARTER + t * 256, 256)].astype(F32)
            for step in range(3):
                total += self.got1[step, at].astype(F32)
            self.acc1[at] = total.astype(BF)
            return carry

        lax.fori_loop(0, QUARTER // 256, add, 0)
        copies = []
        for step in range(1, 16):
            other, to = ring.in_plane(step)
            theirs = self.acc1.at[span(other * CHUNK, CHUNK)]
            copies.append(self.remote(theirs, self.got2.at[step - 1], 5 + step, to))
        self.launch(copies)

    def step3(self):
        ring = self.ring
        finish(self.flying)
        total = self.acc1[span(ring.place * CHUNK, CHUNK)].astype(F32)
        for step in range(15):
            total += self.got2[step].astype(F32)
        own = span(ring.place * CHUNK, CHUNK)
        self.acc2[own] = total.astype(BF)
        copies = []
        for step in range(1, 16):
            other, to = ring.in_plane(step)
            copies.append(self.remote(self.acc2.at[own], self.acc2.at[own], 20 + step, to))
        self.launch(copies)

    def step4(self):
        ring = self.ring
        finish(self.flying)
        own = span(ring.core * HALF + ring.first * QUARTER, QUARTER)
        copies = []
        for step in range(1, 4):
            for side, to in enumerate(ring.both_cores(step)):
                at = 35 + side * 3 + step
                copies.append(self.remote(self.acc2, self.out.at[own], at, to))
        copies.append(self.remote(self.acc2, self.out.at[own], 42, ring.twin))
        self.launch(copies)
        self.out[own] = self.acc2[...]

    def step5(self):
        finish(self.flying)


def lane_of(dims):
    return lax.broadcasted_iota(jnp.int32, dims, len(dims) - 1)


def conv_window(field, i, y):
    return rows(
        [
            lanes(
                [
                    field[i + 4 * h + k, pl.ds(y + e, 3)].reshape(192, 128)
                    for e in range(2)
                    for h in range(2)
                ]
            )
            for k in range(3)
        ]
    )


def join_taps(taps, lane):
    back = jnp.where(lane == 0, 0.0, pltpu.roll(taps[0:64], 1, 1))
    ahead = jnp.where(lane == 127, 0.0, pltpu.roll(taps[128:192], 127, 1))
    return taps[64:128] + back + ahead


def main_body(
    skip_any,
    cot_any,
    upw_any,
    coarse_any,
    convw_any,
    spread_any,
    gather_any,
    conv_bias,
    occupancy,
    wide_rows,
    wide_columns,
    feat_any,
    gs_any,
    low,
    total,
    skip,
    cot,
    upw,
    coarse,
    convw,
    spread_up,
    gather_z,
    feat,
    gs,
    feat_t,
    gs_t,
    local_sem,
    sf,
    cf,
    mf,
    masks,
    keep_ref,
    bias,
    cot_t,
    wc,
    wb,
    wu,
    wt,
    ac,
    ups,
    mx,
    gpf,
    g3,
    gacc,
    d4,
    acc,
    part,
    part_in,
    mine,
    got0,
    got1,
    got2,
    acc1,
    acc2,
    halo_send,
    halo_recv,
    sum_send,
    sum_recv,
):
    ring = Ring()
    barrier = pltpu.get_barrier_semaphore()
    for dx, dy in AROUND:
        pl.semaphore_signal(barrier, inc=1, device_id=neighbour(dx, dy), device_id_type=MESH)
    greeted = ring.greet(barrier) + len(AROUND)
    loads = [
        pltpu.make_async_copy(coarse_any, coarse, local_sem.at[5]),
        pltpu.make_async_copy(skip_any, skip, local_sem.at[0]),
        pltpu.make_async_copy(cot_any, cot, local_sem.at[1]),
        pltpu.make_async_copy(convw_any, convw, local_sem.at[6]),
        pltpu.make_async_copy(upw_any, upw, local_sem.at[2]),
        pltpu.make_async_copy(spread_any, spread_up, local_sem.at[7]),
        pltpu.make_async_copy(gather_any, gather_z, local_sem.at[8]),
    ]
    start(loads)
    lane = lane_of((64, 128))

    there = jnp.where(occupancy[0] > 0, 1.0, 0.0)
    mf[1, 1] = mm(jnp.broadcast_to(there, (16, 16)).astype(BF), wide_rows[...]).astype(BF)
    keep_ref[...] = mm_t(wide_columns[...], jnp.broadcast_to(there, (128, 16)).astype(BF))

    loads[0].wait()

    def fill_coarse(t, carry):
        x, y = t // 4, t % 4
        own = jnp.where(keep_ref[...] > 0.5, coarse[x, y].astype(F32), 0.0)
        cf[x + 1, y + 1] = own.astype(BF)
        return carry

    lax.fori_loop(0, 16, fill_coarse, 0, unroll=4)
    pl.semaphore_wait(barrier, greeted)
    coarse_copies = halo_copies(cf, cf, halo_send, halo_recv, 0)
    mask_copies = halo_copies(mf, mf, halo_send, halo_recv, 8)
    start(coarse_copies)
    start(mask_copies)

    loads[1].wait()

    def fill_skip(x, carry):
        sf[x + 1, pl.ds(1, 8)] = jnp.swapaxes(skip[:, x], 0, 1)
        return carry

    lax.fori_loop(0, 8, fill_skip, 0, unroll=2)
    skip_copies = halo_copies(sf, sf, halo_send, halo_recv, 16)
    start(skip_copies)

    loads[2].wait()

    def fill_cot(x, carry):
        cot_t[x] = jnp.swapaxes(cot[:, x], 0, 1)
        return carry

    lax.fori_loop(0, 8, fill_cot, 0, unroll=2)
    finish(loads[3:7])
    bias[...] = jnp.broadcast_to(conv_bias[...], (128, 64)).T
    for kz in range(3):
        for pair in range(5):
            taps = [(k // 3, k % 3) for k in (2 * pair, 2 * pair + 1) if k < 9]
            fore = [convw[kx, ky, kz] for kx, ky in taps]
            aft = [convw[2 - kx, 2 - ky, 2 - kz] for kx, ky in taps]
            at, col = kz * 64, pair * 128
            wide = 64 * len(taps)
            wc[at : at + 64, col : col + wide] = rows(fore).T
            wb[at : at + 64, col : col + wide] = lanes(aft)
    for sx in range(2):
        for sy in range(2):
            for tx in range(2):
                for ty in range(2):
                    block = upw[2 + sx - 2 * tx, 2 + sy - 2 * ty].reshape(256, 128)
                    at, col = (sx * 2 + sy) * 256, (tx * 2 + ty) * 128
                    wu[at : at + 256, col : col + 128] = block
                    wt[sy, col : col + 128, sx * 256 : sx * 256 + 256] = block.T

    def pair_coarse(i, y):
        ac[i, y] = rows([cf[i, y], cf[i + 2, y]]).T

    def pair_middle(t, carry):
        pair_coarse(1 + t // 4, 1 + t % 4)
        return carry

    def pair_across(t, carry):
        pair_coarse((t // 6) * 3, t % 6)
        return carry

    def pair_along(t, carry):
        pair_coarse(1 + t // 2, (t % 2) * 5)
        return carry

    def join(p, q, taps):
        wide = rows(
            [
                lanes([taps[(s * 4 + kz) * 64 : (s * 4 + kz + 1) * 64] for kz in range(4)])
                for s in range(4)
            ]
        )
        up = mm(wide, spread_up[...])
        for s in range(4):
            for h in range(2):
                ups[2 * p + s // 2 + 4 * h, 2 * q + s % 2] = up[
                    s * 64 : s * 64 + 64, h * 128 : h * 128 + 128
                ]

    def upsample(blocks):
        window = lanes([ac[p : p + 2, q : q + 2].reshape(512, 128) for p, q in blocks])
        taps = mm(wu[...], window).astype(BF)
        for at, (p, q) in enumerate(blocks):
            join(p, q, taps[:, at * 128 : at * 128 + 128])

    lax.fori_loop(0, 8, pair_middle, 0, unroll=4)
    upsample([(1, 1), (1, 2), (1, 3)])
    finish(coarse_copies)
    clear_outside(cf)
    lax.fori_loop(0, 12, pair_across, 0, unroll=4)
    lax.fori_loop(0, 4, pair_along, 0, unroll=4)
    for p in (0, 2):
        upsample([(p, 0), (p, 1)])
        upsample([(p, 2), (p, 3)])
        upsample([(p, 4), (1, p * 2)])

    finish(mask_copies)
    clear_outside(mf)
    for bx in range(3):
        for by in range(3):
            masks[bx, by] = mf[bx, by].astype(F32)

    def mix(x, y):
        bx = jnp.where(x == 0, 0, jnp.where(x == 9, 2, 1))
        by = jnp.where(y == 0, 0, jnp.where(y == 9, 2, 1))
        value = ups[x, y] + sf[x, y].astype(F32)
        mx[x, y] = jnp.where(masks[bx, by, 0:1, :] > 0.5, value, 0.0).astype(BF)

    def mix_middle(t, carry):
        mix(1 + t // 8, 1 + t % 8)
        return carry

    def mix_across(t, carry):
        mix((t // 10) * 9, t % 10)
        return carry

    def mix_along(t, carry):
        mix(1 + t // 2, (t % 2) * 9)
        return carry

    lax.fori_loop(0, 64, mix_middle, 0, unroll=4)

    inside = masks[1, 1, 0:1, :] > 0.5

    def conv(i, y):
        taps = mm(wc[...], conv_window(mx, i, y))
        for e in range(2):
            for h in range(2):
                at = (e * 2 + h) * 128
                pre = join_taps(taps[:, at : at + 128], lane) + bias[...]
                sig = 1.0 / (1.0 + jnp.exp(-pre))
                feat[i + 4 * h, y + e] = jnp.where(inside, pre * sig, 0.0).astype(BF)
                slope = sig * (1.0 + pre * (1.0 - sig))
                grad = cot_t[i + 4 * h, y + e].astype(F32) * slope
                grad = jnp.where(inside, grad, 0.0).astype(BF)
                gpf[i + 4 * h + 1, y + e + 1] = grad
                wide = grad.astype(F32)
                before = jnp.where(lane == 127, 0.0, pltpu.roll(wide, 127, 1)).astype(BF)
                after = jnp.where(lane == 0, 0.0, pltpu.roll(wide, 1, 1)).astype(BF)
                g3[i, y + e, :, h * 128 : h * 128 + 128] = rows([before, grad, after])

    def middle(step):
        def run(t, carry):
            step(1 + t // 2, 2 + (t % 2) * 2)
            return carry

        lax.fori_loop(0, 4, run, 0, unroll=4)

    def ends_along(step):
        def run(t, carry):
            step(t // 2, (t % 2) * 6)
            return carry

        lax.fori_loop(0, 8, run, 0, unroll=4)

    def ends_across(step):
        def run(t, carry):
            step((t // 2) * 3, 2 + (t % 2) * 2)
            return carry

        lax.fori_loop(0, 4, run, 0, unroll=4)

    gp_copies = halo_copies(gpf, gpf, halo_send, halo_recv, 24)
    middle(conv)
    finish(skip_copies)
    lax.fori_loop(0, 20, mix_across, 0, unroll=4)
    lax.fori_loop(0, 16, mix_along, 0, unroll=4)
    ends_along(conv)
    start(gp_copies[0:2])
    start(gp_copies[4:8])
    ends_across(conv)
    start(gp_copies[2:4])

    gacc[...] = jnp.zeros_like(gacc)

    def kernel_grad(t, carry):
        i, y = t // 2, (t % 2) * 4
        grads = lanes([g3[i, y + j] for j in range(4)])
        for k in range(3):
            cells = lanes(
                [
                    mx[i + 4 * h + k, pl.ds(y + j, 3)].reshape(192, 128)
                    for j in range(4)
                    for h in range(2)
                ]
            )
            gacc[k * 192 : k * 192 + 192, :] += mm_t(cells, grads)
        gacc[576:592, :] += mm_t(jnp.ones((16, 1024), BF), grads)
        return carry

    lax.fori_loop(0, 8, kernel_grad, 0, unroll=4)
    mine[0, 2, 0:C_ROWS] = gacc[:, 0:128].astype(BF)
    mine[1, 2, 0:C_ROWS, 0:64] = gacc[:, 128:192].astype(BF)
    mine[1, 2, 0:C_ROWS, 64:128] = jnp.zeros((C_ROWS, 64), BF)
    for half in range(2):
        mine[half, 2, C_ROWS:SUB] = jnp.zeros((SUB - C_ROWS, 128), BF)
    sums = Sums(ring, mine, got0, got1, got2, acc1, acc2, total, sum_send, sum_recv)
    sums.step0(2)

    def back(i, y):
        taps = mm(wb[...], conv_window(gpf, i, y))
        for e in range(2):
            both = []
            for h in range(2):
                at = (e * 2 + h) * 128
                grad = join_taps(taps[:, at : at + 128], lane)
                grad = jnp.where(inside, grad, 0.0).astype(BF)
                gs[i + 4 * h, y + e] = grad
                both.append(grad)
            apart = mm(lanes(both), gather_z[...]).astype(BF)
            for kz in range(4):
                d4[i, y + e, kz * 64 : kz * 64 + 64, :] = apart[:, kz * 128 : kz * 128 + 128]

    middle(back)
    finish(gp_copies)
    clear_outside(gpf)
    ends_along(back)
    ends_across(back)

    def up_grad(sx, sy):
        spots = [(pi, qi) for pi in range(1 - sx, 3 - sx) for qi in range(1 - sy, 5 - sy)]
        grads = lanes([d4[2 * pi - 1 + sx, 2 * qi - 1 + sy] for pi, qi in spots])
        cells = rows(
            [
                lanes([ac[pi + tx, qi + ty] for pi, qi in spots])
                for tx in range(2)
                for ty in range(2)
            ]
        )
        result = mm_t(grads, cells).astype(BF)
        for tx in range(2):
            for ty in range(2):
                at, col = (2 + sy - 2 * ty) * 256, (tx * 2 + ty) * 128
                mine[tx, sx, at : at + 256] = result[:, col : col + 128]

    up_grad(0, 0)
    up_grad(0, 1)
    sums.step0(0)
    up_grad(1, 0)
    up_grad(1, 1)
    sums.step0(1)

    acc[...] = jnp.zeros_like(acc)

    def lower(sy, across):
        if across == 1:
            weight = wt[sy]
            cells = rows([lanes([d4[1 + sx, 2 * q + 1 - sy] for q in range(4)]) for sx in range(2)])
        else:
            sx, i = (1, 0) if across == 0 else (0, 3)
            weight = wt[sy, :, sx * 256 : sx * 256 + 256]
            cells = lanes([d4[i, 2 * q + 1 - sy] for q in range(4)])
        result = mm(weight, cells)
        for tx in range(2):
            for ty in range(2):
                at = (tx * 2 + ty) * 128
                for q in range(4):
                    acc[across + tx, q + ty + 1 - sy] += result[
                        at : at + 128, q * 128 : q * 128 + 128
                    ]

    lower(0, 0)
    lower(1, 0)
    sums.step1()
    lower(0, 1)
    lower(1, 1)
    lower(0, 2)
    lower(1, 2)

    def turned(i, y):
        return acc[i, y].T

    def fold(y, carry):
        cells = [turned(i, y) for i in range(4)]
        left, right = [c[0:64] for c in cells], [c[64:128] for c in cells]
        folded = [
            left[0],
            left[1],
            left[2] + right[0],
            left[3] + right[1],
            right[2],
            right[3],
        ]
        for x in range(6):
            part[x, y] = folded[x].astype(BF)
        return carry

    lax.fori_loop(0, 6, fold, 0)
    part_copies = halo_copies(part, part_in, halo_send, halo_recv, 32, padding)
    start(part_copies)
    sums.step2()

    def turn_feat(x, carry):
        feat_t[:, x] = jnp.swapaxes(feat[x], 0, 1)
        return carry

    lax.fori_loop(0, 8, turn_feat, 0, unroll=2)
    stores = [
        pltpu.make_async_copy(feat_t, feat_any, local_sem.at[3]),
        pltpu.make_async_copy(gs_t, gs_any, local_sem.at[4]),
    ]
    start(stores[0:1])
    sums.step3()

    def turn_gs(x, carry):
        gs_t[:, x] = jnp.swapaxes(gs[x], 0, 1)
        return carry

    lax.fori_loop(0, 8, turn_gs, 0, unroll=2)
    start(stores[1:2])
    sums.step4()
    finish(part_copies)
    clear_outside(part_in)
    for x in range(4):
        for y in range(4):
            across = [x + 1] + [0] * (x == 0) + [5] * (x == 3)
            along = [y + 1] + [0] * (y == 0) + [5] * (y == 3)
            value = part[x + 1, y + 1].astype(F32)
            for px in across:
                for py in along:
                    if (px, py) != (x + 1, y + 1):
                        value += part_in[px, py].astype(F32)
            low[x, y] = jnp.where(keep_ref[...] > 0.5, value, 0.0).astype(BF)
    finish(stores)
    sums.step5()


def final_body(
    scale,
    feat,
    gs,
    low,
    total,
    features,
    grad_skip,
    grad_coarse,
    up_any,
    conv,
    bias,
    v0,
    v1,
    v2,
    sums,
    up,
    come_sem,
    go_sem,
):
    def part(at, count):
        return total.at[pl.ds(at, count)], sums.at[pl.ds(at, count)]

    taps = [(2 + sx - 2 * tx, tx * HALF + sx * SUB) for tx in range(2) for sx in range(2)]
    pieces = [part(2 * SUB, C_ROWS), part(HALF + 2 * SUB, C_ROWS)]
    pieces += [part(at, SUB) for kx, at in taps]
    pieces += [(feat, v0), (gs, v1), (low, v2)]
    come = [pltpu.make_async_copy(a, b, come_sem.at[n]) for n, (a, b) in enumerate(pieces)]
    start(come)
    go = [(v0, features), (v1, grad_skip), (v2, grad_coarse)]
    go += [(up.at[kx], up_any.at[kx]) for kx, at in taps]
    go = [pltpu.make_async_copy(a, b, go_sem.at[n]) for n, (a, b) in enumerate(go)]
    finish(come[0:2])
    for tap in range(9):
        at = 2 * SUB + tap * 64
        left = sums[at : at + 64].astype(F32) * scale
        right = sums[HALF + at : HALF + at + 64].astype(F32) * scale
        conv[tap // 3, tap % 3, 0] = left[:, 0:64]
        conv[tap // 3, tap % 3, 1] = left[:, 64:128]
        conv[tap // 3, tap % 3, 2] = right[:, 0:64]
    bias[...] = (sums[2 * SUB + 576 : 2 * SUB + 592].astype(F32) * scale)[0:1, 64:128]
    for n, (kx, at) in enumerate(taps):
        come[2 + n].wait()

        def column(t, carry):
            block = sums[pl.ds(pl.multiple_of(at + t * 256, 256), 256)]
            up[kx, t] = (block.astype(F32) * scale).reshape(4, 64, 128)
            return carry

        lax.fori_loop(0, 4, column, 0)
        go[3 + n].start()
    for n in range(3):
        come[6 + n].wait()
        go[n].start()
    finish(go)


def spread_matrix():
    row, column = np.arange(512)[:, None], np.arange(256)[None, :]
    kz, h, j = row // 128, (row // 64) % 2, row % 64
    hit = (h == column // 128) & (column % 128 == 2 * j - 1 + kz)
    return hit.astype(ml_dtypes.bfloat16)


def body(coarse, skip, occupancy, cotangent, up_weight, conv_weight, conv_bias):
    spread_up = spread_matrix()
    wide_rows = np.repeat(np.eye(16), EDGE, axis=1).astype(ml_dtypes.bfloat16)
    wide_columns = np.repeat(np.eye(16), EDGE // 2, axis=0).astype(ml_dtypes.bfloat16)
    vmem, anywhere = pl.BlockSpec(memory_space=pltpu.VMEM), pl.BlockSpec(memory_space=pl.ANY)
    plane = (64, 8, 8, 128)
    feat, gs, low, total = pl.pallas_call(
        main_body,
        out_shape=[shape(plane), shape(plane), shape((4, 4, 64, 128)), shape((2 * HALF, 128))],
        in_specs=[anywhere] * 7 + [vmem] * 4,
        out_specs=[anywhere] * 2 + [vmem] * 2,
        scratch_shapes=[
            pltpu.VMEM(plane, BF),
            pltpu.VMEM(plane, BF),
            pltpu.VMEM((4, 4, 4, 64, 128), BF),
            pltpu.VMEM((4, 4, 64, 128), BF),
            pltpu.VMEM((3, 3, 3, 64, 64), BF),
            pltpu.VMEM((512, 256), BF),
            pltpu.VMEM((256, 512), BF),
            pltpu.VMEM((8, 8, 64, 128), BF),
            pltpu.VMEM((8, 8, 64, 128), BF),
            pltpu.VMEM(plane, BF),
            pltpu.VMEM(plane, BF),
            pltpu.SemaphoreType.DMA((9,)),
            pltpu.VMEM((10, 10, 64, 128), BF),
            pltpu.VMEM((6, 6, 64, 128), BF),
            pltpu.VMEM((3, 3, 16, 128), BF),
            pltpu.VMEM((3, 3, 16, 128), F32),
            pltpu.VMEM((64, 128), F32),
            pltpu.VMEM((64, 128), F32),
            pltpu.VMEM((8, 8, 64, 128), BF),
            pltpu.VMEM((192, 576), BF),
            pltpu.VMEM((192, 576), BF),
            pltpu.VMEM((1024, 512), BF),
            pltpu.VMEM((2, 512, 512), BF),
            pltpu.VMEM((4, 6, 128, 128), BF),
            pltpu.VMEM((10, 10, 64, 128), F32),
            pltpu.VMEM((10, 10, 64, 128), BF),
            pltpu.VMEM((10, 10, 64, 128), BF),
            pltpu.VMEM((4, 8, 192, 256), BF),
            pltpu.VMEM((C_ROWS, 192), F32),
            pltpu.VMEM((4, 8, 256, 128), BF),
            pltpu.VMEM((4, 6, 128, 128), F32),
            pltpu.VMEM((6, 6, 64, 128), BF),
            pltpu.VMEM((6, 6, 64, 128), BF),
            pltpu.VMEM((2, 3, SUB, 128), BF),
            pltpu.VMEM((HALF, 128), BF),
            pltpu.VMEM((3, QUARTER, 128), BF),
            pltpu.VMEM((15, CHUNK, 128), BF),
            pltpu.VMEM((QUARTER, 128), BF),
            pltpu.VMEM((QUARTER, 128), BF),
            pltpu.SemaphoreType.DMA((40,)),
            pltpu.SemaphoreType.DMA((40,)),
            pltpu.SemaphoreType.DMA((43,)),
            pltpu.SemaphoreType.DMA((43,)),
        ],
        compiler_params=pltpu.CompilerParams(
            vmem_limit_bytes=LIMIT, collective_id=1, has_side_effects=True
        ),
    )(
        skip,
        cotangent,
        jnp.transpose(up_weight, (0, 1, 2, 4, 3)),
        jnp.transpose(coarse, (1, 2, 3, 0)),
        conv_weight,
        spread_up,
        np.ascontiguousarray(spread_up.T),
        conv_bias[None],
        occupancy[0],
        wide_rows,
        wide_columns,
    )
    cells = 8192 * lax.axis_size("gx") * lax.axis_size("gy")
    features, grad_skip, low, up, grad_conv, bias = pl.pallas_call(
        functools.partial(final_body, float(cells) ** -0.5),
        out_shape=[
            shape(plane),
            shape(plane),
            shape((4, 4, 64, 128)),
            shape((4, 4, 4, 64, 128), F32),
            shape((3, 3, 3, 64, 64), F32),
            shape((1, 64), F32),
        ],
        in_specs=[anywhere] * 4,
        out_specs=[anywhere] * 4 + [vmem] * 2,
        scratch_shapes=[
            pltpu.VMEM(plane, BF),
            pltpu.VMEM(plane, BF),
            pltpu.VMEM((4, 4, 64, 128), BF),
            pltpu.VMEM((2 * HALF, 128), BF),
            pltpu.VMEM((4, 4, 4, 64, 128), F32),
            pltpu.SemaphoreType.DMA((9,)),
            pltpu.SemaphoreType.DMA((7,)),
        ],
        compiler_params=pltpu.CompilerParams(vmem_limit_bytes=LIMIT),
    )(feat, gs, low, total)
    grad_coarse = jnp.transpose(low, (3, 0, 1, 2))
    grad_up = jnp.transpose(up, (0, 1, 2, 4, 3))
    return features, grad_skip, grad_coarse, grad_up, grad_conv, bias[0]


def solution(mesh):
    field = P(None, "gx", "gy", None)
    return jax.shard_map(
        body,
        mesh=mesh,
        in_specs=(field, field, P("gx", "gy", None), field, P(), P(), P()),
        out_specs=(field, field, field, P(), P(), P()),
        check_vma=False,
    )
```

```python
import functools

import jax
import jax.numpy as jnp
import ml_dtypes
import numpy as np
from jax import lax
from jax.experimental import pallas as pl
from jax.experimental.pallas import tpu as pltpu
from jax.sharding import PartitionSpec as P

BF = jnp.bfloat16
F32 = jnp.float32
EDGE = 8
MESH = pl.DeviceIdType.MESH
LIMIT = 56 * 2**20

C_ROWS = 592
PIECE = 2048
HALF, QUARTER, CHUNK = PIECE // 2, PIECE // 8, PIECE // 128


def mm(a, b):
    return lax.dot_general(a, b, (((1,), (0,)), ((), ())), preferred_element_type=F32)


def mm_t(a, b):
    return lax.dot_general(a, b, (((1,), (1,)), ((), ())), preferred_element_type=F32)


def lanes(parts):
    return jnp.concatenate(parts, axis=1)


def rows(parts):
    return jnp.concatenate(parts, axis=0)


def shape(dims, kind=BF):
    return jax.ShapeDtypeStruct(dims, kind)


AROUND = [(0, 1), (0, -1), (1, 0), (-1, 0), (1, 1), (1, -1), (-1, 1), (-1, -1)]


def neighbour(dx, dy):
    nx, ny = lax.axis_size("gx"), lax.axis_size("gy")
    gx, gy = lax.axis_index("gx"), lax.axis_index("gy")
    return lax.rem(gx + (dx + nx), nx), lax.rem(gy + (dy + ny), ny)


def outer(step, count):
    if step == 0:
        return pl.ds(1, count), pl.ds(1, count)
    if step > 0:
        return pl.ds(count, 1), pl.ds(0, 1)
    return pl.ds(1, 1), pl.ds(count + 1, 1)


def padding(step, count):
    if step == 0:
        return pl.ds(1, count), pl.ds(1, count)
    if step > 0:
        return pl.ds(count + 1, 1), pl.ds(0, 1)
    return pl.ds(0, 1), pl.ds(count + 1, 1)


def halo_copies(source, target, send, recv, first, place=outer):
    across, along = source.shape[0] - 2, source.shape[1] - 2
    copies = []
    for at, (dx, dy) in enumerate(AROUND):
        sx, tx = place(dx, across)
        sy, ty = place(dy, along)
        copies.append(
            pltpu.make_async_remote_copy(
                src_ref=source.at[sx, sy],
                dst_ref=target.at[tx, ty],
                send_sem=send.at[first + at],
                recv_sem=recv.at[first + at],
                device_id=neighbour(dx, dy),
                device_id_type=MESH,
            )
        )
    return copies


def start(copies):
    for copy in copies:
        copy.start()


def finish(copies):
    for copy in copies:
        copy.wait()


def clear_outside(field):
    across, along = field.shape[0], field.shape[1]
    nx, ny = lax.axis_size("gx"), lax.axis_size("gy")
    gx, gy = lax.axis_index("gx"), lax.axis_index("gy")
    row = jnp.zeros((1,) + field.shape[1:], field.dtype)
    column = jnp.zeros((across, 1) + field.shape[2:], field.dtype)

    @pl.when(gx == 0)
    def _():
        field[0:1] = row

    @pl.when(gx == nx - 1)
    def _():
        field[across - 1 : across] = row

    @pl.when(gy == 0)
    def _():
        field[:, 0:1] = column

    @pl.when(gy == ny - 1)
    def _():
        field[:, along - 1 : along] = column


class Ring:
    def __init__(self):
        gx, gy = lax.axis_index("gx"), lax.axis_index("gy")
        self.core = lax.rem(gx, 2)
        self.x, self.y = gx // 4, gy // 2
        self.z = lax.rem(gy, 2) * 2 + lax.rem(gx // 2, 2)
        self.first = jnp.where(self.core == 0, self.x, self.y)
        self.second = jnp.where(self.core == 0, self.y, self.x)
        self.place = self.second * 4 + self.z
        self.twin = self.device(self.x, self.y, self.z, 1 - self.core)

    def device(self, x, y, z, core):
        return x * 4 + lax.rem(z, 2) * 2 + core, y * 2 + z // 2

    def along_first(self, step):
        other = lax.rem(self.first + step, 4)
        x = jnp.where(self.core == 0, other, self.x)
        y = jnp.where(self.core == 0, self.y, other)
        return other, self.device(x, y, self.z, self.core)

    def in_plane(self, step):
        a, b = lax.rem(self.second + step // 4, 4), lax.rem(self.z + step % 4, 4)
        x = jnp.where(self.core == 0, self.x, a)
        y = jnp.where(self.core == 0, a, self.y)
        return a * 4 + b, self.device(x, y, b, self.core)

    def greet(self, barrier):
        partners = [self.twin]
        partners += [self.along_first(step)[1] for step in range(1, 4)]
        partners += [self.in_plane(step)[1] for step in range(1, 16)]
        for partner in partners:
            pl.semaphore_signal(barrier, inc=1, device_id=partner, device_id_type=MESH)
        return len(partners)


def span(begin, count):
    return pl.ds(pl.multiple_of(begin, 16), count)


class Piece:
    def __init__(self, ring, index, mine, got0, got1, got2, acc1, acc2, out, send, recv):
        self.ring, self.base = ring, index * 38
        self.mine, self.got0, self.got1 = mine.at[index], got0.at[index], got1.at[index]
        self.got2, self.acc1, self.acc2 = got2.at[index], acc1.at[index], acc2.at[index]
        self.out, self.send, self.recv = out.at[index], send, recv
        self.flying = []

    def remote(self, src, dst, at, to):
        return pltpu.make_async_remote_copy(
            src_ref=src,
            dst_ref=dst,
            send_sem=self.send.at[self.base + at],
            recv_sem=self.recv.at[self.base + at],
            device_id=to,
            device_id_type=MESH,
        )

    def launch(self, copies):
        start(copies)
        self.flying = copies

    def step0(self):
        ring = self.ring
        theirs = self.mine.at[span((1 - ring.core) * HALF, HALF)]
        self.launch([self.remote(theirs, self.got0, 0, ring.twin)])

    def step1(self):
        ring = self.ring
        finish(self.flying)

        def add(t, carry):
            own = self.mine[span(ring.core * HALF + t * 256, 256)].astype(F32)
            at = span(t * 256, 256)
            self.got0[at] = (own + self.got0[at].astype(F32)).astype(BF)
            return carry

        lax.fori_loop(0, HALF // 256, add, 0)
        copies = []
        for step in range(1, 4):
            other, to = ring.along_first(step)
            theirs = self.got0.at[span(other * QUARTER, QUARTER)]
            copies.append(self.remote(theirs, self.got1.at[step - 1], step, to))
        self.launch(copies)

    def step2(self):
        ring = self.ring
        finish(self.flying)
        total = self.got0[span(ring.first * QUARTER, QUARTER)].astype(F32)
        for step in range(3):
            total += self.got1[step].astype(F32)
        self.acc1[...] = total.astype(BF)
        copies = []
        for step in range(1, 16):
            other, to = ring.in_plane(step)
            theirs = self.acc1.at[span(other * CHUNK, CHUNK)]
            copies.append(self.remote(theirs, self.got2.at[step - 1], 3 + step, to))
        self.launch(copies)

    def step3(self):
        ring = self.ring
        finish(self.flying)
        total = self.acc1[span(ring.place * CHUNK, CHUNK)].astype(F32)
        for step in range(15):
            total += self.got2[step].astype(F32)
        own = span(ring.place * CHUNK, CHUNK)
        self.acc2[own] = total.astype(BF)
        copies = []
        for step in range(1, 16):
            other, to = ring.in_plane(step)
            copies.append(self.remote(self.acc2.at[own], self.acc2.at[own], 18 + step, to))
        self.launch(copies)

    def step4(self):
        ring = self.ring
        finish(self.flying)
        own = span(ring.core * HALF + ring.first * QUARTER, QUARTER)
        copies = []
        for step in range(1, 4):
            other, to = ring.along_first(step)
            copies.append(self.remote(self.acc2, self.out.at[own], 33 + step, to))
        self.launch(copies)
        self.out[own] = self.acc2[...]

    def step5(self):
        ring = self.ring
        finish(self.flying)
        own = self.out.at[span(ring.core * HALF, HALF)]
        self.launch([self.remote(own, own, 37, ring.twin)])

    def step6(self):
        finish(self.flying)


def lane_of(dims):
    return lax.broadcasted_iota(jnp.int32, dims, len(dims) - 1)


def conv_window(field, i, pair):
    return rows(
        [
            lanes(
                [
                    field[i + 4 * h + k, pl.ds(y, 3)].reshape(192, 128)
                    for y in pair
                    for h in range(2)
                ]
            )
            for k in range(3)
        ]
    )


def join_taps(taps, lane):
    back = jnp.where(lane == 0, 0.0, pltpu.roll(taps[0:64], 1, 1))
    ahead = jnp.where(lane == 127, 0.0, pltpu.roll(taps[128:192], 127, 1))
    return taps[64:128] + back + ahead


def main_body(
    skip_any,
    cot_any,
    upw_any,
    coarse_any,
    convw_any,
    spread_any,
    gather_any,
    conv_bias,
    occupancy,
    wide_rows,
    wide_columns,
    feat_any,
    gs_any,
    low,
    total,
    skip,
    cot,
    upw,
    coarse,
    convw,
    spread_up,
    gather_z,
    feat,
    gs,
    feat_t,
    gs_t,
    local_sem,
    sf,
    cf,
    mf,
    masks,
    keep_ref,
    bias,
    cot_t,
    wc,
    wb,
    wu,
    wt,
    ac,
    ups,
    mx,
    gpf,
    g3,
    gacc,
    d4,
    acc,
    part,
    part_in,
    mine,
    got0,
    got1,
    got2,
    acc1,
    acc2,
    halo_send,
    halo_recv,
    sum_send,
    sum_recv,
):
    ring = Ring()
    barrier = pltpu.get_barrier_semaphore()
    for dx, dy in AROUND:
        pl.semaphore_signal(barrier, inc=1, device_id=neighbour(dx, dy), device_id_type=MESH)
    greeted = ring.greet(barrier) + len(AROUND)
    loads = [
        pltpu.make_async_copy(coarse_any, coarse, local_sem.at[5]),
        pltpu.make_async_copy(skip_any, skip, local_sem.at[0]),
        pltpu.make_async_copy(cot_any, cot, local_sem.at[1]),
        pltpu.make_async_copy(convw_any, convw, local_sem.at[6]),
        pltpu.make_async_copy(upw_any, upw, local_sem.at[2]),
        pltpu.make_async_copy(spread_any, spread_up, local_sem.at[7]),
        pltpu.make_async_copy(gather_any, gather_z, local_sem.at[8]),
    ]
    start(loads)
    lane = lane_of((64, 128))

    there = jnp.where(occupancy[0] > 0, 1.0, 0.0)
    mf[1, 1] = mm(jnp.broadcast_to(there, (16, 16)).astype(BF), wide_rows[...]).astype(BF)
    keep_ref[...] = mm_t(wide_columns[...], jnp.broadcast_to(there, (128, 16)).astype(BF))

    loads[0].wait()

    def fill_coarse(t, carry):
        x, y = t // 4, t % 4
        own = jnp.where(keep_ref[...] > 0.5, coarse[x, y].astype(F32), 0.0)
        cf[x + 1, y + 1] = own.astype(BF)
        return carry

    lax.fori_loop(0, 16, fill_coarse, 0, unroll=4)
    pl.semaphore_wait(barrier, greeted)
    coarse_copies = halo_copies(cf, cf, halo_send, halo_recv, 0)
    mask_copies = halo_copies(mf, mf, halo_send, halo_recv, 8)
    start(coarse_copies)
    start(mask_copies)

    loads[1].wait()

    def fill_skip(x, carry):
        sf[x + 1, pl.ds(1, 8)] = jnp.swapaxes(skip[:, x], 0, 1)
        return carry

    lax.fori_loop(0, 8, fill_skip, 0, unroll=2)
    skip_copies = halo_copies(sf, sf, halo_send, halo_recv, 16)

    loads[2].wait()

    def fill_cot(x, carry):
        cot_t[x] = jnp.swapaxes(cot[:, x], 0, 1)
        return carry

    lax.fori_loop(0, 8, fill_cot, 0, unroll=2)
    start(skip_copies)
    finish(loads[3:7])
    bias[...] = jnp.broadcast_to(conv_bias[...], (128, 64)).T
    for kz in range(3):
        for pair in range(5):
            taps = [(k // 3, k % 3) for k in (2 * pair, 2 * pair + 1) if k < 9]
            fore = [convw[kx, ky, kz] for kx, ky in taps]
            aft = [convw[2 - kx, 2 - ky, 2 - kz] for kx, ky in taps]
            at, col = kz * 64, pair * 128
            wide = 64 * len(taps)
            wc[at : at + 64, col : col + wide] = rows(fore).T
            wb[at : at + 64, col : col + wide] = lanes(aft)
    for sx in range(2):
        for sy in range(2):
            for tx in range(2):
                for ty in range(2):
                    block = upw[2 + sx - 2 * tx, 2 + sy - 2 * ty].reshape(256, 128)
                    at, col = (sx * 2 + sy) * 256, (tx * 2 + ty) * 128
                    wu[at : at + 256, col : col + 128] = block
                    wt[sy, col : col + 128, sx * 256 : sx * 256 + 256] = block.T

    def pair_coarse(i, y):
        ac[i, y] = rows([cf[i, y], cf[i + 2, y]]).T

    def pair_middle(t, carry):
        pair_coarse(1 + t // 4, 1 + t % 4)
        return carry

    def pair_across(t, carry):
        pair_coarse((t // 6) * 3, t % 6)
        return carry

    def pair_along(t, carry):
        pair_coarse(1 + t // 2, (t % 2) * 5)
        return carry

    def join(p, q, taps):
        wide = rows(
            [
                lanes([taps[(s * 4 + kz) * 64 : (s * 4 + kz + 1) * 64] for kz in range(4)])
                for s in range(4)
            ]
        )
        up = mm(wide, spread_up[...])
        for s in range(4):
            for h in range(2):
                ups[2 * p + s // 2 + 4 * h, 2 * q + s % 2] = up[
                    s * 64 : s * 64 + 64, h * 128 : h * 128 + 128
                ]

    def upsample(blocks):
        window = lanes([ac[p : p + 2, q : q + 2].reshape(512, 128) for p, q in blocks])
        taps = mm(wu[...], window).astype(BF)
        for at, (p, q) in enumerate(blocks):
            join(p, q, taps[:, at * 128 : at * 128 + 128])

    lax.fori_loop(0, 8, pair_middle, 0, unroll=4)
    upsample([(1, 1), (1, 2), (1, 3)])
    finish(coarse_copies)
    clear_outside(cf)
    lax.fori_loop(0, 12, pair_across, 0, unroll=4)
    lax.fori_loop(0, 4, pair_along, 0, unroll=4)
    for p in (0, 2):
        upsample([(p, 0), (p, 1)])
        upsample([(p, 2), (p, 3)])
        upsample([(p, 4), (1, p * 2)])

    finish(mask_copies)
    clear_outside(mf)
    for bx in range(3):
        for by in range(3):
            masks[bx, by] = mf[bx, by].astype(F32)

    def mix(x, y):
        bx = jnp.where(x == 0, 0, jnp.where(x == 9, 2, 1))
        by = jnp.where(y == 0, 0, jnp.where(y == 9, 2, 1))
        value = ups[x, y] + sf[x, y].astype(F32)
        mx[x, y] = jnp.where(masks[bx, by, 0:1, :] > 0.5, value, 0.0).astype(BF)

    def mix_middle(t, carry):
        mix(1 + t // 8, 1 + t % 8)
        return carry

    def mix_across(t, carry):
        mix((t // 10) * 9, t % 10)
        return carry

    def mix_along(t, carry):
        mix(1 + t // 2, (t % 2) * 9)
        return carry

    lax.fori_loop(0, 64, mix_middle, 0, unroll=4)

    inside = masks[1, 1, 0:1, :] > 0.5

    def conv(i, pair):
        taps = mm(wc[...], conv_window(mx, i, pair))
        for e, y in enumerate(pair):
            for h in range(2):
                at = (e * 2 + h) * 128
                pre = join_taps(taps[:, at : at + 128], lane) + bias[...]
                sig = 1.0 / (1.0 + jnp.exp(-pre))
                feat[i + 4 * h, y] = jnp.where(inside, pre * sig, 0.0).astype(BF)
                slope = sig * (1.0 + pre * (1.0 - sig))
                grad = cot_t[i + 4 * h, y].astype(F32) * slope
                grad = jnp.where(inside, grad, 0.0).astype(BF)
                gpf[i + 4 * h + 1, y + 1] = grad
                wide = grad.astype(F32)
                before = jnp.where(lane == 127, 0.0, pltpu.roll(wide, 127, 1)).astype(BF)
                after = jnp.where(lane == 0, 0.0, pltpu.roll(wide, 1, 1)).astype(BF)
                g3[i, y, :, h * 128 : h * 128 + 128] = rows([before, grad, after])

    def middle(step):
        def run(t, carry):
            y = 1 + (t % 3) * 2
            step(1 + t // 3, (y, y + 1))
            return carry

        lax.fori_loop(0, 6, run, 0, unroll=3)

    def ends_along(step, first, last):
        def run(i, carry):
            step(i, (0, 7))
            return carry

        lax.fori_loop(first, last, run, 0, unroll=last - first)

    def ends_across(step, i):
        def run(t, carry):
            y = 1 + t * 2
            step(i, (y, y + 1))
            return carry

        lax.fori_loop(0, 3, run, 0, unroll=3)

    gp_copies = halo_copies(gpf, gpf, halo_send, halo_recv, 24)
    middle(conv)
    finish(skip_copies)
    lax.fori_loop(0, 20, mix_across, 0, unroll=4)
    lax.fori_loop(0, 16, mix_along, 0, unroll=4)
    ends_along(conv, 0, 4)
    start(gp_copies[0:2])
    start(gp_copies[4:8])
    ends_across(conv, 0)
    ends_across(conv, 3)
    start(gp_copies[2:4])

    gacc[...] = jnp.zeros_like(gacc)

    def kernel_grad(t, carry):
        i, y = t // 2, (t % 2) * 4
        grads = lanes([g3[i, y + j] for j in range(4)])
        for k in range(3):
            cells = lanes(
                [
                    mx[i + 4 * h + k, pl.ds(y + j, 3)].reshape(192, 128)
                    for j in range(4)
                    for h in range(2)
                ]
            )
            gacc[k * 192 : k * 192 + 192, :] += mm_t(cells, grads)
        gacc[576:592, :] += mm_t(jnp.ones((16, 1024), BF), grads)
        return carry

    lax.fori_loop(0, 8, kernel_grad, 0, unroll=4)
    mine[2, 0:C_ROWS] = gacc[:, 0:128].astype(BF)
    mine[2, C_ROWS : 2 * C_ROWS, 0:64] = gacc[:, 128:192].astype(BF)
    mine[2, C_ROWS : 2 * C_ROWS, 64:128] = jnp.zeros((C_ROWS, 64), BF)
    mine[2, 2 * C_ROWS : PIECE] = jnp.zeros((PIECE - 2 * C_ROWS, 128), BF)
    sums = [
        Piece(ring, at, mine, got0, got1, got2, acc1, acc2, total, sum_send, sum_recv)
        for at in range(3)
    ]
    even, odd, conv_sum = sums
    conv_sum.step0()

    def back(i, pair):
        taps = mm(wb[...], conv_window(gpf, i, pair))
        for e, y in enumerate(pair):
            both = []
            for h in range(2):
                at = (e * 2 + h) * 128
                grad = join_taps(taps[:, at : at + 128], lane)
                grad = jnp.where(inside, grad, 0.0).astype(BF)
                gs[i + 4 * h, y] = grad
                both.append(grad)
            apart = mm(lanes(both), gather_z[...]).astype(BF)
            for kz in range(4):
                d4[i, y, kz * 64 : kz * 64 + 64, :] = apart[:, kz * 128 : kz * 128 + 128]

    def up_grad(sx, sy):
        spots = [(pi, qi) for pi in range(1 - sx, 3 - sx) for qi in range(1 - sy, 5 - sy)]
        grads = lanes([d4[2 * pi - 1 + sx, 2 * qi - 1 + sy] for pi, qi in spots])
        cells = rows(
            [
                lanes([ac[pi + tx, qi + ty] for pi, qi in spots])
                for tx in range(2)
                for ty in range(2)
            ]
        )
        result = mm_t(grads, cells).astype(BF)
        for tx in range(2):
            for ty in range(2):
                at, col = (tx * 4 + 2 + sy - 2 * ty) * 256, (tx * 2 + ty) * 128
                mine[sx, at : at + 256] = result[:, col : col + 128]

    middle(back)
    finish(gp_copies)
    clear_outside(gpf)
    ends_along(back, 1, 2)
    ends_along(back, 3, 4)
    ends_across(back, 3)
    conv_sum.step1()
    up_grad(0, 0)
    up_grad(0, 1)
    even.step0()
    ends_along(back, 2, 3)
    ends_along(back, 0, 1)
    ends_across(back, 0)
    even.step1()
    up_grad(1, 0)
    up_grad(1, 1)
    odd.step0()
    conv_sum.step2()

    acc[...] = jnp.zeros_like(acc)

    def lower(sy, across):
        if across == 1:
            weight = wt[sy]
            cells = rows([lanes([d4[1 + sx, 2 * q + 1 - sy] for q in range(4)]) for sx in range(2)])
        else:
            sx, i = (1, 0) if across == 0 else (0, 3)
            weight = wt[sy, :, sx * 256 : sx * 256 + 256]
            cells = lanes([d4[i, 2 * q + 1 - sy] for q in range(4)])
        result = mm(weight, cells)
        for tx in range(2):
            for ty in range(2):
                at = (tx * 2 + ty) * 128
                for q in range(4):
                    acc[across + tx, q + ty + 1 - sy] += result[
                        at : at + 128, q * 128 : q * 128 + 128
                    ]

    lower(0, 0)
    lower(1, 0)
    lower(0, 1)
    odd.step1()
    lower(1, 1)
    lower(0, 2)
    lower(1, 2)
    even.step2()

    def turned(i, y):
        return acc[i, y].T

    def fold(y, carry):
        cells = [turned(i, y) for i in range(4)]
        left, right = [c[0:64] for c in cells], [c[64:128] for c in cells]
        folded = [
            left[0],
            left[1],
            left[2] + right[0],
            left[3] + right[1],
            right[2],
            right[3],
        ]
        for x in range(6):
            part[x, y] = folded[x].astype(BF)
        return carry

    lax.fori_loop(0, 6, fold, 0)
    part_copies = halo_copies(part, part_in, halo_send, halo_recv, 32, padding)
    start(part_copies)
    conv_sum.step3()
    odd.step2()

    def turn_feat(x, carry):
        feat_t[:, x] = jnp.swapaxes(feat[x], 0, 1)
        return carry

    lax.fori_loop(0, 8, turn_feat, 0, unroll=2)
    stores = [
        pltpu.make_async_copy(feat_t, feat_any, local_sem.at[3]),
        pltpu.make_async_copy(gs_t, gs_any, local_sem.at[4]),
    ]
    start(stores[0:1])
    even.step3()
    odd.step3()

    def turn_gs(x, carry):
        gs_t[:, x] = jnp.swapaxes(gs[x], 0, 1)
        return carry

    lax.fori_loop(0, 8, turn_gs, 0, unroll=2)
    start(stores[1:2])
    conv_sum.step4()
    even.step4()
    odd.step4()
    finish(part_copies)
    clear_outside(part_in)
    for x in range(4):
        for y in range(4):
            across = [x + 1] + [0] * (x == 0) + [5] * (x == 3)
            along = [y + 1] + [0] * (y == 0) + [5] * (y == 3)
            value = part[x + 1, y + 1].astype(F32)
            for px in across:
                for py in along:
                    if (px, py) != (x + 1, y + 1):
                        value += part_in[px, py].astype(F32)
            low[x, y] = jnp.where(keep_ref[...] > 0.5, value, 0.0).astype(BF)
    conv_sum.step5()
    even.step5()
    odd.step5()
    finish(stores)
    conv_sum.step6()
    even.step6()
    odd.step6()


def final_body(
    scale,
    feat,
    gs,
    low,
    total,
    features,
    grad_skip,
    grad_coarse,
    up_any,
    conv,
    bias,
    v0,
    v1,
    v2,
    sums,
    up,
    come_sem,
    go_sem,
):
    def part(at, count):
        return total.at[pl.ds(at, count)], sums.at[pl.ds(at, count)]

    taps = [(2 + sx - 2 * tx, sx * PIECE + tx * HALF) for tx in range(2) for sx in range(2)]
    pieces = [part(2 * PIECE, C_ROWS), part(2 * PIECE + C_ROWS, C_ROWS)]
    pieces += [part(at, HALF) for kx, at in taps]
    pieces += [(feat, v0), (gs, v1), (low, v2)]
    come = [pltpu.make_async_copy(a, b, come_sem.at[n]) for n, (a, b) in enumerate(pieces)]
    start(come)
    go = [(v0, features), (v1, grad_skip), (v2, grad_coarse)]
    go += [(up.at[kx], up_any.at[kx]) for kx, at in taps]
    go = [pltpu.make_async_copy(a, b, go_sem.at[n]) for n, (a, b) in enumerate(go)]
    finish(come[0:2])
    for tap in range(9):
        at = 2 * PIECE + tap * 64
        left = sums[at : at + 64].astype(F32) * scale
        right = sums[C_ROWS + at : C_ROWS + at + 64].astype(F32) * scale
        conv[tap // 3, tap % 3, 0] = left[:, 0:64]
        conv[tap // 3, tap % 3, 1] = left[:, 64:128]
        conv[tap // 3, tap % 3, 2] = right[:, 0:64]
    bias[...] = (sums[2 * PIECE + 576 : 2 * PIECE + 592].astype(F32) * scale)[0:1, 64:128]
    for n, (kx, at) in enumerate(taps):
        come[2 + n].wait()

        def column(t, carry):
            block = sums[pl.ds(pl.multiple_of(at + t * 256, 256), 256)]
            up[kx, t] = (block.astype(F32) * scale).reshape(4, 64, 128)
            return carry

        lax.fori_loop(0, 4, column, 0)
        go[3 + n].start()
    for n in range(3):
        come[6 + n].wait()
        go[n].start()
    finish(go)


def spread_matrix():
    row, column = np.arange(512)[:, None], np.arange(256)[None, :]
    kz, h, j = row // 128, (row // 64) % 2, row % 64
    hit = (h == column // 128) & (column % 128 == 2 * j - 1 + kz)
    return hit.astype(ml_dtypes.bfloat16)


def body(coarse, skip, occupancy, cotangent, up_weight, conv_weight, conv_bias):
    spread_up = spread_matrix()
    wide_rows = np.repeat(np.eye(16), EDGE, axis=1).astype(ml_dtypes.bfloat16)
    wide_columns = np.repeat(np.eye(16), EDGE // 2, axis=0).astype(ml_dtypes.bfloat16)
    vmem, anywhere = pl.BlockSpec(memory_space=pltpu.VMEM), pl.BlockSpec(memory_space=pl.ANY)
    plane = (64, 8, 8, 128)
    feat, gs, low, total = pl.pallas_call(
        main_body,
        out_shape=[shape(plane), shape(plane), shape((4, 4, 64, 128)), shape((3, PIECE, 128))],
        in_specs=[anywhere] * 7 + [vmem] * 4,
        out_specs=[anywhere] * 2 + [vmem] * 2,
        scratch_shapes=[
            pltpu.VMEM(plane, BF),
            pltpu.VMEM(plane, BF),
            pltpu.VMEM((4, 4, 4, 64, 128), BF),
            pltpu.VMEM((4, 4, 64, 128), BF),
            pltpu.VMEM((3, 3, 3, 64, 64), BF),
            pltpu.VMEM((512, 256), BF),
            pltpu.VMEM((256, 512), BF),
            pltpu.VMEM((8, 8, 64, 128), BF),
            pltpu.VMEM((8, 8, 64, 128), BF),
            pltpu.VMEM(plane, BF),
            pltpu.VMEM(plane, BF),
            pltpu.SemaphoreType.DMA((9,)),
            pltpu.VMEM((10, 10, 64, 128), BF),
            pltpu.VMEM((6, 6, 64, 128), BF),
            pltpu.VMEM((3, 3, 16, 128), BF),
            pltpu.VMEM((3, 3, 16, 128), F32),
            pltpu.VMEM((64, 128), F32),
            pltpu.VMEM((64, 128), F32),
            pltpu.VMEM((8, 8, 64, 128), BF),
            pltpu.VMEM((192, 576), BF),
            pltpu.VMEM((192, 576), BF),
            pltpu.VMEM((1024, 512), BF),
            pltpu.VMEM((2, 512, 512), BF),
            pltpu.VMEM((4, 6, 128, 128), BF),
            pltpu.VMEM((10, 10, 64, 128), F32),
            pltpu.VMEM((10, 10, 64, 128), BF),
            pltpu.VMEM((10, 10, 64, 128), BF),
            pltpu.VMEM((4, 8, 192, 256), BF),
            pltpu.VMEM((C_ROWS, 192), F32),
            pltpu.VMEM((4, 8, 256, 128), BF),
            pltpu.VMEM((4, 6, 128, 128), F32),
            pltpu.VMEM((6, 6, 64, 128), BF),
            pltpu.VMEM((6, 6, 64, 128), BF),
            pltpu.VMEM((3, PIECE, 128), BF),
            pltpu.VMEM((3, HALF, 128), BF),
            pltpu.VMEM((3, 3, QUARTER, 128), BF),
            pltpu.VMEM((3, 15, CHUNK, 128), BF),
            pltpu.VMEM((3, QUARTER, 128), BF),
            pltpu.VMEM((3, QUARTER, 128), BF),
            pltpu.SemaphoreType.DMA((40,)),
            pltpu.SemaphoreType.DMA((40,)),
            pltpu.SemaphoreType.DMA((3 * 38,)),
            pltpu.SemaphoreType.DMA((3 * 38,)),
        ],
        compiler_params=pltpu.CompilerParams(
            vmem_limit_bytes=LIMIT, collective_id=1, has_side_effects=True
        ),
    )(
        skip,
        cotangent,
        jnp.transpose(up_weight, (0, 1, 2, 4, 3)),
        jnp.transpose(coarse, (1, 2, 3, 0)),
        conv_weight,
        spread_up,
        np.ascontiguousarray(spread_up.T),
        conv_bias[None],
        occupancy[0],
        wide_rows,
        wide_columns,
    )
    cells = 8192 * lax.axis_size("gx") * lax.axis_size("gy")
    features, grad_skip, low, up, grad_conv, bias = pl.pallas_call(
        functools.partial(final_body, float(cells) ** -0.5),
        out_shape=[
            shape(plane),
            shape(plane),
            shape((4, 4, 64, 128)),
            shape((4, 4, 4, 64, 128), F32),
            shape((3, 3, 3, 64, 64), F32),
            shape((1, 64), F32),
        ],
        in_specs=[anywhere] * 4,
        out_specs=[anywhere] * 4 + [vmem] * 2,
        scratch_shapes=[
            pltpu.VMEM(plane, BF),
            pltpu.VMEM(plane, BF),
            pltpu.VMEM((4, 4, 64, 128), BF),
            pltpu.VMEM((3 * PIECE, 128), BF),
            pltpu.VMEM((4, 4, 4, 64, 128), F32),
            pltpu.SemaphoreType.DMA((9,)),
            pltpu.SemaphoreType.DMA((7,)),
        ],
        compiler_params=pltpu.CompilerParams(vmem_limit_bytes=LIMIT),
    )(feat, gs, low, total.reshape(3 * PIECE, 128))
    grad_coarse = jnp.transpose(low, (3, 0, 1, 2))
    grad_up = jnp.transpose(up, (0, 1, 2, 4, 3))
    return features, grad_skip, grad_coarse, grad_up, grad_conv, bias[0]


def solution(mesh):
    field = P(None, "gx", "gy", None)
    return jax.shard_map(
        body,
        mesh=mesh,
        in_specs=(field, field, P("gx", "gy", None), field, P(), P(), P()),
        out_specs=(field, field, field, P(), P(), P()),
        check_vma=False,
    )
```

```python
import functools

import jax
import jax.numpy as jnp
import ml_dtypes
import numpy as np
from jax import lax
from jax.experimental import pallas as pl
from jax.experimental.pallas import tpu as pltpu
from jax.sharding import PartitionSpec as P

BF = jnp.bfloat16
F32 = jnp.float32
EDGE = 8
MESH = pl.DeviceIdType.MESH
LIMIT = 56 * 2**20

C_ROWS = 592
PIECE = 2048
HALF, QUARTER, CHUNK = PIECE // 2, PIECE // 8, PIECE // 128


def mm(a, b):
    return lax.dot_general(a, b, (((1,), (0,)), ((), ())), preferred_element_type=F32)


def mm_t(a, b):
    return lax.dot_general(a, b, (((1,), (1,)), ((), ())), preferred_element_type=F32)


def lanes(parts):
    return jnp.concatenate(parts, axis=1)


def rows(parts):
    return jnp.concatenate(parts, axis=0)


def shape(dims, kind=BF):
    return jax.ShapeDtypeStruct(dims, kind)


AROUND = [(0, 1), (0, -1), (1, 0), (-1, 0), (1, 1), (1, -1), (-1, 1), (-1, -1)]


def neighbour(dx, dy):
    nx, ny = lax.axis_size("gx"), lax.axis_size("gy")
    gx, gy = lax.axis_index("gx"), lax.axis_index("gy")
    return lax.rem(gx + (dx + nx), nx), lax.rem(gy + (dy + ny), ny)


def outer(step, count):
    if step == 0:
        return pl.ds(1, count), pl.ds(1, count)
    if step > 0:
        return pl.ds(count, 1), pl.ds(0, 1)
    return pl.ds(1, 1), pl.ds(count + 1, 1)


def padding(step, count):
    if step == 0:
        return pl.ds(1, count), pl.ds(1, count)
    if step > 0:
        return pl.ds(count + 1, 1), pl.ds(0, 1)
    return pl.ds(0, 1), pl.ds(count + 1, 1)


def halo_copies(source, target, send, recv, first, place=outer):
    across, along = source.shape[0] - 2, source.shape[1] - 2
    copies = []
    for at, (dx, dy) in enumerate(AROUND):
        sx, tx = place(dx, across)
        sy, ty = place(dy, along)
        copies.append(
            pltpu.make_async_remote_copy(
                src_ref=source.at[sx, sy],
                dst_ref=target.at[tx, ty],
                send_sem=send.at[first + at],
                recv_sem=recv.at[first + at],
                device_id=neighbour(dx, dy),
                device_id_type=MESH,
            )
        )
    return copies


def start(copies):
    for copy in copies:
        copy.start()


def finish(copies):
    for copy in copies:
        copy.wait()


def clear_across(field):
    across, along = field.shape[0], field.shape[1]
    row = jnp.zeros((1, along - 2) + field.shape[2:], field.dtype)

    @pl.when(lax.axis_index("gx") == 0)
    def _():
        field[0:1, 1 : along - 1] = row

    @pl.when(lax.axis_index("gx") == lax.axis_size("gx") - 1)
    def _():
        field[across - 1 : across, 1 : along - 1] = row


def clear_outside(field):
    across, along = field.shape[0], field.shape[1]
    nx, ny = lax.axis_size("gx"), lax.axis_size("gy")
    gx, gy = lax.axis_index("gx"), lax.axis_index("gy")
    row = jnp.zeros((1,) + field.shape[1:], field.dtype)
    column = jnp.zeros((across, 1) + field.shape[2:], field.dtype)

    @pl.when(gx == 0)
    def _():
        field[0:1] = row

    @pl.when(gx == nx - 1)
    def _():
        field[across - 1 : across] = row

    @pl.when(gy == 0)
    def _():
        field[:, 0:1] = column

    @pl.when(gy == ny - 1)
    def _():
        field[:, along - 1 : along] = column


class Ring:
    def __init__(self):
        gx, gy = lax.axis_index("gx"), lax.axis_index("gy")
        self.core = lax.rem(gx, 2)
        self.x, self.y = gx // 4, gy // 2
        self.z = lax.rem(gy, 2) * 2 + lax.rem(gx // 2, 2)
        self.first = jnp.where(self.core == 0, self.x, self.y)
        self.second = jnp.where(self.core == 0, self.y, self.x)
        self.place = self.second * 4 + self.z
        self.twin = self.device(self.x, self.y, self.z, 1 - self.core)

    def device(self, x, y, z, core):
        return x * 4 + lax.rem(z, 2) * 2 + core, y * 2 + z // 2

    def along_first(self, step):
        other = lax.rem(self.first + step, 4)
        x = jnp.where(self.core == 0, other, self.x)
        y = jnp.where(self.core == 0, self.y, other)
        return other, self.device(x, y, self.z, self.core)

    def in_plane(self, step):
        a, b = lax.rem(self.second + step // 4, 4), lax.rem(self.z + step % 4, 4)
        x = jnp.where(self.core == 0, self.x, a)
        y = jnp.where(self.core == 0, a, self.y)
        return a * 4 + b, self.device(x, y, b, self.core)

    def across_first(self, step):
        x = jnp.where(self.core == 0, self.x, lax.rem(self.x + step, 4))
        y = jnp.where(self.core == 0, lax.rem(self.y + step, 4), self.y)
        return self.device(x, y, self.z, 1 - self.core)

    def beside_first(self, step):
        other = lax.rem(self.first + step, 4)
        x = jnp.where(self.core == 0, other, self.x)
        y = jnp.where(self.core == 0, self.y, other)
        return self.device(x, y, self.z, 1 - self.core)

    def greet(self, barrier):
        partners = [self.twin]
        partners += [self.along_first(step)[1] for step in range(1, 4)]
        partners += [self.across_first(step) for step in range(1, 4)]
        partners += [self.in_plane(step)[1] for step in range(1, 16)]
        for partner in partners:
            pl.semaphore_signal(barrier, inc=1, device_id=partner, device_id_type=MESH)
        return len(partners)


def span(begin, count):
    return pl.ds(pl.multiple_of(begin, 16), count)


class Piece:
    def __init__(self, ring, index, wide, mine, got0, got1, got2, acc1, acc2, out, send, recv):
        self.ring, self.base, self.wide = ring, index * 42, wide
        self.mine, self.got0, self.got1 = mine.at[index], got0.at[index], got1.at[index]
        self.got2, self.acc1, self.acc2 = got2.at[index], acc1.at[index], acc2.at[index]
        self.out, self.send, self.recv = out.at[index], send, recv
        self.flying = []

    def remote(self, src, dst, at, to):
        return pltpu.make_async_remote_copy(
            src_ref=src,
            dst_ref=dst,
            send_sem=self.send.at[self.base + at],
            recv_sem=self.recv.at[self.base + at],
            device_id=to,
            device_id_type=MESH,
        )

    def launch(self, copies):
        start(copies)
        self.flying = copies

    def step0(self):
        ring = self.ring
        theirs = self.mine.at[span((1 - ring.core) * HALF, HALF)]
        self.launch([self.remote(theirs, self.got0, 0, ring.twin)])

    def step1(self):
        ring = self.ring
        finish(self.flying)

        def add(t, carry):
            own = self.mine[span(ring.core * HALF + t * 256, 256)].astype(F32)
            at = span(t * 256, 256)
            self.got0[at] = (own + self.got0[at].astype(F32)).astype(BF)
            return carry

        lax.fori_loop(0, HALF // 256, add, 0)
        copies = []
        for step in range(1, 4):
            other, to = ring.along_first(step)
            theirs = self.got0.at[span(other * QUARTER, QUARTER)]
            copies.append(self.remote(theirs, self.got1.at[step - 1], step, to))
        self.launch(copies)

    def step2(self):
        ring = self.ring
        finish(self.flying)
        total = self.got0[span(ring.first * QUARTER, QUARTER)].astype(F32)
        for step in range(3):
            total += self.got1[step].astype(F32)
        self.acc1[...] = total.astype(BF)
        copies = []
        for step in range(1, 16):
            other, to = ring.in_plane(step)
            theirs = self.acc1.at[span(other * CHUNK, CHUNK)]
            copies.append(self.remote(theirs, self.got2.at[step - 1], 3 + step, to))
        self.launch(copies)

    def step3(self):
        ring = self.ring
        finish(self.flying)
        total = self.acc1[span(ring.place * CHUNK, CHUNK)].astype(F32)
        for step in range(15):
            total += self.got2[step].astype(F32)
        own = span(ring.place * CHUNK, CHUNK)
        self.acc2[own] = total.astype(BF)
        copies = []
        for step in range(1, 16):
            other, to = ring.in_plane(step)
            copies.append(self.remote(self.acc2.at[own], self.acc2.at[own], 18 + step, to))
        self.launch(copies)

    def step4(self):
        ring = self.ring
        finish(self.flying)
        own = span(ring.core * HALF + ring.first * QUARTER, QUARTER)
        copies = []
        for step in range(1, 4):
            other, to = ring.along_first(step)
            copies.append(self.remote(self.acc2, self.out.at[own], 33 + step, to))
            if self.wide:
                to = ring.beside_first(step)
                copies.append(self.remote(self.acc2, self.out.at[own], 36 + step, to))
        if self.wide:
            copies.append(self.remote(self.acc2, self.out.at[own], 40, ring.twin))
        self.launch(copies)
        self.out[own] = self.acc2[...]

    def step5(self):
        ring = self.ring
        finish(self.flying)
        own = self.out.at[span(ring.core * HALF, HALF)]
        self.launch([self.remote(own, own, 37, ring.twin)])

    def step6(self):
        finish(self.flying)


def lane_of(dims):
    return lax.broadcasted_iota(jnp.int32, dims, len(dims) - 1)


def conv_window(field, i, pair):
    return rows(
        [
            lanes(
                [
                    field[i + 4 * h + k, pl.ds(y, 3)].reshape(192, 128)
                    for y in pair
                    for h in range(2)
                ]
            )
            for k in range(3)
        ]
    )


def join_taps(taps, lane):
    back = jnp.where(lane == 0, 0.0, pltpu.roll(taps[0:64], 1, 1))
    ahead = jnp.where(lane == 127, 0.0, pltpu.roll(taps[128:192], 127, 1))
    return taps[64:128] + back + ahead


def main_body(
    skip_any,
    cot_any,
    upw_any,
    coarse_any,
    convw_any,
    spread_any,
    gather_any,
    conv_bias,
    occupancy,
    wide_rows,
    wide_columns,
    feat_any,
    gs_any,
    low_any,
    total_any,
    low,
    total,
    skip,
    cot,
    upw,
    coarse,
    convw,
    spread_up,
    gather_z,
    feat,
    gs,
    feat_t,
    gs_t,
    local_sem,
    sf,
    cf,
    mf,
    masks,
    keep_ref,
    bias,
    cot_t,
    wc,
    wb,
    wu,
    wt,
    ac,
    ups,
    mx,
    gpf,
    g3,
    gacc,
    d4,
    acc,
    part,
    part_in,
    mine,
    got0,
    got1,
    got2,
    acc1,
    acc2,
    halo_send,
    halo_recv,
    sum_send,
    sum_recv,
):
    ring = Ring()
    barrier = pltpu.get_barrier_semaphore()
    for dx, dy in AROUND:
        pl.semaphore_signal(barrier, inc=1, device_id=neighbour(dx, dy), device_id_type=MESH)
    greeted = ring.greet(barrier) + len(AROUND)
    loads = [
        pltpu.make_async_copy(coarse_any, coarse, local_sem.at[5]),
        pltpu.make_async_copy(skip_any, skip, local_sem.at[0]),
        pltpu.make_async_copy(cot_any, cot, local_sem.at[1]),
        pltpu.make_async_copy(convw_any, convw, local_sem.at[6]),
        pltpu.make_async_copy(upw_any, upw, local_sem.at[2]),
        pltpu.make_async_copy(spread_any, spread_up, local_sem.at[7]),
        pltpu.make_async_copy(gather_any, gather_z, local_sem.at[8]),
    ]
    start(loads)
    lane = lane_of((64, 128))

    there = jnp.where(occupancy[0] > 0, 1.0, 0.0)
    mf[1, 1] = mm(jnp.broadcast_to(there, (16, 16)).astype(BF), wide_rows[...]).astype(BF)
    keep_ref[...] = mm_t(wide_columns[...], jnp.broadcast_to(there, (128, 16)).astype(BF))

    loads[0].wait()

    def fill_coarse(t, carry):
        x, y = t // 4, t % 4
        own = jnp.where(keep_ref[...] > 0.5, coarse[x, y].astype(F32), 0.0)
        cf[x + 1, y + 1] = own.astype(BF)
        return carry

    lax.fori_loop(0, 16, fill_coarse, 0, unroll=4)
    pl.semaphore_wait(barrier, greeted)
    coarse_copies = halo_copies(cf, cf, halo_send, halo_recv, 0)
    mask_copies = halo_copies(mf, mf, halo_send, halo_recv, 8)
    start(coarse_copies)
    start(mask_copies)

    loads[1].wait()

    def fill_skip(x, carry):
        sf[x + 1, pl.ds(1, 8)] = jnp.swapaxes(skip[:, x], 0, 1)
        return carry

    lax.fori_loop(0, 8, fill_skip, 0, unroll=2)
    skip_copies = halo_copies(sf, sf, halo_send, halo_recv, 16)

    loads[2].wait()

    def fill_cot(x, carry):
        cot_t[x] = jnp.swapaxes(cot[:, x], 0, 1)
        return carry

    lax.fori_loop(0, 8, fill_cot, 0, unroll=2)
    finish(loads[3:7])
    bias[...] = jnp.broadcast_to(conv_bias[...], (128, 64)).T
    for kz in range(3):
        for pair in range(5):
            taps = [(k // 3, k % 3) for k in (2 * pair, 2 * pair + 1) if k < 9]
            fore = [convw[kx, ky, kz] for kx, ky in taps]
            aft = [convw[2 - kx, 2 - ky, 2 - kz] for kx, ky in taps]
            at, col = kz * 64, pair * 128
            wide = 64 * len(taps)
            wc[at : at + 64, col : col + wide] = rows(fore).T
            wb[at : at + 64, col : col + wide] = lanes(aft)
    for sx in range(2):
        for sy in range(2):
            for tx in range(2):
                for ty in range(2):
                    block = upw[2 + sx - 2 * tx, 2 + sy - 2 * ty].reshape(256, 128)
                    at, col = (sx * 2 + sy) * 256, (tx * 2 + ty) * 128
                    wu[at : at + 256, col : col + 128] = block
                    wt[sy, col : col + 128, sx * 256 : sx * 256 + 256] = block.T

    def pair_coarse(i, y):
        ac[i, y] = rows([cf[i, y], cf[i + 2, y]]).T

    def pair_middle(t, carry):
        pair_coarse(1 + t // 4, 1 + t % 4)
        return carry

    def pair_across(t, carry):
        pair_coarse((t // 6) * 3, t % 6)
        return carry

    def pair_along(t, carry):
        pair_coarse(1 + t // 2, (t % 2) * 5)
        return carry

    def join(p, q, taps):
        wide = rows(
            [
                lanes([taps[(s * 4 + kz) * 64 : (s * 4 + kz + 1) * 64] for kz in range(4)])
                for s in range(4)
            ]
        )
        up = mm(wide, spread_up[...])
        for s in range(4):
            for h in range(2):
                ups[2 * p + s // 2 + 4 * h, 2 * q + s % 2] = up[
                    s * 64 : s * 64 + 64, h * 128 : h * 128 + 128
                ]

    def upsample(blocks):
        window = lanes([ac[p : p + 2, q : q + 2].reshape(512, 128) for p, q in blocks])
        taps = mm(wu[...], window).astype(BF)
        for at, (p, q) in enumerate(blocks):
            join(p, q, taps[:, at * 128 : at * 128 + 128])

    start(skip_copies)
    lax.fori_loop(0, 8, pair_middle, 0, unroll=4)
    upsample([(1, 1), (1, 2), (1, 3)])
    finish(coarse_copies)
    clear_outside(cf)
    lax.fori_loop(0, 12, pair_across, 0, unroll=4)
    lax.fori_loop(0, 4, pair_along, 0, unroll=4)
    for p in (0, 2):
        upsample([(p, 0), (p, 1)])
        upsample([(p, 2), (p, 3)])
        upsample([(p, 4), (1, p * 2)])

    finish(mask_copies)
    clear_outside(mf)
    for bx in range(3):
        for by in range(3):
            masks[bx, by] = mf[bx, by].astype(F32)

    def mix(x, y):
        bx = jnp.where(x == 0, 0, jnp.where(x == 9, 2, 1))
        by = jnp.where(y == 0, 0, jnp.where(y == 9, 2, 1))
        value = ups[x, y] + sf[x, y].astype(F32)
        mx[x, y] = jnp.where(masks[bx, by, 0:1, :] > 0.5, value, 0.0).astype(BF)

    def mix_middle(t, carry):
        mix(1 + t // 8, 1 + t % 8)
        return carry

    def mix_across(t, carry):
        mix((t // 8) * 9, 1 + t % 8)
        return carry

    def mix_along(t, carry):
        mix(t // 2, (t % 2) * 9)
        return carry

    lax.fori_loop(0, 64, mix_middle, 0, unroll=4)

    inside = masks[1, 1, 0:1, :] > 0.5

    def conv(i, pair):
        taps = mm(wc[...], conv_window(mx, i, pair))
        for e, y in enumerate(pair):
            for h in range(2):
                at = (e * 2 + h) * 128
                pre = join_taps(taps[:, at : at + 128], lane) + bias[...]
                sig = 1.0 / (1.0 + jnp.exp(-pre))
                feat[i + 4 * h, y] = jnp.where(inside, pre * sig, 0.0).astype(BF)
                slope = sig * (1.0 + pre * (1.0 - sig))
                grad = cot_t[i + 4 * h, y].astype(F32) * slope
                grad = jnp.where(inside, grad, 0.0).astype(BF)
                gpf[i + 4 * h + 1, y + 1] = grad
                wide = grad.astype(F32)
                before = jnp.where(lane == 127, 0.0, pltpu.roll(wide, 127, 1)).astype(BF)
                after = jnp.where(lane == 0, 0.0, pltpu.roll(wide, 1, 1)).astype(BF)
                g3[i, y, :, h * 128 : h * 128 + 128] = rows([before, grad, after])

    def middle(step):
        def run(t, carry):
            y = 1 + (t % 3) * 2
            step(1 + t // 3, (y, y + 1))
            return carry

        lax.fori_loop(0, 6, run, 0, unroll=3)

    def ends_along(step, first, last):
        def run(i, carry):
            step(i, (0, 7))
            return carry

        lax.fori_loop(first, last, run, 0, unroll=last - first)

    def ends_across(step, i):
        def run(t, carry):
            y = 1 + t * 2
            step(i, (y, y + 1))
            return carry

        lax.fori_loop(0, 3, run, 0, unroll=3)

    gp_copies = halo_copies(gpf, gpf, halo_send, halo_recv, 24)
    middle(conv)
    finish(skip_copies)
    lax.fori_loop(0, 16, mix_across, 0, unroll=4)
    lax.fori_loop(0, 20, mix_along, 0, unroll=4)
    ends_along(conv, 0, 4)
    start(gp_copies[0:2])
    start(gp_copies[4:8])
    ends_across(conv, 0)
    ends_across(conv, 3)
    start(gp_copies[2:4])

    gacc[...] = jnp.zeros_like(gacc)

    def kernel_grad(t, carry):
        i, y = t // 2, (t % 2) * 4
        grads = lanes([g3[i, y + j] for j in range(4)])
        for k in range(3):
            cells = lanes(
                [
                    mx[i + 4 * h + k, pl.ds(y + j, 3)].reshape(192, 128)
                    for j in range(4)
                    for h in range(2)
                ]
            )
            gacc[k * 192 : k * 192 + 192, :] += mm_t(cells, grads)
        gacc[576:592, :] += mm_t(jnp.ones((16, 1024), BF), grads)
        return carry

    lax.fori_loop(0, 8, kernel_grad, 0, unroll=4)
    mine[2, 0:C_ROWS] = gacc[:, 0:128].astype(BF)
    mine[2, C_ROWS : 2 * C_ROWS, 0:64] = gacc[:, 128:192].astype(BF)
    mine[2, C_ROWS : 2 * C_ROWS, 64:128] = jnp.zeros((C_ROWS, 64), BF)
    mine[2, 2 * C_ROWS : PIECE] = jnp.zeros((PIECE - 2 * C_ROWS, 128), BF)
    sums = [
        Piece(ring, at, at == 1, mine, got0, got1, got2, acc1, acc2, total, sum_send, sum_recv)
        for at in range(3)
    ]
    even, odd, conv_sum = sums
    conv_sum.step0()

    def back(i, pair):
        taps = mm(wb[...], conv_window(gpf, i, pair))
        for e, y in enumerate(pair):
            both = []
            for h in range(2):
                at = (e * 2 + h) * 128
                grad = join_taps(taps[:, at : at + 128], lane)
                grad = jnp.where(inside, grad, 0.0).astype(BF)
                gs[i + 4 * h, y] = grad
                both.append(grad)
            apart = mm(lanes(both), gather_z[...]).astype(BF)
            for kz in range(4):
                d4[i, y, kz * 64 : kz * 64 + 64, :] = apart[:, kz * 128 : kz * 128 + 128]

    def up_grad(sx, sy):
        spots = [(pi, qi) for pi in range(1 - sx, 3 - sx) for qi in range(1 - sy, 5 - sy)]
        grads = lanes([d4[2 * pi - 1 + sx, 2 * qi - 1 + sy] for pi, qi in spots])
        cells = rows(
            [
                lanes([ac[pi + tx, qi + ty] for pi, qi in spots])
                for tx in range(2)
                for ty in range(2)
            ]
        )
        result = mm_t(grads, cells).astype(BF)
        for tx in range(2):
            for ty in range(2):
                at, col = (tx * 4 + 2 + sy - 2 * ty) * 256, (tx * 2 + ty) * 128
                mine[sx, at : at + 256] = result[:, col : col + 128]

    middle(back)
    finish(gp_copies)
    clear_outside(gpf)
    ends_along(back, 1, 2)
    ends_along(back, 3, 4)
    ends_across(back, 3)
    conv_sum.step1()
    up_grad(0, 0)
    up_grad(0, 1)
    even.step0()
    ends_along(back, 2, 3)
    ends_along(back, 0, 1)
    ends_across(back, 0)
    even.step1()
    up_grad(1, 0)
    up_grad(1, 1)
    odd.step0()
    conv_sum.step2()

    acc[...] = jnp.zeros_like(acc)

    def lower(sy, across):
        if across == 1:
            weight = wt[sy]
            cells = rows([lanes([d4[1 + sx, 2 * q + 1 - sy] for q in range(4)]) for sx in range(2)])
        else:
            sx, i = (1, 0) if across == 0 else (0, 3)
            weight = wt[sy, :, sx * 256 : sx * 256 + 256]
            cells = lanes([d4[i, 2 * q + 1 - sy] for q in range(4)])
        result = mm(weight, cells)
        for tx in range(2):
            for ty in range(2):
                at = (tx * 2 + ty) * 128
                for q in range(4):
                    acc[across + tx, q + ty + 1 - sy] += result[
                        at : at + 128, q * 128 : q * 128 + 128
                    ]

    lower(0, 0)
    lower(1, 0)
    lower(0, 1)
    odd.step1()
    lower(1, 1)
    lower(0, 2)
    lower(1, 2)
    even.step2()

    def turned(i, y):
        return acc[i, y].T

    def fold(y, carry):
        cells = [turned(i, y) for i in range(4)]
        left, right = [c[0:64] for c in cells], [c[64:128] for c in cells]
        folded = [
            left[0],
            left[1],
            left[2] + right[0],
            left[3] + right[1],
            right[2],
            right[3],
        ]
        for x in range(6):
            part[x, y] = folded[x].astype(BF)
        return carry

    lax.fori_loop(0, 6, fold, 0)
    part_copies = halo_copies(part, part_in, halo_send, halo_recv, 32, padding)
    start(part_copies)
    conv_sum.step3()
    odd.step2()

    def turn_feat(x, carry):
        feat_t[:, x] = jnp.swapaxes(feat[x], 0, 1)
        return carry

    lax.fori_loop(0, 8, turn_feat, 0, unroll=2)
    stores = [
        pltpu.make_async_copy(feat_t, feat_any, local_sem.at[3]),
        pltpu.make_async_copy(gs_t, gs_any, local_sem.at[4]),
    ]
    start(stores[0:1])
    even.step3()
    odd.step3()

    def turn_gs(x, carry):
        gs_t[:, x] = jnp.swapaxes(gs[x], 0, 1)
        return carry

    lax.fori_loop(0, 8, turn_gs, 0, unroll=2)
    start(stores[1:2])
    conv_sum.step4()
    even.step4()
    odd.step4()
    stores.append(pltpu.make_async_copy(low, low_any, local_sem.at[9]))
    stores += [
        pltpu.make_async_copy(total.at[at], total_any.at[at], local_sem.at[10 + at])
        for at in range(3)
    ]
    conv_sum.step5()
    even.step5()
    finish(part_copies)
    clear_outside(part_in)
    for x in range(4):
        for y in range(4):
            across = [x + 1] + [0] * (x == 0) + [5] * (x == 3)
            along = [y + 1] + [0] * (y == 0) + [5] * (y == 3)
            value = part[x + 1, y + 1].astype(F32)
            for px in across:
                for py in along:
                    if (px, py) != (x + 1, y + 1):
                        value += part_in[px, py].astype(F32)
            low[x, y] = jnp.where(keep_ref[...] > 0.5, value, 0.0).astype(BF)
    stores[2].start()
    conv_sum.step6()
    stores[5].start()
    even.step6()
    stores[3].start()
    odd.step6()
    stores[4].start()
    finish(stores)


def final_body(
    scale,
    feat,
    gs,
    low,
    total,
    features,
    grad_skip,
    grad_coarse,
    up_any,
    conv,
    bias,
    v0,
    v1,
    v2,
    sums,
    up,
    come_sem,
    go_sem,
):
    def part(at, count):
        return total.at[pl.ds(at, count)], sums.at[pl.ds(at, count)]

    taps = [(2 + sx - 2 * tx, sx * PIECE + tx * HALF) for tx in range(2) for sx in range(2)]
    pieces = [(feat, v0), (gs, v1), (low, v2)]
    pieces += [part(at, HALF) for kx, at in taps]
    pieces += [part(2 * PIECE, C_ROWS), part(2 * PIECE + C_ROWS, C_ROWS)]
    come = [pltpu.make_async_copy(a, b, come_sem.at[n]) for n, (a, b) in enumerate(pieces)]
    start(come)
    go = [(v0, features), (v1, grad_skip), (v2, grad_coarse)]
    go += [(up.at[kx], up_any.at[kx]) for kx, at in taps]
    go = [pltpu.make_async_copy(a, b, go_sem.at[n]) for n, (a, b) in enumerate(go)]
    for n in range(3):
        come[n].wait()
        go[n].start()
    for n, (kx, at) in enumerate(taps):
        come[3 + n].wait()

        def column(t, carry):
            block = sums[pl.ds(pl.multiple_of(at + t * 256, 256), 256)]
            up[kx, t] = (block.astype(F32) * scale).reshape(4, 64, 128)
            return carry

        lax.fori_loop(0, 4, column, 0)
        go[3 + n].start()
    finish(come[7:9])
    for tap in range(9):
        at = 2 * PIECE + tap * 64
        left = sums[at : at + 64].astype(F32) * scale
        right = sums[C_ROWS + at : C_ROWS + at + 64].astype(F32) * scale
        conv[tap // 3, tap % 3, 0] = left[:, 0:64]
        conv[tap // 3, tap % 3, 1] = left[:, 64:128]
        conv[tap // 3, tap % 3, 2] = right[:, 0:64]
    bias[...] = (sums[2 * PIECE + 576 : 2 * PIECE + 592].astype(F32) * scale)[0:1, 64:128]
    finish(go)


def spread_matrix():
    row, column = np.arange(512)[:, None], np.arange(256)[None, :]
    kz, h, j = row // 128, (row // 64) % 2, row % 64
    hit = (h == column // 128) & (column % 128 == 2 * j - 1 + kz)
    return hit.astype(ml_dtypes.bfloat16)


def body(coarse, skip, occupancy, cotangent, up_weight, conv_weight, conv_bias):
    spread_up = spread_matrix()
    wide_rows = np.repeat(np.eye(16), EDGE, axis=1).astype(ml_dtypes.bfloat16)
    wide_columns = np.repeat(np.eye(16), EDGE // 2, axis=0).astype(ml_dtypes.bfloat16)
    vmem, anywhere = pl.BlockSpec(memory_space=pltpu.VMEM), pl.BlockSpec(memory_space=pl.ANY)
    plane = (64, 8, 8, 128)
    feat, gs, low, total = pl.pallas_call(
        main_body,
        out_shape=[shape(plane), shape(plane), shape((4, 4, 64, 128)), shape((3, PIECE, 128))],
        in_specs=[anywhere] * 7 + [vmem] * 4,
        out_specs=[anywhere] * 4,
        scratch_shapes=[
            pltpu.VMEM((4, 4, 64, 128), BF),
            pltpu.VMEM((3, PIECE, 128), BF),
            pltpu.VMEM(plane, BF),
            pltpu.VMEM(plane, BF),
            pltpu.VMEM((4, 4, 4, 64, 128), BF),
            pltpu.VMEM((4, 4, 64, 128), BF),
            pltpu.VMEM((3, 3, 3, 64, 64), BF),
            pltpu.VMEM((512, 256), BF),
            pltpu.VMEM((256, 512), BF),
            pltpu.VMEM((8, 8, 64, 128), BF),
            pltpu.VMEM((8, 8, 64, 128), BF),
            pltpu.VMEM(plane, BF),
            pltpu.VMEM(plane, BF),
            pltpu.SemaphoreType.DMA((13,)),
            pltpu.VMEM((10, 10, 64, 128), BF),
            pltpu.VMEM((6, 6, 64, 128), BF),
            pltpu.VMEM((3, 3, 16, 128), BF),
            pltpu.VMEM((3, 3, 16, 128), F32),
            pltpu.VMEM((64, 128), F32),
            pltpu.VMEM((64, 128), F32),
            pltpu.VMEM((8, 8, 64, 128), BF),
            pltpu.VMEM((192, 576), BF),
            pltpu.VMEM((192, 576), BF),
            pltpu.VMEM((1024, 512), BF),
            pltpu.VMEM((2, 512, 512), BF),
            pltpu.VMEM((4, 6, 128, 128), BF),
            pltpu.VMEM((10, 10, 64, 128), F32),
            pltpu.VMEM((10, 10, 64, 128), BF),
            pltpu.VMEM((10, 10, 64, 128), BF),
            pltpu.VMEM((4, 8, 192, 256), BF),
            pltpu.VMEM((C_ROWS, 192), F32),
            pltpu.VMEM((4, 8, 256, 128), BF),
            pltpu.VMEM((4, 6, 128, 128), F32),
            pltpu.VMEM((6, 6, 64, 128), BF),
            pltpu.VMEM((6, 6, 64, 128), BF),
            pltpu.VMEM((3, PIECE, 128), BF),
            pltpu.VMEM((3, HALF, 128), BF),
            pltpu.VMEM((3, 3, QUARTER, 128), BF),
            pltpu.VMEM((3, 15, CHUNK, 128), BF),
            pltpu.VMEM((3, QUARTER, 128), BF),
            pltpu.VMEM((3, QUARTER, 128), BF),
            pltpu.SemaphoreType.DMA((40,)),
            pltpu.SemaphoreType.DMA((40,)),
            pltpu.SemaphoreType.DMA((3 * 42,)),
            pltpu.SemaphoreType.DMA((3 * 42,)),
        ],
        compiler_params=pltpu.CompilerParams(
            vmem_limit_bytes=LIMIT, collective_id=1, has_side_effects=True
        ),
    )(
        skip,
        cotangent,
        jnp.transpose(up_weight, (0, 1, 2, 4, 3)),
        jnp.transpose(coarse, (1, 2, 3, 0)),
        conv_weight,
        spread_up,
        np.ascontiguousarray(spread_up.T),
        conv_bias[None],
        occupancy[0],
        wide_rows,
        wide_columns,
    )
    cells = 8192 * lax.axis_size("gx") * lax.axis_size("gy")
    features, grad_skip, low, up, grad_conv, bias = pl.pallas_call(
        functools.partial(final_body, float(cells) ** -0.5),
        out_shape=[
            shape(plane),
            shape(plane),
            shape((4, 4, 64, 128)),
            shape((4, 4, 4, 64, 128), F32),
            shape((3, 3, 3, 64, 64), F32),
            shape((1, 64), F32),
        ],
        in_specs=[anywhere] * 4,
        out_specs=[anywhere] * 4 + [vmem] * 2,
        scratch_shapes=[
            pltpu.VMEM(plane, BF),
            pltpu.VMEM(plane, BF),
            pltpu.VMEM((4, 4, 64, 128), BF),
            pltpu.VMEM((3 * PIECE, 128), BF),
            pltpu.VMEM((4, 4, 4, 64, 128), F32),
            pltpu.SemaphoreType.DMA((9,)),
            pltpu.SemaphoreType.DMA((7,)),
        ],
        compiler_params=pltpu.CompilerParams(vmem_limit_bytes=LIMIT),
    )(feat, gs, low, total.reshape(3 * PIECE, 128))
    grad_coarse = jnp.transpose(low, (3, 0, 1, 2))
    grad_up = jnp.transpose(up, (0, 1, 2, 4, 3))
    return features, grad_skip, grad_coarse, grad_up, grad_conv, bias[0]


def solution(mesh):
    field = P(None, "gx", "gy", None)
    return jax.shard_map(
        body,
        mesh=mesh,
        in_specs=(field, field, P("gx", "gy", None), field, P(), P(), P()),
        out_specs=(field, field, field, P(), P(), P()),
        check_vma=False,
    )
```

```python
import functools

import jax
import jax.numpy as jnp
import ml_dtypes
import numpy as np
from jax import lax
from jax.experimental import pallas as pl
from jax.experimental.pallas import tpu as pltpu
from jax.sharding import PartitionSpec as P

BF = jnp.bfloat16
F32 = jnp.float32
EDGE = 8
MESH = pl.DeviceIdType.MESH
LIMIT = 56 * 2**20

C_ROWS = 592
PIECE = 2048
HALF, QUARTER, CHUNK = PIECE // 2, PIECE // 8, PIECE // 128


def mm(a, b):
    return lax.dot_general(a, b, (((1,), (0,)), ((), ())), preferred_element_type=F32)


def mm_t(a, b):
    return lax.dot_general(a, b, (((1,), (1,)), ((), ())), preferred_element_type=F32)


def lanes(parts):
    return jnp.concatenate(parts, axis=1)


def rows(parts):
    return jnp.concatenate(parts, axis=0)


def shape(dims, kind=BF):
    return jax.ShapeDtypeStruct(dims, kind)


AROUND = [(0, 1), (0, -1), (1, 0), (-1, 0), (1, 1), (1, -1), (-1, 1), (-1, -1)]


def neighbour(dx, dy):
    nx, ny = lax.axis_size("gx"), lax.axis_size("gy")
    gx, gy = lax.axis_index("gx"), lax.axis_index("gy")
    return lax.rem(gx + (dx + nx), nx), lax.rem(gy + (dy + ny), ny)


def outer(step, count):
    if step == 0:
        return pl.ds(1, count), pl.ds(1, count)
    if step > 0:
        return pl.ds(count, 1), pl.ds(0, 1)
    return pl.ds(1, 1), pl.ds(count + 1, 1)


def padding(step, count):
    if step == 0:
        return pl.ds(1, count), pl.ds(1, count)
    if step > 0:
        return pl.ds(count + 1, 1), pl.ds(0, 1)
    return pl.ds(0, 1), pl.ds(count + 1, 1)


def halo_copies(source, target, send, recv, first, place=outer):
    across, along = source.shape[0] - 2, source.shape[1] - 2
    copies = []
    for at, (dx, dy) in enumerate(AROUND):
        sx, tx = place(dx, across)
        sy, ty = place(dy, along)
        copies.append(
            pltpu.make_async_remote_copy(
                src_ref=source.at[sx, sy],
                dst_ref=target.at[tx, ty],
                send_sem=send.at[first + at],
                recv_sem=recv.at[first + at],
                device_id=neighbour(dx, dy),
                device_id_type=MESH,
            )
        )
    return copies


def start(copies):
    for copy in copies:
        copy.start()


def finish(copies):
    for copy in copies:
        copy.wait()


def clear_across(field):
    across, along = field.shape[0], field.shape[1]
    row = jnp.zeros((1, along - 2) + field.shape[2:], field.dtype)

    @pl.when(lax.axis_index("gx") == 0)
    def _():
        field[0:1, 1 : along - 1] = row

    @pl.when(lax.axis_index("gx") == lax.axis_size("gx") - 1)
    def _():
        field[across - 1 : across, 1 : along - 1] = row


def clear_outside(field):
    across, along = field.shape[0], field.shape[1]
    nx, ny = lax.axis_size("gx"), lax.axis_size("gy")
    gx, gy = lax.axis_index("gx"), lax.axis_index("gy")
    row = jnp.zeros((1,) + field.shape[1:], field.dtype)
    column = jnp.zeros((across, 1) + field.shape[2:], field.dtype)

    @pl.when(gx == 0)
    def _():
        field[0:1] = row

    @pl.when(gx == nx - 1)
    def _():
        field[across - 1 : across] = row

    @pl.when(gy == 0)
    def _():
        field[:, 0:1] = column

    @pl.when(gy == ny - 1)
    def _():
        field[:, along - 1 : along] = column


class Ring:
    def __init__(self):
        gx, gy = lax.axis_index("gx"), lax.axis_index("gy")
        self.core = lax.rem(gx, 2)
        self.x, self.y = gx // 4, gy // 2
        self.z = lax.rem(gy, 2) * 2 + lax.rem(gx // 2, 2)
        self.first = jnp.where(self.core == 0, self.x, self.y)
        self.second = jnp.where(self.core == 0, self.y, self.x)
        self.place = self.second * 4 + self.z
        self.twin = self.device(self.x, self.y, self.z, 1 - self.core)

    def device(self, x, y, z, core):
        return x * 4 + lax.rem(z, 2) * 2 + core, y * 2 + z // 2

    def along_first(self, step):
        other = lax.rem(self.first + step, 4)
        x = jnp.where(self.core == 0, other, self.x)
        y = jnp.where(self.core == 0, self.y, other)
        return other, self.device(x, y, self.z, self.core)

    def in_plane(self, step):
        a, b = lax.rem(self.second + step // 4, 4), lax.rem(self.z + step % 4, 4)
        x = jnp.where(self.core == 0, self.x, a)
        y = jnp.where(self.core == 0, a, self.y)
        return a * 4 + b, self.device(x, y, b, self.core)

    def across_first(self, step):
        x = jnp.where(self.core == 0, self.x, lax.rem(self.x + step, 4))
        y = jnp.where(self.core == 0, lax.rem(self.y + step, 4), self.y)
        return self.device(x, y, self.z, 1 - self.core)

    def beside_first(self, step):
        other = lax.rem(self.first + step, 4)
        x = jnp.where(self.core == 0, other, self.x)
        y = jnp.where(self.core == 0, self.y, other)
        return self.device(x, y, self.z, 1 - self.core)

    def greet(self, barrier):
        partners = [self.twin]
        partners += [self.along_first(step)[1] for step in range(1, 4)]
        partners += [self.across_first(step) for step in range(1, 4)]
        partners += [self.in_plane(step)[1] for step in range(1, 16)]
        for partner in partners:
            pl.semaphore_signal(barrier, inc=1, device_id=partner, device_id_type=MESH)
        return len(partners)


def span(begin, count):
    return pl.ds(pl.multiple_of(begin, 16), count)


class Piece:
    def __init__(self, ring, index, wide, mine, got0, got1, got2, acc1, acc2, out, send, recv):
        self.ring, self.base, self.wide = ring, index * 42, wide
        self.mine, self.got0, self.got1 = mine.at[index], got0.at[index], got1.at[index]
        self.got2, self.acc1, self.acc2 = got2.at[index], acc1.at[index], acc2.at[index]
        self.out, self.send, self.recv = out.at[index], send, recv
        self.flying = []

    def remote(self, src, dst, at, to):
        return pltpu.make_async_remote_copy(
            src_ref=src,
            dst_ref=dst,
            send_sem=self.send.at[self.base + at],
            recv_sem=self.recv.at[self.base + at],
            device_id=to,
            device_id_type=MESH,
        )

    def launch(self, copies):
        start(copies)
        self.flying = copies

    def step0(self):
        ring = self.ring
        theirs = self.mine.at[span((1 - ring.core) * HALF, HALF)]
        self.launch([self.remote(theirs, self.got0, 0, ring.twin)])

    def step1(self):
        ring = self.ring
        finish(self.flying)

        def add(t, carry):
            own = self.mine[span(ring.core * HALF + t * 256, 256)].astype(F32)
            at = span(t * 256, 256)
            self.got0[at] = (own + self.got0[at].astype(F32)).astype(BF)
            return carry

        lax.fori_loop(0, HALF // 256, add, 0)
        copies = []
        for step in range(1, 4):
            other, to = ring.along_first(step)
            theirs = self.got0.at[span(other * QUARTER, QUARTER)]
            copies.append(self.remote(theirs, self.got1.at[step - 1], step, to))
        self.launch(copies)

    def step2(self):
        ring = self.ring
        finish(self.flying)
        total = self.got0[span(ring.first * QUARTER, QUARTER)].astype(F32)
        for step in range(3):
            total += self.got1[step].astype(F32)
        self.acc1[...] = total.astype(BF)
        copies = []
        for step in range(1, 16):
            other, to = ring.in_plane(step)
            theirs = self.acc1.at[span(other * CHUNK, CHUNK)]
            copies.append(self.remote(theirs, self.got2.at[step - 1], 3 + step, to))
        self.launch(copies)

    def step3(self):
        ring = self.ring
        finish(self.flying)
        total = self.acc1[span(ring.place * CHUNK, CHUNK)].astype(F32)
        for step in range(15):
            total += self.got2[step].astype(F32)
        own = span(ring.place * CHUNK, CHUNK)
        self.acc2[own] = total.astype(BF)
        copies = []
        for step in range(1, 16):
            other, to = ring.in_plane(step)
            copies.append(self.remote(self.acc2.at[own], self.acc2.at[own], 18 + step, to))
        self.launch(copies)

    def step4(self):
        ring = self.ring
        finish(self.flying)
        own = span(ring.core * HALF + ring.first * QUARTER, QUARTER)
        copies = []
        for step in range(1, 4):
            other, to = ring.along_first(step)
            copies.append(self.remote(self.acc2, self.out.at[own], 33 + step, to))
            if self.wide:
                to = ring.beside_first(step)
                copies.append(self.remote(self.acc2, self.out.at[own], 36 + step, to))
        if self.wide:
            copies.append(self.remote(self.acc2, self.out.at[own], 40, ring.twin))
        self.launch(copies)
        self.out[own] = self.acc2[...]

    def step5(self):
        ring = self.ring
        finish(self.flying)
        own = self.out.at[span(ring.core * HALF, HALF)]
        self.launch([self.remote(own, own, 37, ring.twin)])

    def step6(self):
        finish(self.flying)


def lane_of(dims):
    return lax.broadcasted_iota(jnp.int32, dims, len(dims) - 1)


def conv_window(field, i, pair):
    return rows(
        [
            lanes(
                [
                    field[i + 4 * h + k, pl.ds(y, 3)].reshape(192, 128)
                    for y in pair
                    for h in range(2)
                ]
            )
            for k in range(3)
        ]
    )


def join_taps(taps, lane):
    back = jnp.where(lane == 0, 0.0, pltpu.roll(taps[0:64], 1, 1))
    ahead = jnp.where(lane == 127, 0.0, pltpu.roll(taps[128:192], 127, 1))
    return taps[64:128] + back + ahead


def main_body(
    skip_any,
    cot_any,
    upw_any,
    coarse_any,
    convw_any,
    spread_any,
    gather_any,
    conv_bias,
    occupancy,
    wide_rows,
    wide_columns,
    feat_any,
    gs_any,
    low_any,
    total_any,
    low,
    total,
    skip,
    cot,
    upw,
    coarse,
    convw,
    spread_up,
    gather_z,
    feat,
    gs,
    feat_t,
    gs_t,
    local_sem,
    sf,
    cf,
    mf,
    masks,
    keep_ref,
    bias,
    cot_t,
    wc,
    wb,
    wu,
    wt,
    ac,
    ups,
    mx,
    gpf,
    g3,
    gacc,
    d4,
    acc,
    part,
    part_in,
    mine,
    got0,
    got1,
    got2,
    acc1,
    acc2,
    halo_send,
    halo_recv,
    sum_send,
    sum_recv,
):
    ring = Ring()
    barrier = pltpu.get_barrier_semaphore()
    for dx, dy in AROUND:
        pl.semaphore_signal(barrier, inc=1, device_id=neighbour(dx, dy), device_id_type=MESH)
    greeted = ring.greet(barrier) + len(AROUND)
    loads = [
        pltpu.make_async_copy(coarse_any, coarse, local_sem.at[5]),
        pltpu.make_async_copy(skip_any, skip, local_sem.at[0]),
        pltpu.make_async_copy(cot_any, cot, local_sem.at[1]),
        pltpu.make_async_copy(convw_any, convw, local_sem.at[6]),
        pltpu.make_async_copy(upw_any, upw, local_sem.at[2]),
        pltpu.make_async_copy(spread_any, spread_up, local_sem.at[7]),
        pltpu.make_async_copy(gather_any, gather_z, local_sem.at[8]),
    ]
    start(loads)
    lane = lane_of((64, 128))

    there = jnp.where(occupancy[0] > 0, 1.0, 0.0)
    mf[1, 1] = mm(jnp.broadcast_to(there, (16, 16)).astype(BF), wide_rows[...]).astype(BF)
    keep_ref[...] = mm_t(wide_columns[...], jnp.broadcast_to(there, (128, 16)).astype(BF))

    loads[0].wait()

    def fill_coarse(t, carry):
        x, y = t // 4, t % 4
        own = jnp.where(keep_ref[...] > 0.5, coarse[x, y].astype(F32), 0.0)
        cf[x + 1, y + 1] = own.astype(BF)
        return carry

    lax.fori_loop(0, 16, fill_coarse, 0, unroll=4)
    pl.semaphore_wait(barrier, greeted)
    coarse_copies = halo_copies(cf, cf, halo_send, halo_recv, 0)
    mask_copies = halo_copies(mf, mf, halo_send, halo_recv, 8)
    start(coarse_copies)
    start(mask_copies)

    loads[1].wait()

    def fill_skip(x, carry):
        sf[x + 1, pl.ds(1, 8)] = jnp.swapaxes(skip[:, x], 0, 1)
        return carry

    lax.fori_loop(0, 8, fill_skip, 0, unroll=2)
    skip_copies = halo_copies(sf, sf, halo_send, halo_recv, 16)

    loads[2].wait()

    def fill_cot(x, carry):
        cot_t[x] = jnp.swapaxes(cot[:, x], 0, 1)
        return carry

    lax.fori_loop(0, 8, fill_cot, 0, unroll=2)
    finish(loads[3:7])
    bias[...] = jnp.broadcast_to(conv_bias[...], (128, 64)).T
    for kz in range(3):
        for pair in range(5):
            taps = [(k // 3, k % 3) for k in (2 * pair, 2 * pair + 1) if k < 9]
            fore = [convw[kx, ky, kz] for kx, ky in taps]
            aft = [convw[2 - kx, 2 - ky, 2 - kz] for kx, ky in taps]
            at, col = kz * 64, pair * 128
            wide = 64 * len(taps)
            wc[at : at + 64, col : col + wide] = rows(fore).T
            wb[at : at + 64, col : col + wide] = lanes(aft)
    for sx in range(2):
        for sy in range(2):
            for tx in range(2):
                for ty in range(2):
                    block = upw[2 + sx - 2 * tx, 2 + sy - 2 * ty].reshape(256, 128)
                    at, col = (sx * 2 + sy) * 256, (tx * 2 + ty) * 128
                    wu[at : at + 256, col : col + 128] = block
                    wt[sy, col : col + 128, sx * 256 : sx * 256 + 256] = block.T

    def pair_coarse(i, y):
        ac[i, y] = rows([cf[i, y], cf[i + 2, y]]).T

    def pair_middle(t, carry):
        pair_coarse(1 + t // 4, 1 + t % 4)
        return carry

    def pair_across(t, carry):
        pair_coarse((t // 6) * 3, t % 6)
        return carry

    def pair_along(t, carry):
        pair_coarse(1 + t // 2, (t % 2) * 5)
        return carry

    def join(p, q, taps):
        wide = rows(
            [
                lanes([taps[(s * 4 + kz) * 64 : (s * 4 + kz + 1) * 64] for kz in range(4)])
                for s in range(4)
            ]
        )
        up = mm(wide, spread_up[...])
        for s in range(4):
            for h in range(2):
                ups[2 * p + s // 2 + 4 * h, 2 * q + s % 2] = up[
                    s * 64 : s * 64 + 64, h * 128 : h * 128 + 128
                ]

    def upsample(blocks):
        window = lanes([ac[p : p + 2, q : q + 2].reshape(512, 128) for p, q in blocks])
        taps = mm(wu[...], window).astype(BF)
        for at, (p, q) in enumerate(blocks):
            join(p, q, taps[:, at * 128 : at * 128 + 128])

    start(skip_copies)
    lax.fori_loop(0, 8, pair_middle, 0, unroll=4)
    upsample([(1, 1), (1, 2), (1, 3)])
    finish(coarse_copies)
    clear_outside(cf)
    lax.fori_loop(0, 12, pair_across, 0, unroll=4)
    lax.fori_loop(0, 4, pair_along, 0, unroll=4)
    for p in (0, 2):
        upsample([(p, 0), (p, 1)])
        upsample([(p, 2), (p, 3)])
        upsample([(p, 4), (1, p * 2)])

    finish(mask_copies)
    clear_outside(mf)
    for bx in range(3):
        for by in range(3):
            masks[bx, by] = mf[bx, by].astype(F32)

    def mix(x, y):
        bx = jnp.where(x == 0, 0, jnp.where(x == 9, 2, 1))
        by = jnp.where(y == 0, 0, jnp.where(y == 9, 2, 1))
        value = ups[x, y] + sf[x, y].astype(F32)
        mx[x, y] = jnp.where(masks[bx, by, 0:1, :] > 0.5, value, 0.0).astype(BF)

    def mix_middle(t, carry):
        mix(1 + t // 8, 1 + t % 8)
        return carry

    def mix_across(t, carry):
        mix((t // 8) * 9, 1 + t % 8)
        return carry

    def mix_along(t, carry):
        mix(t // 2, (t % 2) * 9)
        return carry

    lax.fori_loop(0, 64, mix_middle, 0, unroll=4)

    inside = masks[1, 1, 0:1, :] > 0.5

    def conv(i, pair):
        taps = mm(wc[...], conv_window(mx, i, pair))
        for e, y in enumerate(pair):
            for h in range(2):
                at = (e * 2 + h) * 128
                pre = join_taps(taps[:, at : at + 128], lane) + bias[...]
                sig = 1.0 / (1.0 + jnp.exp(-pre))
                feat[i + 4 * h, y] = jnp.where(inside, pre * sig, 0.0).astype(BF)
                slope = sig * (1.0 + pre * (1.0 - sig))
                grad = cot_t[i + 4 * h, y].astype(F32) * slope
                grad = jnp.where(inside, grad, 0.0).astype(BF)
                gpf[i + 4 * h + 1, y + 1] = grad
                wide = grad.astype(F32)
                before = jnp.where(lane == 127, 0.0, pltpu.roll(wide, 127, 1)).astype(BF)
                after = jnp.where(lane == 0, 0.0, pltpu.roll(wide, 1, 1)).astype(BF)
                g3[i, y, :, h * 128 : h * 128 + 128] = rows([before, grad, after])

    def middle(step):
        def run(t, carry):
            y = 1 + (t % 3) * 2
            step(1 + t // 3, (y, y + 1))
            return carry

        lax.fori_loop(0, 6, run, 0, unroll=3)

    def ends_along(step, first, last):
        def run(i, carry):
            step(i, (0, 7))
            return carry

        lax.fori_loop(first, last, run, 0, unroll=last - first)

    def ends_across(step, i):
        def run(t, carry):
            y = 1 + t * 2
            step(i, (y, y + 1))
            return carry

        lax.fori_loop(0, 3, run, 0, unroll=3)

    gp_copies = halo_copies(gpf, gpf, halo_send, halo_recv, 24)
    middle(conv)
    finish(skip_copies)
    lax.fori_loop(0, 16, mix_across, 0, unroll=4)
    lax.fori_loop(0, 20, mix_along, 0, unroll=4)
    ends_along(conv, 0, 4)
    start(gp_copies[0:2])
    start(gp_copies[4:8])
    ends_across(conv, 0)
    ends_across(conv, 3)
    start(gp_copies[2:4])

    gacc[...] = jnp.zeros_like(gacc)

    def kernel_grad(t, carry):
        i, y = t // 2, (t % 2) * 4
        grads = lanes([g3[i, y + j] for j in range(4)])
        for k in range(3):
            cells = lanes(
                [
                    mx[i + 4 * h + k, pl.ds(y + j, 3)].reshape(192, 128)
                    for j in range(4)
                    for h in range(2)
                ]
            )
            gacc[k * 192 : k * 192 + 192, :] += mm_t(cells, grads)
        gacc[576:592, :] += mm_t(jnp.ones((16, 1024), BF), grads)
        return carry

    lax.fori_loop(0, 8, kernel_grad, 0, unroll=4)
    mine[2, 0:C_ROWS] = gacc[:, 0:128].astype(BF)
    mine[2, C_ROWS : 2 * C_ROWS, 0:64] = gacc[:, 128:192].astype(BF)
    mine[2, C_ROWS : 2 * C_ROWS, 64:128] = jnp.zeros((C_ROWS, 64), BF)
    mine[2, 2 * C_ROWS : PIECE] = jnp.zeros((PIECE - 2 * C_ROWS, 128), BF)
    sums = [
        Piece(ring, at, at == 1, mine, got0, got1, got2, acc1, acc2, total, sum_send, sum_recv)
        for at in range(3)
    ]
    even, odd, conv_sum = sums
    conv_sum.step0()

    def back(i, pair):
        taps = mm(wb[...], conv_window(gpf, i, pair))
        for e, y in enumerate(pair):
            both = []
            for h in range(2):
                at = (e * 2 + h) * 128
                grad = join_taps(taps[:, at : at + 128], lane)
                grad = jnp.where(inside, grad, 0.0).astype(BF)
                gs[i + 4 * h, y] = grad
                both.append(grad)
            apart = mm(lanes(both), gather_z[...]).astype(BF)
            for kz in range(4):
                d4[i, y, kz * 64 : kz * 64 + 64, :] = apart[:, kz * 128 : kz * 128 + 128]

    def up_grad(sx, sy):
        spots = [(pi, qi) for pi in range(1 - sx, 3 - sx) for qi in range(1 - sy, 5 - sy)]
        grads = lanes([d4[2 * pi - 1 + sx, 2 * qi - 1 + sy] for pi, qi in spots])
        cells = rows(
            [
                lanes([ac[pi + tx, qi + ty] for pi, qi in spots])
                for tx in range(2)
                for ty in range(2)
            ]
        )
        result = mm_t(grads, cells).astype(BF)
        for tx in range(2):
            for ty in range(2):
                at, col = (tx * 4 + 2 + sy - 2 * ty) * 256, (tx * 2 + ty) * 128
                mine[sx, at : at + 256] = result[:, col : col + 128]

    middle(back)
    finish(gp_copies)
    clear_outside(gpf)
    ends_along(back, 1, 2)
    ends_along(back, 3, 4)
    ends_across(back, 3)
    conv_sum.step1()
    up_grad(0, 0)
    up_grad(0, 1)
    even.step0()
    ends_along(back, 2, 3)
    ends_along(back, 0, 1)
    ends_across(back, 0)
    even.step1()
    up_grad(1, 0)
    up_grad(1, 1)
    odd.step0()
    conv_sum.step2()

    acc[...] = jnp.zeros_like(acc)

    def lower(sy, across):
        if across == 1:
            weight = wt[sy]
            cells = rows([lanes([d4[1 + sx, 2 * q + 1 - sy] for q in range(4)]) for sx in range(2)])
        else:
            sx, i = (1, 0) if across == 0 else (0, 3)
            weight = wt[sy, :, sx * 256 : sx * 256 + 256]
            cells = lanes([d4[i, 2 * q + 1 - sy] for q in range(4)])
        result = mm(weight, cells)
        for tx in range(2):
            for ty in range(2):
                at = (tx * 2 + ty) * 128
                for q in range(4):
                    acc[across + tx, q + ty + 1 - sy] += result[
                        at : at + 128, q * 128 : q * 128 + 128
                    ]

    lower(0, 0)
    lower(1, 0)
    lower(0, 1)
    odd.step1()
    lower(1, 1)
    lower(0, 2)
    lower(1, 2)
    even.step2()

    def turned(i, y):
        return acc[i, y].T

    def fold(y, carry):
        cells = [turned(i, y) for i in range(4)]
        left, right = [c[0:64] for c in cells], [c[64:128] for c in cells]
        folded = [
            left[0],
            left[1],
            left[2] + right[0],
            left[3] + right[1],
            right[2],
            right[3],
        ]
        for x in range(6):
            part[x, y] = folded[x].astype(BF)
        return carry

    lax.fori_loop(0, 6, fold, 0)
    part_copies = halo_copies(part, part_in, halo_send, halo_recv, 32, padding)
    conv_sum.step3()
    odd.step2()

    def turn_feat(x, carry):
        feat_t[:, x] = jnp.swapaxes(feat[x], 0, 1)
        return carry

    lax.fori_loop(0, 8, turn_feat, 0, unroll=2)
    stores = [
        pltpu.make_async_copy(feat_t, feat_any, local_sem.at[3]),
        pltpu.make_async_copy(gs_t, gs_any, local_sem.at[4]),
    ]
    start(stores[0:1])
    even.step3()
    odd.step3()
    start(part_copies)

    def turn_gs(x, carry):
        gs_t[:, x] = jnp.swapaxes(gs[x], 0, 1)
        return carry

    lax.fori_loop(0, 8, turn_gs, 0, unroll=2)
    start(stores[1:2])
    conv_sum.step4()
    even.step4()
    odd.step4()
    stores.append(pltpu.make_async_copy(low, low_any, local_sem.at[9]))
    stores += [
        pltpu.make_async_copy(total.at[at], total_any.at[at], local_sem.at[10 + at])
        for at in range(3)
    ]
    conv_sum.step5()
    even.step5()
    finish(part_copies)
    clear_outside(part_in)
    for x in range(4):
        for y in range(4):
            across = [x + 1] + [0] * (x == 0) + [5] * (x == 3)
            along = [y + 1] + [0] * (y == 0) + [5] * (y == 3)
            value = part[x + 1, y + 1].astype(F32)
            for px in across:
                for py in along:
                    if (px, py) != (x + 1, y + 1):
                        value += part_in[px, py].astype(F32)
            low[x, y] = jnp.where(keep_ref[...] > 0.5, value, 0.0).astype(BF)
    stores[2].start()
    conv_sum.step6()
    stores[5].start()
    even.step6()
    stores[3].start()
    odd.step6()
    stores[4].start()
    finish(stores)


def final_body(
    scale,
    feat,
    gs,
    low,
    total,
    features,
    grad_skip,
    grad_coarse,
    up_any,
    conv,
    bias,
    v0,
    v1,
    v2,
    sums,
    up,
    come_sem,
    go_sem,
):
    def part(at, count):
        return total.at[pl.ds(at, count)], sums.at[pl.ds(at, count)]

    taps = [(2 + sx - 2 * tx, sx * PIECE + tx * HALF) for tx in range(2) for sx in range(2)]
    pieces = [(feat, v0), (gs, v1), (low, v2)]
    pieces += [part(at, HALF) for kx, at in taps]
    pieces += [part(2 * PIECE, C_ROWS), part(2 * PIECE + C_ROWS, C_ROWS)]
    come = [pltpu.make_async_copy(a, b, come_sem.at[n]) for n, (a, b) in enumerate(pieces)]
    start(come)
    go = [(v0, features), (v1, grad_skip), (v2, grad_coarse)]
    go += [(up.at[kx], up_any.at[kx]) for kx, at in taps]
    go = [pltpu.make_async_copy(a, b, go_sem.at[n]) for n, (a, b) in enumerate(go)]
    for n in range(3):
        come[n].wait()
        go[n].start()
    for n, (kx, at) in enumerate(taps):
        come[3 + n].wait()

        def column(t, carry):
            block = sums[pl.ds(pl.multiple_of(at + t * 256, 256), 256)]
            up[kx, t] = (block.astype(F32) * scale).reshape(4, 64, 128)
            return carry

        lax.fori_loop(0, 4, column, 0)
        go[3 + n].start()
    finish(come[7:9])
    for tap in range(9):
        at = 2 * PIECE + tap * 64
        left = sums[at : at + 64].astype(F32) * scale
        right = sums[C_ROWS + at : C_ROWS + at + 64].astype(F32) * scale
        conv[tap // 3, tap % 3, 0] = left[:, 0:64]
        conv[tap // 3, tap % 3, 1] = left[:, 64:128]
        conv[tap // 3, tap % 3, 2] = right[:, 0:64]
    bias[...] = (sums[2 * PIECE + 576 : 2 * PIECE + 592].astype(F32) * scale)[0:1, 64:128]
    finish(go)


def spread_matrix():
    row, column = np.arange(512)[:, None], np.arange(256)[None, :]
    kz, h, j = row // 128, (row // 64) % 2, row % 64
    hit = (h == column // 128) & (column % 128 == 2 * j - 1 + kz)
    return hit.astype(ml_dtypes.bfloat16)


def body(coarse, skip, occupancy, cotangent, up_weight, conv_weight, conv_bias):
    spread_up = spread_matrix()
    wide_rows = np.repeat(np.eye(16), EDGE, axis=1).astype(ml_dtypes.bfloat16)
    wide_columns = np.repeat(np.eye(16), EDGE // 2, axis=0).astype(ml_dtypes.bfloat16)
    vmem, anywhere = pl.BlockSpec(memory_space=pltpu.VMEM), pl.BlockSpec(memory_space=pl.ANY)
    plane = (64, 8, 8, 128)
    feat, gs, low, total = pl.pallas_call(
        main_body,
        out_shape=[shape(plane), shape(plane), shape((4, 4, 64, 128)), shape((3, PIECE, 128))],
        in_specs=[anywhere] * 7 + [vmem] * 4,
        out_specs=[anywhere] * 4,
        scratch_shapes=[
            pltpu.VMEM((4, 4, 64, 128), BF),
            pltpu.VMEM((3, PIECE, 128), BF),
            pltpu.VMEM(plane, BF),
            pltpu.VMEM(plane, BF),
            pltpu.VMEM((4, 4, 4, 64, 128), BF),
            pltpu.VMEM((4, 4, 64, 128), BF),
            pltpu.VMEM((3, 3, 3, 64, 64), BF),
            pltpu.VMEM((512, 256), BF),
            pltpu.VMEM((256, 512), BF),
            pltpu.VMEM((8, 8, 64, 128), BF),
            pltpu.VMEM((8, 8, 64, 128), BF),
            pltpu.VMEM(plane, BF),
            pltpu.VMEM(plane, BF),
            pltpu.SemaphoreType.DMA((13,)),
            pltpu.VMEM((10, 10, 64, 128), BF),
            pltpu.VMEM((6, 6, 64, 128), BF),
            pltpu.VMEM((3, 3, 16, 128), BF),
            pltpu.VMEM((3, 3, 16, 128), F32),
            pltpu.VMEM((64, 128), F32),
            pltpu.VMEM((64, 128), F32),
            pltpu.VMEM((8, 8, 64, 128), BF),
            pltpu.VMEM((192, 576), BF),
            pltpu.VMEM((192, 576), BF),
            pltpu.VMEM((1024, 512), BF),
            pltpu.VMEM((2, 512, 512), BF),
            pltpu.VMEM((4, 6, 128, 128), BF),
            pltpu.VMEM((10, 10, 64, 128), F32),
            pltpu.VMEM((10, 10, 64, 128), BF),
            pltpu.VMEM((10, 10, 64, 128), BF),
            pltpu.VMEM((4, 8, 192, 256), BF),
            pltpu.VMEM((C_ROWS, 192), F32),
            pltpu.VMEM((4, 8, 256, 128), BF),
            pltpu.VMEM((4, 6, 128, 128), F32),
            pltpu.VMEM((6, 6, 64, 128), BF),
            pltpu.VMEM((6, 6, 64, 128), BF),
            pltpu.VMEM((3, PIECE, 128), BF),
            pltpu.VMEM((3, HALF, 128), BF),
            pltpu.VMEM((3, 3, QUARTER, 128), BF),
            pltpu.VMEM((3, 15, CHUNK, 128), BF),
            pltpu.VMEM((3, QUARTER, 128), BF),
            pltpu.VMEM((3, QUARTER, 128), BF),
            pltpu.SemaphoreType.DMA((40,)),
            pltpu.SemaphoreType.DMA((40,)),
            pltpu.SemaphoreType.DMA((3 * 42,)),
            pltpu.SemaphoreType.DMA((3 * 42,)),
        ],
        compiler_params=pltpu.CompilerParams(
            vmem_limit_bytes=LIMIT, collective_id=1, has_side_effects=True
        ),
    )(
        skip,
        cotangent,
        jnp.transpose(up_weight, (0, 1, 2, 4, 3)),
        jnp.transpose(coarse, (1, 2, 3, 0)),
        conv_weight,
        spread_up,
        np.ascontiguousarray(spread_up.T),
        conv_bias[None],
        occupancy[0],
        wide_rows,
        wide_columns,
    )
    cells = 8192 * lax.axis_size("gx") * lax.axis_size("gy")
    features, grad_skip, low, up, grad_conv, bias = pl.pallas_call(
        functools.partial(final_body, float(cells) ** -0.5),
        out_shape=[
            shape(plane),
            shape(plane),
            shape((4, 4, 64, 128)),
            shape((4, 4, 4, 64, 128), F32),
            shape((3, 3, 3, 64, 64), F32),
            shape((1, 64), F32),
        ],
        in_specs=[anywhere] * 4,
        out_specs=[anywhere] * 4 + [vmem] * 2,
        scratch_shapes=[
            pltpu.VMEM(plane, BF),
            pltpu.VMEM(plane, BF),
            pltpu.VMEM((4, 4, 64, 128), BF),
            pltpu.VMEM((3 * PIECE, 128), BF),
            pltpu.VMEM((4, 4, 4, 64, 128), F32),
            pltpu.SemaphoreType.DMA((9,)),
            pltpu.SemaphoreType.DMA((7,)),
        ],
        compiler_params=pltpu.CompilerParams(vmem_limit_bytes=LIMIT),
    )(feat, gs, low, total.reshape(3 * PIECE, 128))
    grad_coarse = jnp.transpose(low, (3, 0, 1, 2))
    grad_up = jnp.transpose(up, (0, 1, 2, 4, 3))
    return features, grad_skip, grad_coarse, grad_up, grad_conv, bias[0]


def solution(mesh):
    field = P(None, "gx", "gy", None)
    return jax.shard_map(
        body,
        mesh=mesh,
        in_specs=(field, field, P("gx", "gy", None), field, P(), P(), P()),
        out_specs=(field, field, field, P(), P(), P()),
        check_vma=False,
    )
```

```python
import functools

import jax
import jax.numpy as jnp
import ml_dtypes
import numpy as np
from jax import lax
from jax.experimental import pallas as pl
from jax.experimental.pallas import tpu as pltpu
from jax.sharding import PartitionSpec as P

BF = jnp.bfloat16
F32 = jnp.float32
EDGE = 8
MESH = pl.DeviceIdType.MESH
LIMIT = 56 * 2**20

C_ROWS = 592
PIECE = 2048
HALF, QUARTER, CHUNK = PIECE // 2, PIECE // 8, PIECE // 128


def mm(a, b):
    return lax.dot_general(a, b, (((1,), (0,)), ((), ())), preferred_element_type=F32)


def mm_t(a, b):
    return lax.dot_general(a, b, (((1,), (1,)), ((), ())), preferred_element_type=F32)


def lanes(parts):
    return jnp.concatenate(parts, axis=1)


def rows(parts):
    return jnp.concatenate(parts, axis=0)


def shape(dims, kind=BF):
    return jax.ShapeDtypeStruct(dims, kind)


AROUND = [(0, 1), (0, -1), (1, 0), (-1, 0), (1, 1), (1, -1), (-1, 1), (-1, -1)]


def neighbour(dx, dy):
    nx, ny = lax.axis_size("gx"), lax.axis_size("gy")
    gx, gy = lax.axis_index("gx"), lax.axis_index("gy")
    return lax.rem(gx + (dx + nx), nx), lax.rem(gy + (dy + ny), ny)


def outer(step, count):
    if step == 0:
        return pl.ds(1, count), pl.ds(1, count)
    if step > 0:
        return pl.ds(count, 1), pl.ds(0, 1)
    return pl.ds(1, 1), pl.ds(count + 1, 1)


def padding(step, count):
    if step == 0:
        return pl.ds(1, count), pl.ds(1, count)
    if step > 0:
        return pl.ds(count + 1, 1), pl.ds(0, 1)
    return pl.ds(0, 1), pl.ds(count + 1, 1)


def halo_copies(source, target, send, recv, first, place=outer):
    across, along = source.shape[0] - 2, source.shape[1] - 2
    copies = []
    for at, (dx, dy) in enumerate(AROUND):
        sx, tx = place(dx, across)
        sy, ty = place(dy, along)
        copies.append(
            pltpu.make_async_remote_copy(
                src_ref=source.at[sx, sy],
                dst_ref=target.at[tx, ty],
                send_sem=send.at[first + at],
                recv_sem=recv.at[first + at],
                device_id=neighbour(dx, dy),
                device_id_type=MESH,
            )
        )
    return copies


def start(copies):
    for copy in copies:
        copy.start()


def finish(copies):
    for copy in copies:
        copy.wait()


def clear_across(field):
    across, along = field.shape[0], field.shape[1]
    row = jnp.zeros((1, along - 2) + field.shape[2:], field.dtype)

    @pl.when(lax.axis_index("gx") == 0)
    def _():
        field[0:1, 1 : along - 1] = row

    @pl.when(lax.axis_index("gx") == lax.axis_size("gx") - 1)
    def _():
        field[across - 1 : across, 1 : along - 1] = row


def clear_outside(field):
    across, along = field.shape[0], field.shape[1]
    nx, ny = lax.axis_size("gx"), lax.axis_size("gy")
    gx, gy = lax.axis_index("gx"), lax.axis_index("gy")
    row = jnp.zeros((1,) + field.shape[1:], field.dtype)
    column = jnp.zeros((across, 1) + field.shape[2:], field.dtype)

    @pl.when(gx == 0)
    def _():
        field[0:1] = row

    @pl.when(gx == nx - 1)
    def _():
        field[across - 1 : across] = row

    @pl.when(gy == 0)
    def _():
        field[:, 0:1] = column

    @pl.when(gy == ny - 1)
    def _():
        field[:, along - 1 : along] = column


class Ring:
    def __init__(self):
        gx, gy = lax.axis_index("gx"), lax.axis_index("gy")
        self.core = lax.rem(gx, 2)
        self.x, self.y = gx // 4, gy // 2
        self.z = lax.rem(gy, 2) * 2 + lax.rem(gx // 2, 2)
        self.first = jnp.where(self.core == 0, self.x, self.y)
        self.second = jnp.where(self.core == 0, self.y, self.x)
        self.place = self.second * 4 + self.z
        self.twin = self.device(self.x, self.y, self.z, 1 - self.core)

    def device(self, x, y, z, core):
        return x * 4 + lax.rem(z, 2) * 2 + core, y * 2 + z // 2

    def along_first(self, step):
        other = lax.rem(self.first + step, 4)
        x = jnp.where(self.core == 0, other, self.x)
        y = jnp.where(self.core == 0, self.y, other)
        return other, self.device(x, y, self.z, self.core)

    def in_plane(self, step):
        a, b = lax.rem(self.second + step // 4, 4), lax.rem(self.z + step % 4, 4)
        x = jnp.where(self.core == 0, self.x, a)
        y = jnp.where(self.core == 0, a, self.y)
        return a * 4 + b, self.device(x, y, b, self.core)

    def across_first(self, step):
        x = jnp.where(self.core == 0, self.x, lax.rem(self.x + step, 4))
        y = jnp.where(self.core == 0, lax.rem(self.y + step, 4), self.y)
        return self.device(x, y, self.z, 1 - self.core)

    def beside_first(self, step):
        other = lax.rem(self.first + step, 4)
        x = jnp.where(self.core == 0, other, self.x)
        y = jnp.where(self.core == 0, self.y, other)
        return self.device(x, y, self.z, 1 - self.core)

    def greet(self, barrier):
        partners = [self.twin]
        partners += [self.along_first(step)[1] for step in range(1, 4)]
        partners += [self.across_first(step) for step in range(1, 4)]
        partners += [self.in_plane(step)[1] for step in range(1, 16)]
        for partner in partners:
            pl.semaphore_signal(barrier, inc=1, device_id=partner, device_id_type=MESH)
        return len(partners)


def span(begin, count):
    return pl.ds(pl.multiple_of(begin, 16), count)


class Piece:
    def __init__(self, ring, index, wide, mine, got0, got1, got2, acc1, acc2, out, send, recv):
        self.ring, self.base, self.wide = ring, index * 42, wide
        self.mine, self.got0, self.got1 = mine.at[index], got0.at[index], got1.at[index]
        self.got2, self.acc1, self.acc2 = got2.at[index], acc1.at[index], acc2.at[index]
        self.out, self.send, self.recv = out.at[index], send, recv
        self.flying = []

    def remote(self, src, dst, at, to):
        return pltpu.make_async_remote_copy(
            src_ref=src,
            dst_ref=dst,
            send_sem=self.send.at[self.base + at],
            recv_sem=self.recv.at[self.base + at],
            device_id=to,
            device_id_type=MESH,
        )

    def launch(self, copies):
        start(copies)
        self.flying = copies

    def step0(self):
        ring = self.ring
        theirs = self.mine.at[span((1 - ring.core) * HALF, HALF)]
        self.launch([self.remote(theirs, self.got0, 0, ring.twin)])

    def step1(self):
        ring = self.ring
        finish(self.flying)

        def add(t, carry):
            own = self.mine[span(ring.core * HALF + t * 256, 256)].astype(F32)
            at = span(t * 256, 256)
            self.got0[at] = (own + self.got0[at].astype(F32)).astype(BF)
            return carry

        lax.fori_loop(0, HALF // 256, add, 0)
        copies = []
        for step in range(1, 4):
            other, to = ring.along_first(step)
            theirs = self.got0.at[span(other * QUARTER, QUARTER)]
            copies.append(self.remote(theirs, self.got1.at[step - 1], step, to))
        self.launch(copies)

    def step2(self):
        ring = self.ring
        finish(self.flying)
        total = self.got0[span(ring.first * QUARTER, QUARTER)].astype(F32)
        for step in range(3):
            total += self.got1[step].astype(F32)
        self.acc1[...] = total.astype(BF)
        copies = []
        for step in range(1, 16):
            other, to = ring.in_plane(step)
            theirs = self.acc1.at[span(other * CHUNK, CHUNK)]
            copies.append(self.remote(theirs, self.got2.at[step - 1], 3 + step, to))
        self.launch(copies)

    def step3(self):
        ring = self.ring
        finish(self.flying)
        total = self.acc1[span(ring.place * CHUNK, CHUNK)].astype(F32)
        for step in range(15):
            total += self.got2[step].astype(F32)
        own = span(ring.place * CHUNK, CHUNK)
        self.acc2[own] = total.astype(BF)
        copies = []
        for step in range(1, 16):
            other, to = ring.in_plane(step)
            copies.append(self.remote(self.acc2.at[own], self.acc2.at[own], 18 + step, to))
        self.launch(copies)

    def step4(self):
        ring = self.ring
        finish(self.flying)
        own = span(ring.core * HALF + ring.first * QUARTER, QUARTER)
        copies = []
        for step in range(1, 4):
            other, to = ring.along_first(step)
            copies.append(self.remote(self.acc2, self.out.at[own], 33 + step, to))
            if self.wide:
                to = ring.beside_first(step)
                copies.append(self.remote(self.acc2, self.out.at[own], 36 + step, to))
        if self.wide:
            copies.append(self.remote(self.acc2, self.out.at[own], 40, ring.twin))
        self.launch(copies)
        self.out[own] = self.acc2[...]

    def step5(self):
        ring = self.ring
        finish(self.flying)
        own = self.out.at[span(ring.core * HALF, HALF)]
        self.launch([self.remote(own, own, 37, ring.twin)])

    def step6(self):
        finish(self.flying)


def lane_of(dims):
    return lax.broadcasted_iota(jnp.int32, dims, len(dims) - 1)


def conv_window(field, i, pair):
    return rows(
        [
            lanes(
                [
                    field[i + 4 * h + k, pl.ds(y, 3)].reshape(192, 128)
                    for y in pair
                    for h in range(2)
                ]
            )
            for k in range(3)
        ]
    )


def join_taps(taps, lane):
    back = jnp.where(lane == 0, 0.0, pltpu.roll(taps[0:64], 1, 1))
    ahead = jnp.where(lane == 127, 0.0, pltpu.roll(taps[128:192], 127, 1))
    return taps[64:128] + back + ahead


def main_body(
    skip_any,
    cot_any,
    upw_any,
    coarse_any,
    convw_any,
    spread_any,
    gather_any,
    conv_bias,
    occupancy,
    wide_rows,
    wide_columns,
    feat_any,
    gs_any,
    low_any,
    total_any,
    low,
    total,
    skip,
    cot,
    upw,
    coarse,
    convw,
    spread_up,
    gather_z,
    feat,
    gs,
    feat_t,
    gs_t,
    local_sem,
    sf,
    cf,
    mf,
    masks,
    keep_ref,
    bias,
    cot_t,
    wc,
    wb,
    wu,
    wt,
    ac,
    ups,
    mx,
    gpf,
    g3,
    gacc,
    d4,
    acc,
    part,
    part_in,
    mine,
    got0,
    got1,
    got2,
    acc1,
    acc2,
    halo_send,
    halo_recv,
    sum_send,
    sum_recv,
):
    ring = Ring()
    barrier = pltpu.get_barrier_semaphore()
    for dx, dy in AROUND:
        pl.semaphore_signal(barrier, inc=1, device_id=neighbour(dx, dy), device_id_type=MESH)
    greeted = ring.greet(barrier) + len(AROUND)
    loads = [
        pltpu.make_async_copy(coarse_any, coarse, local_sem.at[5]),
        pltpu.make_async_copy(skip_any, skip, local_sem.at[0]),
        pltpu.make_async_copy(cot_any, cot, local_sem.at[1]),
        pltpu.make_async_copy(convw_any, convw, local_sem.at[6]),
        pltpu.make_async_copy(upw_any, upw, local_sem.at[2]),
        pltpu.make_async_copy(spread_any, spread_up, local_sem.at[7]),
        pltpu.make_async_copy(gather_any, gather_z, local_sem.at[8]),
    ]
    start(loads)
    lane = lane_of((64, 128))

    there = jnp.where(occupancy[0] > 0, 1.0, 0.0)
    mf[1, 1] = mm(jnp.broadcast_to(there, (16, 16)).astype(BF), wide_rows[...]).astype(BF)
    keep_ref[...] = mm_t(wide_columns[...], jnp.broadcast_to(there, (128, 16)).astype(BF))

    loads[0].wait()

    def fill_coarse(t, carry):
        x, y = t // 4, t % 4
        own = jnp.where(keep_ref[...] > 0.5, coarse[x, y].astype(F32), 0.0)
        cf[x + 1, y + 1] = own.astype(BF)
        return carry

    lax.fori_loop(0, 16, fill_coarse, 0, unroll=4)
    pl.semaphore_wait(barrier, greeted)
    coarse_copies = halo_copies(cf, cf, halo_send, halo_recv, 0)
    mask_copies = halo_copies(mf, mf, halo_send, halo_recv, 8)
    start(coarse_copies)
    start(mask_copies)

    loads[1].wait()

    def fill_skip(x, carry):
        sf[x + 1, pl.ds(1, 8)] = jnp.swapaxes(skip[:, x], 0, 1)
        return carry

    lax.fori_loop(0, 8, fill_skip, 0, unroll=2)
    skip_copies = halo_copies(sf, sf, halo_send, halo_recv, 16)

    loads[2].wait()

    def fill_cot(x, carry):
        cot_t[x] = jnp.swapaxes(cot[:, x], 0, 1)
        return carry

    lax.fori_loop(0, 8, fill_cot, 0, unroll=2)
    finish(loads[3:7])
    bias[...] = jnp.broadcast_to(conv_bias[...], (128, 64)).T
    for kz in range(3):
        for pair in range(5):
            taps = [(k // 3, k % 3) for k in (2 * pair, 2 * pair + 1) if k < 9]
            fore = [convw[kx, ky, kz] for kx, ky in taps]
            aft = [convw[2 - kx, 2 - ky, 2 - kz] for kx, ky in taps]
            at, col = kz * 64, pair * 128
            wide = 64 * len(taps)
            wc[at : at + 64, col : col + wide] = rows(fore).T
            wb[at : at + 64, col : col + wide] = lanes(aft)
    for sx in range(2):
        for sy in range(2):
            for tx in range(2):
                for ty in range(2):
                    block = upw[2 + sx - 2 * tx, 2 + sy - 2 * ty].reshape(256, 128)
                    at, col = (sx * 2 + sy) * 256, (tx * 2 + ty) * 128
                    wu[at : at + 256, col : col + 128] = block
                    wt[sy, col : col + 128, sx * 256 : sx * 256 + 256] = block.T

    def pair_coarse(i, y):
        ac[i, y] = rows([cf[i, y], cf[i + 2, y]]).T

    def pair_middle(t, carry):
        pair_coarse(1 + t // 4, 1 + t % 4)
        return carry

    def pair_across(t, carry):
        pair_coarse((t // 6) * 3, t % 6)
        return carry

    def pair_along(t, carry):
        pair_coarse(1 + t // 2, (t % 2) * 5)
        return carry

    def join(p, q, taps):
        wide = rows(
            [
                lanes([taps[(s * 4 + kz) * 64 : (s * 4 + kz + 1) * 64] for kz in range(4)])
                for s in range(4)
            ]
        )
        up = mm(wide, spread_up[...])
        for s in range(4):
            for h in range(2):
                ups[2 * p + s // 2 + 4 * h, 2 * q + s % 2] = up[
                    s * 64 : s * 64 + 64, h * 128 : h * 128 + 128
                ]

    def upsample(blocks):
        window = lanes([ac[p : p + 2, q : q + 2].reshape(512, 128) for p, q in blocks])
        taps = mm(wu[...], window).astype(BF)
        for at, (p, q) in enumerate(blocks):
            join(p, q, taps[:, at * 128 : at * 128 + 128])

    start(skip_copies)
    lax.fori_loop(0, 8, pair_middle, 0, unroll=4)
    upsample([(1, 1), (1, 2), (1, 3)])
    finish(coarse_copies)
    clear_outside(cf)
    lax.fori_loop(0, 12, pair_across, 0, unroll=4)
    lax.fori_loop(0, 4, pair_along, 0, unroll=4)
    for p in (0, 2):
        upsample([(p, 0), (p, 1)])
        upsample([(p, 2), (p, 3)])
        upsample([(p, 4), (1, p * 2)])

    finish(mask_copies)
    clear_outside(mf)
    for bx in range(3):
        for by in range(3):
            masks[bx, by] = mf[bx, by].astype(F32)

    def mix(x, y):
        bx = jnp.where(x == 0, 0, jnp.where(x == 9, 2, 1))
        by = jnp.where(y == 0, 0, jnp.where(y == 9, 2, 1))
        value = ups[x, y] + sf[x, y].astype(F32)
        mx[x, y] = jnp.where(masks[bx, by, 0:1, :] > 0.5, value, 0.0).astype(BF)

    def mix_middle(t, carry):
        mix(1 + t // 8, 1 + t % 8)
        return carry

    def mix_across(t, carry):
        mix((t // 8) * 9, 1 + t % 8)
        return carry

    def mix_along(t, carry):
        mix(t // 2, (t % 2) * 9)
        return carry

    lax.fori_loop(0, 64, mix_middle, 0, unroll=4)

    inside = masks[1, 1, 0:1, :] > 0.5

    def conv(i, pair):
        taps = mm(wc[...], conv_window(mx, i, pair))
        for e, y in enumerate(pair):
            for h in range(2):
                at = (e * 2 + h) * 128
                pre = join_taps(taps[:, at : at + 128], lane) + bias[...]
                sig = 1.0 / (1.0 + jnp.exp(-pre))
                feat[i + 4 * h, y] = jnp.where(inside, pre * sig, 0.0).astype(BF)
                slope = sig * (1.0 + pre * (1.0 - sig))
                grad = cot_t[i + 4 * h, y].astype(F32) * slope
                grad = jnp.where(inside, grad, 0.0).astype(BF)
                gpf[i + 4 * h + 1, y + 1] = grad
                wide = grad.astype(F32)
                before = jnp.where(lane == 127, 0.0, pltpu.roll(wide, 127, 1)).astype(BF)
                after = jnp.where(lane == 0, 0.0, pltpu.roll(wide, 1, 1)).astype(BF)
                g3[i, y, :, h * 128 : h * 128 + 128] = rows([before, grad, after])

    def middle(step):
        def run(t, carry):
            y = 1 + (t % 3) * 2
            step(1 + t // 3, (y, y + 1))
            return carry

        lax.fori_loop(0, 6, run, 0, unroll=3)

    def ends_along(step, first, last):
        def run(i, carry):
            step(i, (0, 7))
            return carry

        lax.fori_loop(first, last, run, 0, unroll=last - first)

    def ends_across(step, i):
        def run(t, carry):
            y = 1 + t * 2
            step(i, (y, y + 1))
            return carry

        lax.fori_loop(0, 3, run, 0, unroll=3)

    gp_copies = halo_copies(gpf, gpf, halo_send, halo_recv, 24)
    middle(conv)
    finish(skip_copies)
    lax.fori_loop(0, 16, mix_across, 0, unroll=4)
    lax.fori_loop(0, 20, mix_along, 0, unroll=4)
    ends_along(conv, 0, 4)
    start(gp_copies[0:2])
    start(gp_copies[4:8])
    ends_across(conv, 0)
    ends_across(conv, 3)
    start(gp_copies[2:4])

    gacc[...] = jnp.zeros_like(gacc)

    def kernel_grad(t, carry):
        i, y = t // 2, (t % 2) * 4
        grads = lanes([g3[i, y + j] for j in range(4)])
        for k in range(3):
            cells = lanes(
                [
                    mx[i + 4 * h + k, pl.ds(y + j, 3)].reshape(192, 128)
                    for j in range(4)
                    for h in range(2)
                ]
            )
            gacc[k * 192 : k * 192 + 192, :] += mm_t(cells, grads)
        gacc[576:592, :] += mm_t(jnp.ones((16, 1024), BF), grads)
        return carry

    lax.fori_loop(0, 8, kernel_grad, 0, unroll=4)
    mine[2, 0:C_ROWS] = gacc[:, 0:128].astype(BF)
    mine[2, C_ROWS : 2 * C_ROWS, 0:64] = gacc[:, 128:192].astype(BF)
    mine[2, C_ROWS : 2 * C_ROWS, 64:128] = jnp.zeros((C_ROWS, 64), BF)
    mine[2, 2 * C_ROWS : PIECE] = jnp.zeros((PIECE - 2 * C_ROWS, 128), BF)
    sums = [
        Piece(ring, at, at == 1, mine, got0, got1, got2, acc1, acc2, total, sum_send, sum_recv)
        for at in range(3)
    ]
    even, odd, conv_sum = sums
    conv_sum.step0()

    def back(i, pair):
        taps = mm(wb[...], conv_window(gpf, i, pair))
        for e, y in enumerate(pair):
            both = []
            for h in range(2):
                at = (e * 2 + h) * 128
                grad = join_taps(taps[:, at : at + 128], lane)
                grad = jnp.where(inside, grad, 0.0).astype(BF)
                gs[i + 4 * h, y] = grad
                both.append(grad)
            apart = mm(lanes(both), gather_z[...]).astype(BF)
            for kz in range(4):
                d4[i, y, kz * 64 : kz * 64 + 64, :] = apart[:, kz * 128 : kz * 128 + 128]

    def up_grad(sx, sy):
        spots = [(pi, qi) for pi in range(1 - sx, 3 - sx) for qi in range(1 - sy, 5 - sy)]
        grads = lanes([d4[2 * pi - 1 + sx, 2 * qi - 1 + sy] for pi, qi in spots])
        cells = rows(
            [
                lanes([ac[pi + tx, qi + ty] for pi, qi in spots])
                for tx in range(2)
                for ty in range(2)
            ]
        )
        result = mm_t(grads, cells).astype(BF)
        for tx in range(2):
            for ty in range(2):
                at, col = (tx * 4 + 2 + sy - 2 * ty) * 256, (tx * 2 + ty) * 128
                mine[sx, at : at + 256] = result[:, col : col + 128]

    middle(back)
    finish(gp_copies)
    clear_outside(gpf)
    ends_along(back, 1, 2)
    ends_along(back, 3, 4)
    ends_across(back, 3)
    conv_sum.step1()
    up_grad(0, 0)
    up_grad(0, 1)
    even.step0()
    ends_along(back, 2, 3)
    ends_along(back, 0, 1)
    ends_across(back, 0)
    even.step1()
    up_grad(1, 0)
    up_grad(1, 1)
    odd.step0()
    conv_sum.step2()

    acc[...] = jnp.zeros_like(acc)

    def lower(sy, across):
        if across == 1:
            weight = wt[sy]
            cells = rows([lanes([d4[1 + sx, 2 * q + 1 - sy] for q in range(4)]) for sx in range(2)])
        else:
            sx, i = (1, 0) if across == 0 else (0, 3)
            weight = wt[sy, :, sx * 256 : sx * 256 + 256]
            cells = lanes([d4[i, 2 * q + 1 - sy] for q in range(4)])
        result = mm(weight, cells)
        for tx in range(2):
            for ty in range(2):
                at = (tx * 2 + ty) * 128
                for q in range(4):
                    acc[across + tx, q + ty + 1 - sy] += result[
                        at : at + 128, q * 128 : q * 128 + 128
                    ]

    lower(0, 0)
    lower(1, 0)
    lower(0, 1)
    odd.step1()
    lower(1, 1)
    lower(0, 2)
    lower(1, 2)
    even.step2()

    def turned(i, y):
        return acc[i, y].T

    def fold(y, carry):
        cells = [turned(i, y) for i in range(4)]
        left, right = [c[0:64] for c in cells], [c[64:128] for c in cells]
        folded = [
            left[0],
            left[1],
            left[2] + right[0],
            left[3] + right[1],
            right[2],
            right[3],
        ]
        for x in range(6):
            part[x, y] = folded[x].astype(BF)
        return carry

    lax.fori_loop(0, 6, fold, 0)
    part_copies = halo_copies(part, part_in, halo_send, halo_recv, 32, padding)
    conv_sum.step3()
    odd.step2()

    def turn_feat(x, carry):
        feat_t[:, x] = jnp.swapaxes(feat[x], 0, 1)
        return carry

    lax.fori_loop(0, 8, turn_feat, 0, unroll=2)
    stores = [
        pltpu.make_async_copy(feat_t, feat_any, local_sem.at[3]),
        pltpu.make_async_copy(gs_t, gs_any, local_sem.at[4]),
    ]
    start(stores[0:1])
    even.step3()
    odd.step3()
    conv_sum.step4()
    start(part_copies)

    def turn_gs(x, carry):
        gs_t[:, x] = jnp.swapaxes(gs[x], 0, 1)
        return carry

    lax.fori_loop(0, 8, turn_gs, 0, unroll=2)
    start(stores[1:2])
    conv_sum.step5()
    even.step4()
    odd.step4()
    stores.append(pltpu.make_async_copy(low, low_any, local_sem.at[9]))
    stores += [
        pltpu.make_async_copy(total.at[at], total_any.at[at], local_sem.at[10 + at])
        for at in range(3)
    ]
    even.step5()
    finish(part_copies)
    clear_outside(part_in)
    for x in range(4):
        for y in range(4):
            across = [x + 1] + [0] * (x == 0) + [5] * (x == 3)
            along = [y + 1] + [0] * (y == 0) + [5] * (y == 3)
            value = part[x + 1, y + 1].astype(F32)
            for px in across:
                for py in along:
                    if (px, py) != (x + 1, y + 1):
                        value += part_in[px, py].astype(F32)
            low[x, y] = jnp.where(keep_ref[...] > 0.5, value, 0.0).astype(BF)
    stores[2].start()
    conv_sum.step6()
    stores[5].start()
    even.step6()
    stores[3].start()
    odd.step6()
    stores[4].start()
    finish(stores)


def final_body(
    scale,
    feat,
    gs,
    low,
    total,
    features,
    grad_skip,
    grad_coarse,
    up_any,
    conv,
    bias,
    v0,
    v1,
    v2,
    sums,
    up,
    come_sem,
    go_sem,
):
    def part(at, count):
        return total.at[pl.ds(at, count)], sums.at[pl.ds(at, count)]

    taps = [(2 + sx - 2 * tx, sx * PIECE + tx * HALF) for tx in range(2) for sx in range(2)]
    pieces = [(feat, v0), (gs, v1), (low, v2)]
    pieces += [part(at, HALF) for kx, at in taps]
    pieces += [part(2 * PIECE, C_ROWS), part(2 * PIECE + C_ROWS, C_ROWS)]
    come = [pltpu.make_async_copy(a, b, come_sem.at[n]) for n, (a, b) in enumerate(pieces)]
    start(come)
    go = [(v0, features), (v1, grad_skip), (v2, grad_coarse)]
    go += [(up.at[kx], up_any.at[kx]) for kx, at in taps]
    go = [pltpu.make_async_copy(a, b, go_sem.at[n]) for n, (a, b) in enumerate(go)]
    for n in range(3):
        come[n].wait()
        go[n].start()
    for n, (kx, at) in enumerate(taps):
        come[3 + n].wait()

        def column(t, carry):
            block = sums[pl.ds(pl.multiple_of(at + t * 256, 256), 256)]
            up[kx, t] = (block.astype(F32) * scale).reshape(4, 64, 128)
            return carry

        lax.fori_loop(0, 4, column, 0)
        go[3 + n].start()
    finish(come[7:9])
    for tap in range(9):
        at = 2 * PIECE + tap * 64
        left = sums[at : at + 64].astype(F32) * scale
        right = sums[C_ROWS + at : C_ROWS + at + 64].astype(F32) * scale
        conv[tap // 3, tap % 3, 0] = left[:, 0:64]
        conv[tap // 3, tap % 3, 1] = left[:, 64:128]
        conv[tap // 3, tap % 3, 2] = right[:, 0:64]
    bias[...] = (sums[2 * PIECE + 576 : 2 * PIECE + 592].astype(F32) * scale)[0:1, 64:128]
    finish(go)


def spread_matrix():
    row, column = np.arange(512)[:, None], np.arange(256)[None, :]
    kz, h, j = row // 128, (row // 64) % 2, row % 64
    hit = (h == column // 128) & (column % 128 == 2 * j - 1 + kz)
    return hit.astype(ml_dtypes.bfloat16)


def body(coarse, skip, occupancy, cotangent, up_weight, conv_weight, conv_bias):
    spread_up = spread_matrix()
    wide_rows = np.repeat(np.eye(16), EDGE, axis=1).astype(ml_dtypes.bfloat16)
    wide_columns = np.repeat(np.eye(16), EDGE // 2, axis=0).astype(ml_dtypes.bfloat16)
    vmem, anywhere = pl.BlockSpec(memory_space=pltpu.VMEM), pl.BlockSpec(memory_space=pl.ANY)
    plane = (64, 8, 8, 128)
    feat, gs, low, total = pl.pallas_call(
        main_body,
        out_shape=[shape(plane), shape(plane), shape((4, 4, 64, 128)), shape((3, PIECE, 128))],
        in_specs=[anywhere] * 7 + [vmem] * 4,
        out_specs=[anywhere] * 4,
        scratch_shapes=[
            pltpu.VMEM((4, 4, 64, 128), BF),
            pltpu.VMEM((3, PIECE, 128), BF),
            pltpu.VMEM(plane, BF),
            pltpu.VMEM(plane, BF),
            pltpu.VMEM((4, 4, 4, 64, 128), BF),
            pltpu.VMEM((4, 4, 64, 128), BF),
            pltpu.VMEM((3, 3, 3, 64, 64), BF),
            pltpu.VMEM((512, 256), BF),
            pltpu.VMEM((256, 512), BF),
            pltpu.VMEM((8, 8, 64, 128), BF),
            pltpu.VMEM((8, 8, 64, 128), BF),
            pltpu.VMEM(plane, BF),
            pltpu.VMEM(plane, BF),
            pltpu.SemaphoreType.DMA((13,)),
            pltpu.VMEM((10, 10, 64, 128), BF),
            pltpu.VMEM((6, 6, 64, 128), BF),
            pltpu.VMEM((3, 3, 16, 128), BF),
            pltpu.VMEM((3, 3, 16, 128), F32),
            pltpu.VMEM((64, 128), F32),
            pltpu.VMEM((64, 128), F32),
            pltpu.VMEM((8, 8, 64, 128), BF),
            pltpu.VMEM((192, 576), BF),
            pltpu.VMEM((192, 576), BF),
            pltpu.VMEM((1024, 512), BF),
            pltpu.VMEM((2, 512, 512), BF),
            pltpu.VMEM((4, 6, 128, 128), BF),
            pltpu.VMEM((10, 10, 64, 128), F32),
            pltpu.VMEM((10, 10, 64, 128), BF),
            pltpu.VMEM((10, 10, 64, 128), BF),
            pltpu.VMEM((4, 8, 192, 256), BF),
            pltpu.VMEM((C_ROWS, 192), F32),
            pltpu.VMEM((4, 8, 256, 128), BF),
            pltpu.VMEM((4, 6, 128, 128), F32),
            pltpu.VMEM((6, 6, 64, 128), BF),
            pltpu.VMEM((6, 6, 64, 128), BF),
            pltpu.VMEM((3, PIECE, 128), BF),
            pltpu.VMEM((3, HALF, 128), BF),
            pltpu.VMEM((3, 3, QUARTER, 128), BF),
            pltpu.VMEM((3, 15, CHUNK, 128), BF),
            pltpu.VMEM((3, QUARTER, 128), BF),
            pltpu.VMEM((3, QUARTER, 128), BF),
            pltpu.SemaphoreType.DMA((40,)),
            pltpu.SemaphoreType.DMA((40,)),
            pltpu.SemaphoreType.DMA((3 * 42,)),
            pltpu.SemaphoreType.DMA((3 * 42,)),
        ],
        compiler_params=pltpu.CompilerParams(
            vmem_limit_bytes=LIMIT, collective_id=1, has_side_effects=True
        ),
    )(
        skip,
        cotangent,
        jnp.transpose(up_weight, (0, 1, 2, 4, 3)),
        jnp.transpose(coarse, (1, 2, 3, 0)),
        conv_weight,
        spread_up,
        np.ascontiguousarray(spread_up.T),
        conv_bias[None],
        occupancy[0],
        wide_rows,
        wide_columns,
    )
    cells = 8192 * lax.axis_size("gx") * lax.axis_size("gy")
    features, grad_skip, low, up, grad_conv, bias = pl.pallas_call(
        functools.partial(final_body, float(cells) ** -0.5),
        out_shape=[
            shape(plane),
            shape(plane),
            shape((4, 4, 64, 128)),
            shape((4, 4, 4, 64, 128), F32),
            shape((3, 3, 3, 64, 64), F32),
            shape((1, 64), F32),
        ],
        in_specs=[anywhere] * 4,
        out_specs=[anywhere] * 4 + [vmem] * 2,
        scratch_shapes=[
            pltpu.VMEM(plane, BF),
            pltpu.VMEM(plane, BF),
            pltpu.VMEM((4, 4, 64, 128), BF),
            pltpu.VMEM((3 * PIECE, 128), BF),
            pltpu.VMEM((4, 4, 4, 64, 128), F32),
            pltpu.SemaphoreType.DMA((9,)),
            pltpu.SemaphoreType.DMA((7,)),
        ],
        compiler_params=pltpu.CompilerParams(vmem_limit_bytes=LIMIT),
    )(feat, gs, low, total.reshape(3 * PIECE, 128))
    grad_coarse = jnp.transpose(low, (3, 0, 1, 2))
    grad_up = jnp.transpose(up, (0, 1, 2, 4, 3))
    return features, grad_skip, grad_coarse, grad_up, grad_conv, bias[0]


def solution(mesh):
    field = P(None, "gx", "gy", None)
    return jax.shard_map(
        body,
        mesh=mesh,
        in_specs=(field, field, P("gx", "gy", None), field, P(), P(), P()),
        out_specs=(field, field, field, P(), P(), P()),
        check_vma=False,
    )
```
